32 devices in a mesh: fsdp: 16 (over z, x, core), seq: 2 (over y).
Axes of the slice: x: 2, y: 2, z: 4, core: 2. Of those that a mesh axis runs over, the one named last changes fastest.
Arguments:
- tokens: bfloat16 [16, 2048, 1024], P('fsdp', 'seq'), may hold values from -6 to 6
- prenorm_gain: bfloat16 [1024], P('fsdp'), may hold values from 0.099609375 to 1.8984375
- query_weight: bfloat16 [1024, 1024], P('fsdp'), may hold values from -0.375 to 0.375
- key_weight: bfloat16 [1024, 128], P('fsdp'), may hold values from -0.1875 to 0.1875
- value_weight: bfloat16 [1024, 128], P('fsdp'), may hold values from -0.1875 to 0.1875
- project_weight: bfloat16 [1024, 1024], P('fsdp'), may hold values from -1 to 1
- midnorm_gain: bfloat16 [1024], P('fsdp'), may hold values from 0.099609375 to 1.8984375
- gate_weight: bfloat16 [1024, 3072], P('fsdp'), may hold values from -0.1875 to 0.1875
- up_weight: bfloat16 [1024, 3072], P('fsdp'), may hold values from -0.1875 to 0.1875
- down_weight: bfloat16 [3072, 1024], P('fsdp'), may hold values from -0.109375 to 0.109375
- out_grad: bfloat16 [16, 2048, 1024], P('fsdp', 'seq'), may hold values from -6 to 6
Outputs:
- block_output: bfloat16 [16, 2048, 1024], P('fsdp', 'seq')
- input_grad: bfloat16 [16, 2048, 1024], P('fsdp', 'seq')
- prenorm_gradient: float32 [1024], P('fsdp')
- query_gradient: float32 [1024, 1024], P('fsdp')
- key_gradient: float32 [1024, 128], P('fsdp')
- value_gradient: float32 [1024, 128], P('fsdp')
- project_gradient: float32 [1024, 1024], P('fsdp')
- midnorm_gradient: float32 [1024], P('fsdp')
- gate_gradient: float32 [1024, 3072], P('fsdp')
- up_gradient: float32 [1024, 3072], P('fsdp')
- down_gradient: float32 [3072, 1024], P('fsdp')
The draws below stay inside these ranges and needn't reach their ends.
All inputs are finite; a program needn't handle non-finite values.
Results may differ from the reference program's by a relative error of at most 0.024.
Values may be sent and summed in bfloat16 or wider, within the bound.
No kernel may reach another device: no remote copies, remote signals or barrier semaphores. Data moves between devices by JAX's collectives and lax.ppermute only.
A program may use at most 256 MiB of HBM per device.

```python
import jax
import jax.numpy as jnp
from jax import lax

D = 1024
HEADS = 8
HD = 128
FF = 3072
WINDOW = 1024
QBLOCK = 512
SEQ_LEN = 2048
SEQS = 16


def spiked(drawn, own_key, source, target, shards_of, factor):
    owner, partner = [(jnp.arange(drawn.shape[position]) // (drawn.shape[position] // shards_of)).reshape([-1 if axis == position else 1 for axis in range(drawn.ndim)]) for position in (source, target)]
    chosen = jax.random.permutation(own_key, shards_of)[partner]
    strong = (owner == chosen) | (owner == (partner + shards_of // 2) % shards_of)
    return jnp.where(strong, factor * drawn, drawn)


def level_of(key, shape, shards, smallest, top_value):
    gain, own = 1.0, jax.random.fold_in(key, 6)
    for axis_at, blocks in shards:
        steps = jnp.exp(jax.random.uniform(jax.random.fold_in(own, axis_at), (blocks,), jnp.float32, smallest / len(shards), top_value / len(shards)))
        gain = gain * jnp.repeat(steps, shape[axis_at] // blocks).reshape([-1 if axis == axis_at else 1 for axis in range(len(shape))])
    return gain


def centred(own_key, dims, scale, most, cuts=(), held_as=jnp.bfloat16):
    values = scale * jax.random.normal(own_key, dims, jnp.float32)
    if cuts:
        values = values * level_of(own_key, dims, cuts, -0.22, 0.18)
    return jnp.clip(values, -most, most).astype(held_as)


def heavy_noise(own_key, dims, deviation, limit, cuts, heavy, held_as=jnp.bfloat16):
    values = deviation * jax.random.normal(own_key, dims, jnp.float32)
    if cuts:
        values = values * level_of(own_key, dims, cuts, -0.22, 0.18)
    return jnp.clip(spiked(values, jax.random.fold_in(own_key, 3), *heavy), -limit, limit).astype(held_as)


def setup_inputs(seed: int = 0) -> dict:
    key_list = jax.random.split(jax.random.key(seed), 12)
    return {
        "tokens": heavy_noise(key_list[0], (SEQS, SEQ_LEN, D), 1.0, 6.0, ((0, 16), (1, 2)), (0, 2, 16, 2.0)),
        "prenorm_gain": jnp.clip(1.0 + 0.18 * jax.random.normal(key_list[1], (D,), jnp.float32), 0.099609375, 1.8984375).astype(jnp.bfloat16),
        "query_weight": centred(key_list[2], (D, HEADS * HD), (D // 4) ** -0.5, 0.375, ((0, 16),)),
        "key_weight": centred(key_list[3], (D, HD), D ** -0.5, 0.1875, ((0, 16),)),
        "value_weight": centred(key_list[4], (D, HD), D ** -0.5, 0.1875, ((0, 16),)),
        "project_weight": centred(key_list[5], (HEADS * HD, D), (HEADS * HD // 32) ** -0.5, 1.0, ((0, 16),)),
        "midnorm_gain": jnp.clip(1.0 + 0.18 * jax.random.normal(key_list[6], (D,), jnp.float32), 0.099609375, 1.8984375).astype(jnp.bfloat16),
        "gate_weight": centred(key_list[7], (D, FF), D ** -0.5, 0.1875, ((0, 16),)),
        "up_weight": centred(key_list[8], (D, FF), D ** -0.5, 0.1875, ((0, 16),)),
        "down_weight": centred(key_list[9], (FF, D), FF ** -0.5, 0.109375, ((0, 16),)),
        "out_grad": centred(key_list[10], (SEQS, SEQ_LEN, D), 1.0, 6.0, ((0, 16), (1, 2))),
    }


@jax.custom_vjp
def low(v):
    return lax.optimization_barrier(v.astype(jnp.bfloat16)).astype(jnp.float32)

@jax.custom_vjp
def low_back(v):
    return v

def low_keep(v):
    return (low(v), None)

def low_pass(kept, grad):
    return (grad,)

def back_keep(v):
    return (v, None)

def back_low(kept, grad):
    return (low(grad),)
low.defvjp(low_keep, low_pass)
low_back.defvjp(back_keep, back_low)
highest = lax.Precision.HIGHEST
norm_epsilon = 1e-06
masked_value = -1e+30

def rotary(values, positions):
    half = values.shape[-1] // 2
    frequency = 10000.0 ** (-jnp.arange(half, dtype=jnp.float32) / half)
    angles = positions[..., None].astype(jnp.float32) * frequency
    cosine = jnp.cos(angles)
    sine = jnp.sin(angles)
    first = values[..., :half]
    second = values[..., half:]
    return jnp.concatenate([first * cosine - second * sine, second * cosine + first * sine], axis=-1)

def attention(queries, keys, values):
    length = queries.shape[0]
    key_pad = jnp.concatenate([jnp.zeros((WINDOW, HD), jnp.float32), keys], axis=0)
    value_pad = jnp.concatenate([jnp.zeros((WINDOW, HD), jnp.float32), values], axis=0)

    def one_block(start):
        query_block = lax.dynamic_slice_in_dim(queries, start, QBLOCK, 0)
        key_block = lax.dynamic_slice_in_dim(key_pad, start, WINDOW + QBLOCK, 0)
        value_block = lax.dynamic_slice_in_dim(value_pad, start, WINDOW + QBLOCK, 0)
        scores = jnp.einsum('qhd,kd->hqk', query_block, key_block, precision=highest) * HD ** (-0.5)
        query_places = start + jnp.arange(QBLOCK, dtype=jnp.int32)
        key_places = start - WINDOW + jnp.arange(WINDOW + QBLOCK, dtype=jnp.int32)
        valid = (key_places[None, :] <= query_places[:, None]) & (key_places[None, :] > query_places[:, None] - WINDOW) & (key_places[None, :] >= 0)
        scores = low_back(jnp.where(valid[None], scores, masked_value))
        probability = low(jax.nn.softmax(scores, axis=-1))
        return jnp.einsum('hqk,kd->qhd', probability, value_block, precision=highest)
    starts = jnp.arange(length // QBLOCK, dtype=jnp.int32) * QBLOCK
    blocks = lax.map(jax.checkpoint(one_block), starts)
    return blocks.reshape(length, HEADS, HD)

def block_forward(sequence, prenorm_gain, query_weight, key_weight, value_weight, project_weight, midnorm_gain, gate_weight, up_weight, down_weight):
    length = sequence.shape[0]
    positions = jnp.arange(length, dtype=jnp.int32)
    normed_one = sequence * lax.rsqrt(lax.optimization_barrier(jnp.mean(sequence * sequence, axis=-1, keepdims=True)) + norm_epsilon)
    hidden_one = low(normed_one * prenorm_gain)
    query_lin = low_back(jnp.dot(hidden_one, query_weight, precision=highest)).reshape(length, HEADS, HD)
    queries = low(rotary(query_lin, positions[:, None]))
    keys = low(rotary(low_back(jnp.dot(hidden_one, key_weight, precision=highest)), positions))
    values = low(low_back(jnp.dot(hidden_one, value_weight, precision=highest)))
    attended = low(low_back(attention(queries, keys, values))).reshape(length, HEADS * HD)
    middle = sequence + low_back(jnp.dot(attended, project_weight, precision=highest))
    normed_two = middle * lax.rsqrt(lax.optimization_barrier(jnp.mean(middle * middle, axis=-1, keepdims=True)) + norm_epsilon)
    hidden_two = low(normed_two * midnorm_gain)
    gate = low_back(jnp.dot(hidden_two, gate_weight, precision=highest))
    up = low_back(jnp.dot(hidden_two, up_weight, precision=highest))
    activated = low(jax.nn.gelu(gate, approximate=False) * up)
    return middle + low_back(jnp.dot(activated, down_weight, precision=highest))

def reference(tokens, prenorm_gain, query_weight, key_weight, value_weight, project_weight, midnorm_gain, gate_weight, up_weight, down_weight, out_grad):
    weights = tuple((item.astype(jnp.float32) for item in (prenorm_gain, query_weight, key_weight, value_weight, project_weight, midnorm_gain, gate_weight, up_weight, down_weight)))

    def one_sequence(totals, pair):
        sequence, cotangent = pair
        result, pullback = jax.vjp(block_forward, sequence.astype(jnp.float32), *weights)
        grads = pullback(cotangent.astype(jnp.float32))
        totals = tuple((total + grad for total, grad in zip(totals, grads[1:])))
        return (totals, (result.astype(jnp.bfloat16), grads[0].astype(jnp.bfloat16)))
    start_totals = tuple((jnp.zeros(item.shape, jnp.float32) for item in weights))
    totals, (outputs, input_grads) = lax.scan(one_sequence, start_totals, (tokens, out_grad))
    return (outputs, input_grads, totals[0], totals[1], totals[2], totals[3], totals[4], totals[5], totals[6], totals[7], totals[8])
```

```python
import functools

import jax
import jax.numpy as jnp
from jax import lax
from jax.experimental import pallas as pl
from jax.experimental.pallas import tpu as pltpu
from jax.sharding import Mesh
from jax.sharding import PartitionSpec as P

HEADS = 8
HD = 128
WINDOW = 1024

norm_epsilon = 1e-06
masked_value = -1e30
LOG2E = 1.4426950408889634
bf16 = jnp.bfloat16
f32 = jnp.float32
OWN = ("z", "x", "c")
ALL = ("z", "x", "c", "y")


def nn(a, b):
    return lax.dot_general(a, b, (((1,), (0,)), ((), ())), preferred_element_type=f32)


def nt(a, b):
    return lax.dot_general(a, b, (((1,), (1,)), ((), ())), preferred_element_type=f32)


def tn(a, b):
    return lax.dot_general(a, b, (((0,), (0,)), ((), ())), preferred_element_type=f32)


def params(mib):
    return pltpu.CompilerParams(vmem_limit_bytes=mib << 20)


def cost(flops, moved, exps=0):
    return pl.CostEstimate(flops=int(flops), bytes_accessed=int(moved), transcendentals=int(exps))


def window_scores(scores, block, first_valid, limited):
    rows, keys = scores.shape
    r = lax.rem(lax.broadcasted_iota(jnp.int32, (rows, block), 0), block)
    j = lax.broadcasted_iota(jnp.int32, (rows, block), 1)
    front = jnp.where(j > r, scores[:, :block], masked_value)
    back = jnp.where(j <= r, scores[:, keys - block :], masked_value)
    scores = jnp.concatenate([front, scores[:, block : keys - block], back], axis=1)
    if limited:
        place = lax.broadcasted_iota(jnp.int32, scores.shape, 1)
        scores = jnp.where(place >= first_valid, scores, masked_value)
    return scores


def stacked(ref, heads):
    return jnp.concatenate([ref[:, a * HD : (a + 1) * HD] for a in heads], axis=0)


def attention_fwd_kernel(start_ref, q_ref, kv_ref, o_ref, lse_ref, *, block, group):
    i = pl.program_id(0)
    keys = WINDOW + block
    base = pl.multiple_of(i * block, block)
    k = kv_ref[pl.ds(base, keys), :HD]
    v = kv_ref[pl.ds(base, keys), HD:]
    ones = jnp.ones_like(v)
    value_one = jnp.concatenate([v, ones], axis=1)
    first_valid = WINDOW - start_ref[0] - i * block
    scale = HD**-0.5 * LOG2E
    lane = lax.broadcasted_iota(jnp.int32, (block, HD), 1)

    def run(limited):
        stats = jnp.zeros((block, HD), f32)
        for g in range(HEADS // group):
            heads = range(g * group, (g + 1) * group)
            scores = window_scores(nt(stacked(q_ref, heads), k), block, first_valid, limited)
            top = jnp.max(scores, axis=1, keepdims=True) * scale
            weight = jnp.exp2(scores * scale - top).astype(bf16)
            both = nn(weight, value_one)
            total = both[:, HD:]
            out = both[:, :HD] / total
            lse = top + jnp.log2(total)
            for h, a in enumerate(heads):
                o_ref[:, a * HD : (a + 1) * HD] = out[h * block : (h + 1) * block].astype(bf16)
                stats = jnp.where(lane == a, lse[h * block : (h + 1) * block], stats)
        lse_ref[...] = stats

    @pl.when(first_valid <= 0)
    def _():
        run(False)

    @pl.when(first_valid > 0)
    def _():
        run(True)


def attention_fwd(start, q, kv, block=256, group=2):
    length, total = q.shape[0], kv.shape[0]
    block = min(block, length)
    rows = lambda w: pl.BlockSpec((block, w), lambda i: (i, 0))
    return pl.pallas_call(
        functools.partial(attention_fwd_kernel, block=block, group=group),
        grid=(length // block,),
        in_specs=[
            pl.BlockSpec(memory_space=pltpu.SMEM),
            rows(HEADS * HD),
            pl.BlockSpec((total, 2 * HD), lambda i: (0, 0)),
        ],
        out_specs=[rows(HEADS * HD), rows(HD)],
        out_shape=[
            jax.ShapeDtypeStruct((length, HEADS * HD), bf16),
            jax.ShapeDtypeStruct((length, HD), f32),
        ],
        compiler_params=params(48),
        cost_estimate=cost(
            20 * length * HEADS * HD * WINDOW, 6 << 20, length * HEADS * WINDOW
        ),
        name="attention_fwd",
    )(start, q, kv)


def attention_bwd_kernel(
    start_ref, q_ref, kv_ref, o_ref, do_ref, lse_ref, cos_ref, sin_ref, dq_ref, dk_ref, dv_ref, *, block, group
):
    i = pl.program_id(0)
    keys = WINDOW + block
    base = pl.multiple_of(i * block, block)
    k = kv_ref[pl.ds(base, keys), :HD]
    v = kv_ref[pl.ds(base, keys), HD:]
    first_valid = WINDOW - start_ref[0] - i * block
    scale = HD**-0.5 * LOG2E

    @pl.when(i == 0)
    def _():
        dk_ref[...] = jnp.zeros_like(dk_ref)
        dv_ref[...] = jnp.zeros_like(dv_ref)

    def run(limited):
        for g in range(HEADS // group):
            heads = range(g * group, (g + 1) * group)
            q = stacked(q_ref, heads)
            do = stacked(do_ref, heads)
            o = stacked(o_ref, heads)
            lse = jnp.concatenate([lse_ref[:, a : a + 1] for a in heads], axis=0)
            inner = jnp.sum(do.astype(f32) * o.astype(f32), axis=1, keepdims=True)
            scores = window_scores(nt(q, k), block, first_valid, limited)
            prob = jnp.exp2(scores * scale - lse)
            prob_grad = nt(do, v)
            score_grad = (prob * (prob_grad - inner)).astype(bf16)
            dv_ref[pl.ds(base, keys), :] += tn(prob.astype(bf16), do)
            dk_ref[pl.ds(base, keys), :] += tn(score_grad, q)
            dq = nn(score_grad, k) * (HD**-0.5)
            for h, a in enumerate(heads):
                t = dq[h * block : (h + 1) * block]
                t = t * cos_ref[...] - pltpu.roll(t, HD // 2, 1) * sin_ref[...]
                dq_ref[:, a * HD : (a + 1) * HD] = t.astype(bf16)

    @pl.when(first_valid <= 0)
    def _():
        run(False)

    @pl.when(first_valid > 0)
    def _():
        run(True)

    @pl.when(i == pl.num_programs(0) - 1)
    def _():
        dk_ref[...] *= HD**-0.5


def attention_bwd(start, q, kv, o, do, lse, cos2, sin2, block=128, group=2):
    length, total = q.shape[0], kv.shape[0]
    rows = lambda w: pl.BlockSpec((block, w), lambda i: (i, 0))
    whole = lambda w: pl.BlockSpec((total, w), lambda i: (0, 0))
    wide = HEADS * HD
    return pl.pallas_call(
        functools.partial(attention_bwd_kernel, block=block, group=group),
        grid=(length // block,),
        in_specs=[
            pl.BlockSpec(memory_space=pltpu.SMEM),
            rows(wide),
            whole(2 * HD),
            rows(wide),
            rows(wide),
            rows(HD),
            rows(HD),
            rows(HD),
        ],
        out_specs=[rows(wide), whole(HD), whole(HD)],
        out_shape=[
            jax.ShapeDtypeStruct((length, wide), bf16),
            jax.ShapeDtypeStruct((total, HD), f32),
            jax.ShapeDtypeStruct((total, HD), f32),
        ],
        compiler_params=params(56),
        cost_estimate=cost(22 * length * wide * WINDOW, 14 << 20, length * HEADS * WINDOW),
        name="attention_bwd",
    )(start, q, kv, o, do, lse, cos2, sin2)


def qkv_kernel(x_ref, gain_ref, w_ref, cos_ref, sin_ref, h_ref, q_ref, kv_ref):
    x = x_ref[...].astype(f32)
    scale = lax.rsqrt(jnp.mean(x * x, axis=-1, keepdims=True) + norm_epsilon)
    h = (x * scale * gain_ref[...]).astype(bf16)
    h_ref[...] = h
    cos2, sin2 = cos_ref[...], sin_ref[...]
    for a in range(0, HEADS, 2):
        lin = nn(h, w_ref[:, a * HD : (a + 2) * HD])
        for b in range(2):
            t = lin[:, b * HD : (b + 1) * HD]
            q_ref[:, (a + b) * HD : (a + b + 1) * HD] = (
                t * cos2 + pltpu.roll(t, HD // 2, 1) * sin2
            ).astype(bf16)
    lin = nn(h, w_ref[:, HEADS * HD :])
    t = lin[:, :HD]
    kv_ref[:, :HD] = (t * cos2 + pltpu.roll(t, HD // 2, 1) * sin2).astype(bf16)
    kv_ref[:, HD:] = lin[:, HD:].astype(bf16)


def qkv_forward(x, gain, w, cos2, sin2, block=256):
    length, width = x.shape
    rows = lambda n: pl.BlockSpec((block, n), lambda i: (i, 0))
    whole = lambda a: pl.BlockSpec(a.shape, lambda i: (0, 0))
    return pl.pallas_call(
        qkv_kernel,
        grid=(length // block,),
        in_specs=[rows(width), whole(gain), whole(w), rows(HD), rows(HD)],
        out_specs=[rows(width), rows(HEADS * HD), rows(2 * HD)],
        out_shape=[
            jax.ShapeDtypeStruct((length, width), bf16),
            jax.ShapeDtypeStruct((length, HEADS * HD), bf16),
            jax.ShapeDtypeStruct((length, 2 * HD), bf16),
        ],
        compiler_params=params(32),
        cost_estimate=cost(4 * length * w.size, 12 << 20),
        name="norm_qkv",
    )(x, gain, w, cos2, sin2)


def middle_kernel(x_ref, a_ref, w_ref, gain_ref, mid_ref, h_ref):
    mid = x_ref[...].astype(f32) + nn(a_ref[...], w_ref[...])
    mid_ref[...] = mid
    scale = lax.rsqrt(jnp.mean(mid * mid, axis=-1, keepdims=True) + norm_epsilon)
    h_ref[...] = (mid * scale * gain_ref[...]).astype(bf16)


def middle_forward(x, attended, w, gain, block=256):
    length, width = x.shape
    rows = pl.BlockSpec((block, width), lambda i: (i, 0))
    whole = lambda a: pl.BlockSpec(a.shape, lambda i: (0, 0))
    return pl.pallas_call(
        middle_kernel,
        grid=(length // block,),
        in_specs=[rows, pl.BlockSpec((block, attended.shape[1]), lambda i: (i, 0)), whole(w), whole(gain)],
        out_specs=[rows, rows],
        out_shape=[
            jax.ShapeDtypeStruct((length, width), f32),
            jax.ShapeDtypeStruct((length, width), bf16),
        ],
        compiler_params=params(32),
        cost_estimate=cost(4 * length * w.size, 12 << 20),
        name="project_norm",
    )(x, attended, w, gain)


def norm_back(dn, normed, scale):
    return scale * (dn - normed * jnp.mean(dn * normed, axis=-1, keepdims=True))


def middle_back_kernel(hg_ref, mid_ref, do_ref, gain_ref, w_ref, mg_ref, low_ref, ag_ref, gain_grad_ref):
    i = pl.program_id(0)
    mid = mid_ref[...]
    hg = hg_ref[...]
    scale = lax.rsqrt(jnp.mean(mid * mid, axis=-1, keepdims=True) + norm_epsilon)
    normed = mid * scale
    mg = do_ref[...].astype(f32) + norm_back(hg * gain_ref[...], normed, scale)
    mg_ref[...] = mg
    low = mg.astype(bf16)
    low_ref[...] = low
    ag_ref[...] = nt(low, w_ref[...]).astype(bf16)

    @pl.when(i == 0)
    def _():
        gain_grad_ref[...] = jnp.zeros_like(gain_grad_ref)

    gain_grad_ref[...] += jnp.sum(hg * normed, axis=0, keepdims=True)


def middle_back(hg, mid, do, gain, w, block=256):
    length, width = mid.shape
    rows = lambda n: pl.BlockSpec((block, n), lambda i: (i, 0))
    whole = lambda s: pl.BlockSpec(s, lambda i: (0, 0))
    return pl.pallas_call(
        middle_back_kernel,
        grid=(length // block,),
        in_specs=[rows(width), rows(width), rows(width), whole(gain.shape), whole(w.shape)],
        out_specs=[rows(width), rows(width), rows(w.shape[0]), whole((1, width))],
        out_shape=[
            jax.ShapeDtypeStruct((length, width), f32),
            jax.ShapeDtypeStruct((length, width), bf16),
            jax.ShapeDtypeStruct((length, w.shape[0]), bf16),
            jax.ShapeDtypeStruct((1, width), f32),
        ],
        compiler_params=params(40),
        cost_estimate=cost(4 * length * w.size, 22 << 20),
        name="norm_two_back",
    )(hg, mid, do, gain, w)


def input_back_kernel(dq_ref, dkv_ref, w_ref, x_ref, gain_ref, mg_ref, out_ref, gain_grad_ref):
    i = pl.program_id(0)
    wide = dq_ref.shape[1]
    hg = nt(dq_ref[...], w_ref[:, :wide]) + nt(dkv_ref[...], w_ref[:, wide:])
    x = x_ref[...].astype(f32)
    scale = lax.rsqrt(jnp.mean(x * x, axis=-1, keepdims=True) + norm_epsilon)
    normed = x * scale
    out_ref[...] = (mg_ref[...] + norm_back(hg * gain_ref[...], normed, scale)).astype(bf16)

    @pl.when(i == 0)
    def _():
        gain_grad_ref[...] = jnp.zeros_like(gain_grad_ref)

    gain_grad_ref[...] += jnp.sum(hg * normed, axis=0, keepdims=True)


def input_back(dq, dkv, w, x, gain, mg, block=256):
    length, width = x.shape
    rows = lambda n: pl.BlockSpec((block, n), lambda i: (i, 0))
    whole = lambda s: pl.BlockSpec(s, lambda i: (0, 0))
    return pl.pallas_call(
        input_back_kernel,
        grid=(length // block,),
        in_specs=[
            rows(dq.shape[1]),
            rows(dkv.shape[1]),
            whole(w.shape),
            rows(width),
            whole(gain.shape),
            rows(width),
        ],
        out_specs=[rows(width), whole((1, width))],
        out_shape=[
            jax.ShapeDtypeStruct((length, width), bf16),
            jax.ShapeDtypeStruct((1, width), f32),
        ],
        compiler_params=params(40),
        cost_estimate=cost(4 * length * w.size, 16 << 20),
        name="norm_one_back",
    )(dq, dkv, w, x, gain, mg)


def gelu_parts(x):
    t = 1.0 / (1.0 + (0.3275911 * 0.7071067811865476) * jnp.abs(x))
    e = jnp.exp2(x * x * (-0.5 * LOG2E))
    poly = 0.5 * 1.061405429 * t - 0.5 * 1.453152027
    poly = poly * t + 0.5 * 1.421413741
    poly = poly * t - 0.5 * 0.284496736
    poly = (poly * t + 0.5 * 0.254829592) * t
    tail = poly * e
    return jnp.where(x >= 0, 1.0 - tail, tail), x * e * 0.3989422804014327


def feed_forward_kernel(
    h_ref, do_ref, wg_ref, wu_ref, wd_ref, mid_ref, act_ref, gg_ref, ug_ref, out_ref, hg_ref, acc
):
    j = pl.program_id(0)

    @pl.when(j == 0)
    def _():
        acc[...] = mid_ref[...]
        hg_ref[...] = jnp.zeros_like(hg_ref)

    h = h_ref[...]
    gate = nn(h, wg_ref[...])
    up = nn(h, wu_ref[...])
    act_grad = nt(do_ref[...], wd_ref[...])
    cdf, x_pdf = gelu_parts(gate)
    gelu = gate * cdf
    act = (gelu * up).astype(bf16)
    gate_grad = (act_grad * up * (cdf + x_pdf)).astype(bf16)
    up_grad = (act_grad * gelu).astype(bf16)
    act_ref[...] = act
    gg_ref[...] = gate_grad
    ug_ref[...] = up_grad
    acc[...] += nn(act, wd_ref[...])
    hg_ref[...] += nt(gate_grad, wg_ref[...]) + nt(up_grad, wu_ref[...])

    @pl.when(j == pl.num_programs(0) - 1)
    def _():
        out_ref[...] = acc[...].astype(bf16)


def feed_forward(h, do, wg, wu, wd, mid, chunk=512):
    length, width = h.shape
    hidden = wg.shape[1]
    whole = pl.BlockSpec((length, width), lambda j: (0, 0))
    col = lambda n: pl.BlockSpec((n, chunk), lambda j: (0, j))
    return pl.pallas_call(
        feed_forward_kernel,
        grid=(hidden // chunk,),
        in_specs=[whole, whole, col(width), col(width), pl.BlockSpec((chunk, width), lambda j: (j, 0)), whole],
        out_specs=[col(length)] * 3 + [whole, whole],
        out_shape=[jax.ShapeDtypeStruct((length, hidden), bf16)] * 3
        + [jax.ShapeDtypeStruct((length, width), bf16), jax.ShapeDtypeStruct((length, width), f32)],
        scratch_shapes=[pltpu.VMEM((length, width), f32)],
        compiler_params=params(60),
        cost_estimate=cost(16 * length * width * hidden, 60 << 20, length * hidden),
        name="feed_forward",
    )(h, do, wg, wu, wd, mid)


def weight_grad_kernel(half_ref, a_ref, b_ref, o_ref):
    o_ref[...] = tn(a_ref[...], b_ref[...]).astype(o_ref.dtype)


def weight_grad_add_kernel(half_ref, a_ref, b_ref, r_ref, o_ref):
    o_ref[...] = (tn(a_ref[...], b_ref[...]) + r_ref[...].astype(f32)).astype(o_ref.dtype)


def weight_grad(a, b, half, received=None, tall=1024, wide=768):
    length, rows = a.shape
    cols = b.shape[1] // 2
    wide = min(wide, cols)
    tall = min(tall, rows)
    per = cols // wide
    out = pl.BlockSpec((tall, wide), lambda i, j, s: (i, j))
    ins = [
        pl.BlockSpec((length, tall), lambda i, j, s: (0, i)),
        pl.BlockSpec((length, wide), lambda i, j, s: (0, s[0] * per + j)),
    ]
    args = [a, b]
    if received is not None:
        ins.append(out)
        args.append(received)
    return pl.pallas_call(
        weight_grad_kernel if received is None else weight_grad_add_kernel,
        grid_spec=pltpu.PrefetchScalarGridSpec(
            num_scalar_prefetch=1, grid=(rows // tall, per), in_specs=ins, out_specs=out
        ),
        out_shape=jax.ShapeDtypeStruct((rows, cols), bf16),
        compiler_params=params(48),
        cost_estimate=cost(4 * length * rows * cols, 2 * (length * rows + length * cols + 2 * rows * cols)),
        name="weight_grad",
    )(half, *args)


def shift(value, axis, k):
    n = lax.axis_size(axis)
    return lax.ppermute(value, axis, [(i, (i + k) % n) for i in range(n)])


def assemble_kernel(place, *refs, deep, part, halves):
    n = 4 * halves
    ins, out, sems = refs[:n], refs[n], refs[n + 1]
    z, x, c, y = place[0], place[1], place[2], place[3]
    copies = []
    for i, ref in enumerate(ins):
        xx = x if i % 2 == 0 else 1 - x
        cc = c if (i // 2) % 2 == 0 else 1 - c
        yy = 0 if halves == 1 else (y if i < 4 else 1 - y)
        for k in range(deep):
            zz = lax.rem(z - k + deep, deep)
            row = pl.multiple_of((((zz * 2 + xx) * 2 + cc) * halves + yy) * part, part)
            copies.append(
                pltpu.make_async_copy(ref.at[k, pl.ds(0, part)], out.at[pl.ds(row, part)], sems.at[i, k])
            )
    for copy in copies:
        copy.start()
    for copy in copies:
        copy.wait()


def assemble(place, pieces, rows):
    n, deep, cols = len(pieces), pieces[0].shape[0], pieces[0].shape[2]
    return pl.pallas_call(
        functools.partial(assemble_kernel, deep=deep, part=rows // (deep * n), halves=n // 4),
        out_shape=jax.ShapeDtypeStruct((rows, cols), bf16),
        in_specs=[pl.BlockSpec(memory_space=pltpu.SMEM)] + [pl.BlockSpec(memory_space=pltpu.VMEM)] * n,
        out_specs=pl.BlockSpec(memory_space=pl.ANY),
        scratch_shapes=[pltpu.SemaphoreType.DMA((n, deep))],
        compiler_params=params(16),
        cost_estimate=cost(0, rows * cols * 4),
        name="assemble",
    )(place, *pieces)


def along_z(piece):
    return jnp.stack([piece] + [shift(piece, "z", k) for k in range(1, lax.axis_size("z"))])


def gather_plain(shard):
    own = along_z(shard)
    pieces = [own, shift(own, "x", 1)]
    return pieces + [shift(p, "c", 1) for p in pieces]


def gather_halved(shard, x_last):
    half = shard.shape[0] // 2
    own = along_z(lax.dynamic_slice_in_dim(shard, lax.axis_index("y") * half, half, 0))
    over_x = shift(own, "x", 1)
    over_y = shift(own, "y", 1)
    over_xy = shift(over_y, "x", 1) if x_last else shift(over_x, "y", 1)
    near = [own, over_x]
    far = [over_y, over_xy]
    return near + [shift(p, "c", 1) for p in near] + far + [shift(p, "c", 1) for p in far]


def half_of(value, axis, index):
    n = value.shape[axis] // 2
    return lax.dynamic_slice_in_dim(value, index * n, n, axis)


def add_low(a, b):
    return (a.astype(f32) + b.astype(f32)).astype(bf16)


def scatter(chip_sum, x_first):
    deep = lax.axis_size("z")
    z, x, c, y = (lax.axis_index(a) for a in ALL)
    rows, cols = chip_sum.shape
    part = rows // (4 * deep)
    s = chip_sum.reshape(deep, 2, 2, part, cols)
    for axis, at, index in [("x", 1, x), ("y", 2, y)] if x_first else [("y", 2, y), ("x", 1, x)]:
        away = shift(half_of(s, at, 1 - index), axis, 1)
        s = add_low(half_of(s, at, index), away)
    s = s.reshape(deep, part, cols)
    total = lax.dynamic_index_in_dim(s, z, 0, False).astype(f32)
    for k in range(1, deep):
        away = lax.dynamic_index_in_dim(s, lax.rem(z + k, deep), 0, False)
        total = total + shift(away, "z", k).astype(f32)
    total = total.astype(bf16)
    other_y = shift(total, "y", 1)
    rows_mine = jnp.where(c == y, total, other_y)
    rows_away = jnp.where(c == y, other_y, total)
    received = shift(rows_away, "c", 1)
    left = jnp.where(c == 0, rows_mine, received)
    right = jnp.where(c == 0, received, rows_mine)
    return jnp.concatenate([left, right], axis=1).astype(f32)


def per_device(
    tokens,
    prenorm_gain,
    query_weight,
    key_weight,
    value_weight,
    project_weight,
    midnorm_gain,
    gate_weight,
    up_weight,
    down_weight,
    out_grad,
    *,
    by_hand,
):
    z, x, c, y = (lax.axis_index(a) for a in ALL)
    deep = lax.axis_size("z")
    seqs = lax.axis_size("y")
    batch, length, width = tokens.shape
    shard = query_weight.shape[0]
    owners = width // shard
    hidden = gate_weight.shape[1]
    wide = HEADS * HD
    tokens = tokens[0]
    do = out_grad[0]

    qkv_shard = jnp.concatenate([query_weight, key_weight, value_weight], axis=1)
    gains_shard = jnp.stack([prenorm_gain, midnorm_gain])
    if by_hand:
        place = jnp.stack([z, x, c, y]).astype(jnp.int32)
        extra = jnp.pad(gains_shard, ((0, 14), (0, qkv_shard.shape[1] - shard)))
        pieces = gather_plain(jnp.concatenate([qkv_shard, extra], axis=0))
        qkv_full = assemble(place, pieces, width)
        gain_rows = jnp.concatenate([p[:, shard : shard + 2, :shard] for p in pieces]).reshape(owners, 2 * shard)
        owner = jnp.arange(owners, dtype=jnp.int32)
        slot = (((owner // 2) % 2) ^ x) * deep + ((owner % 2) ^ c) * (2 * deep) + (z - owner // 4 + deep) % deep
        pick = (slot[:, None] == owner[None, :]).astype(bf16)
        gains = jnp.dot(pick, gain_rows, preferred_element_type=f32).reshape(owners, 2, shard)
        gains = gains.transpose(1, 0, 2).reshape(2, width)
        project_full = assemble(place, gather_plain(project_weight), wide)
        down_full = assemble(place, gather_halved(down_weight, True), hidden)
        gate_full = assemble(place, gather_halved(gate_weight, False), width)
        up_full = assemble(place, gather_halved(up_weight, False), width)
    else:
        gather = lambda w: lax.all_gather(w, OWN, axis=0, tiled=True)
        qkv_full, project_full, down_full, gate_full, up_full = (
            gather(w) for w in (qkv_shard, project_weight, down_weight, gate_weight, up_weight)
        )
        gains = lax.all_gather(gains_shard, OWN, axis=1, tiled=True).astype(f32)
    gain_one, gain_two = gains[0:1], gains[1:2]

    positions = y * length + jnp.arange(length, dtype=jnp.int32)
    frequency = 10000.0 ** (-jnp.arange(HD // 2, dtype=f32) / (HD // 2))
    angles = positions[:, None].astype(f32) * frequency
    cosine, sine = jnp.cos(angles), jnp.sin(angles)
    cos2 = jnp.concatenate([cosine, cosine], axis=1)
    sin2 = jnp.concatenate([-sine, sine], axis=1)
    start = (y * length).astype(jnp.int32)[None]

    hidden_one, queries, own_kv = qkv_forward(tokens, gain_one, qkv_full, cos2, sin2)
    reach = min(seqs - 1, -(-WINDOW // length))
    earlier = [
        lax.ppermute(own_kv, "y", [(i, i + k) for i in range(seqs - k)]) for k in range(reach, 0, -1)
    ]
    have = reach * length
    if have < WINDOW:
        earlier = [jnp.zeros((WINDOW - have, 2 * HD), bf16)] + earlier
    all_kv = jnp.concatenate(earlier + [own_kv], axis=0)[-(WINDOW + length) :]
    attended, log_totals = attention_fwd(start, queries, all_kv)
    middle, hidden_two = middle_forward(tokens, attended, project_full, gain_two)
    act, gate_low, up_low, block_output, hidden_two_grad = feed_forward(
        hidden_two, do, gate_full, up_full, down_full, middle
    )

    half = c.astype(jnp.int32)[None]

    def owned_grad(a, b, x_first):
        if not by_hand:
            zero, one = jnp.zeros((1,), jnp.int32), jnp.ones((1,), jnp.int32)
            return jnp.concatenate([weight_grad(a, b, zero), weight_grad(a, b, one)], axis=1)
        away = weight_grad(a, b, 1 - half)
        return weight_grad(a, b, half, shift(away, "c", 1))

    def finish(value, x_first):
        if by_hand:
            return scatter(value, x_first)
        share = lax.psum_scatter(value, OWN, scatter_dimension=0, tiled=True)
        return lax.psum(share, "y").astype(f32)

    gate_gradient = finish(owned_grad(hidden_two, gate_low, True), True)
    up_gradient = finish(owned_grad(hidden_two, up_low, False), False)
    middle_grad, branch_low, attended_grad, midnorm_part = middle_back(
        hidden_two_grad, middle, do, gain_two, project_full
    )
    down_gradient = finish(owned_grad(act, do, True), True)
    query_grad, key_all, value_all = attention_bwd(
        start, queries, all_kv, attended, attended_grad, log_totals, cos2, sin2
    )
    project_gradient = finish(owned_grad(attended, branch_low, False), False)
    kv_all = jnp.concatenate([key_all, value_all], axis=1)
    kv_sum = kv_all[WINDOW:]
    for k in range(1, reach + 1):
        low = WINDOW - k * length
        part = kv_all[max(low, 0) : low + length].astype(bf16)
        if low < 0:
            part = jnp.pad(part, ((-low, 0), (0, 0)))
        kv_sum = kv_sum + lax.ppermute(part, "y", [(i + k, i) for i in range(seqs - k)]).astype(f32)
    key_sum = kv_sum[:, :HD]
    key_grad = key_sum * cos2 - jnp.roll(key_sum, HD // 2, axis=1) * sin2
    kv_grad = jnp.concatenate([key_grad, kv_sum[:, HD:]], axis=1).astype(bf16)

    if by_hand:
        away = jnp.concatenate(
            [weight_grad(hidden_one, query_grad, 1 - half), weight_grad(hidden_one, kv_grad, 1 - half)], axis=1
        )
        received = shift(away, "c", 1)
        cut = wide // 2
        qkv_sum = jnp.concatenate(
            [
                weight_grad(hidden_one, query_grad, half, received[:, :cut]),
                weight_grad(hidden_one, kv_grad, half, received[:, cut:]),
            ],
            axis=1,
        )
        both = scatter(qkv_sum, True)
        n = both.shape[1] // 2
        query_gradient = jnp.concatenate([both[:, :cut], both[:, n : n + cut]], axis=1)
        key_gradient, value_gradient = both[:, cut:n], both[:, n + cut :]
    else:
        query_gradient = finish(owned_grad(hidden_one, query_grad, True), True)
        kv_gradient = finish(owned_grad(hidden_one, kv_grad, True), True)
        key_gradient, value_gradient = kv_gradient[:, :HD], kv_gradient[:, HD:]
    input_grad, prenorm_part = input_back(query_grad, kv_grad, qkv_full, tokens, gain_one, middle_grad)
    gain_sums = lax.psum(jnp.concatenate([prenorm_part, midnorm_part]), ALL)
    index = (z * 2 + x) * 2 + c
    gain_mine = lax.dynamic_slice_in_dim(gain_sums, index * shard, shard, 1)
    return (
        block_output[None],
        input_grad[None],
        gain_mine[0],
        query_gradient,
        key_gradient,
        value_gradient,
        project_gradient,
        gain_mine[1],
        gate_gradient,
        up_gradient,
        down_gradient,
    )


def solution(mesh):
    owners, seqs = mesh.shape["fsdp"], mesh.shape["seq"]
    deep = owners // 4
    split = Mesh(mesh.devices.reshape(deep, 2, 2, seqs), ALL)
    rows = P(OWN, "y", None)
    weight = P(OWN, None)
    in_specs = (
        rows,
        P(OWN),
        weight,
        weight,
        weight,
        weight,
        P(OWN),
        weight,
        weight,
        weight,
        rows,
    )
    out_specs = (
        rows,
        rows,
        P(OWN),
        weight,
        weight,
        weight,
        weight,
        P(OWN),
        weight,
        weight,
        weight,
    )
    by_hand = seqs == 2 and deep == 4
    return jax.shard_map(
        functools.partial(per_device, by_hand=by_hand),
        mesh=split,
        in_specs=in_specs,
        out_specs=out_specs,
        check_vma=False,
    )
```

```python
import functools

import jax
import jax.numpy as jnp
from jax import lax
from jax.experimental import pallas as pl
from jax.experimental.pallas import tpu as pltpu
from jax.sharding import Mesh
from jax.sharding import PartitionSpec as P

HEADS = 8
HD = 128
WINDOW = 1024

norm_epsilon = 1e-06
masked_value = -1e30
LOG2E = 1.4426950408889634
bf16 = jnp.bfloat16
f32 = jnp.float32
OWN = ("z", "x", "c")
ALL = ("z", "x", "c", "y")


def nn(a, b):
    return lax.dot_general(a, b, (((1,), (0,)), ((), ())), preferred_element_type=f32)


def nt(a, b):
    return lax.dot_general(a, b, (((1,), (1,)), ((), ())), preferred_element_type=f32)


def tn(a, b):
    return lax.dot_general(a, b, (((0,), (0,)), ((), ())), preferred_element_type=f32)


def params(mib):
    return pltpu.CompilerParams(vmem_limit_bytes=mib << 20)


def cost(flops, moved, exps=0):
    return pl.CostEstimate(flops=int(flops), bytes_accessed=int(moved), transcendentals=int(exps))


def window_scores(scores, block, first_valid, limited):
    rows, keys = scores.shape
    r = lax.rem(lax.broadcasted_iota(jnp.int32, (rows, block), 0), block)
    j = lax.broadcasted_iota(jnp.int32, (rows, block), 1)
    front = jnp.where(j > r, scores[:, :block], masked_value)
    back = jnp.where(j <= r, scores[:, keys - block :], masked_value)
    scores = jnp.concatenate([front, scores[:, block : keys - block], back], axis=1)
    if limited:
        place = lax.broadcasted_iota(jnp.int32, scores.shape, 1)
        scores = jnp.where(place >= first_valid, scores, masked_value)
    return scores


def stacked(ref, heads):
    return jnp.concatenate([ref[:, a * HD : (a + 1) * HD] for a in heads], axis=0)


def attention_fwd_kernel(start_ref, q_ref, kv_ref, o_ref, lse_ref, *, block, group):
    i = pl.program_id(0)
    keys = WINDOW + block
    base = pl.multiple_of(i * block, block)
    k = kv_ref[pl.ds(base, keys), :HD]
    v = kv_ref[pl.ds(base, keys), HD:]
    ones = jnp.ones_like(v)
    value_one = jnp.concatenate([v, ones], axis=1)
    first_valid = WINDOW - start_ref[0] - i * block
    scale = HD**-0.5 * LOG2E
    lane = lax.broadcasted_iota(jnp.int32, (block, HD), 1)

    def run(limited):
        stats = [jnp.zeros((block, HD), f32)] * 2
        for g in range(HEADS // group):
            heads = range(g * group, (g + 1) * group)
            scores = window_scores(nt(stacked(q_ref, heads), k), block, first_valid, limited)
            top = jnp.max(scores, axis=1, keepdims=True) * scale
            weight = jnp.exp2(scores * scale - top).astype(bf16)
            both = nn(weight, value_one)
            total = both[:, HD:]
            out = both[:, :HD] / total
            lse = top + jnp.log2(total)
            for h, a in enumerate(heads):
                o_ref[:, a * HD : (a + 1) * HD] = out[h * block : (h + 1) * block].astype(bf16)
                at, spot = divmod(a, HEADS // 2)
                stats[at] = jnp.where(lane == spot, lse[h * block : (h + 1) * block], stats[at])
        lse_ref[...] = jnp.concatenate(stats, axis=1)

    @pl.when(first_valid <= 0)
    def _():
        run(False)

    @pl.when(first_valid > 0)
    def _():
        run(True)


def attention_fwd(start, q, kv, block=256, group=2):
    length, total = q.shape[0], kv.shape[0]
    block = min(block, length)
    rows = lambda w: pl.BlockSpec((block, w), lambda i: (i, 0))
    return pl.pallas_call(
        functools.partial(attention_fwd_kernel, block=block, group=group),
        grid=(length // block,),
        in_specs=[
            pl.BlockSpec(memory_space=pltpu.SMEM),
            rows(HEADS * HD),
            pl.BlockSpec((total, 2 * HD), lambda i: (0, 0)),
        ],
        out_specs=[rows(HEADS * HD), rows(2 * HD)],
        out_shape=[
            jax.ShapeDtypeStruct((length, HEADS * HD), bf16),
            jax.ShapeDtypeStruct((length, 2 * HD), f32),
        ],
        compiler_params=params(48),
        cost_estimate=cost(
            20 * length * HEADS * HD * WINDOW, 6 << 20, length * HEADS * WINDOW
        ),
        name="attention_fwd",
    )(start, q, kv)


def attention_bwd_kernel(
    at_ref, q_ref, kv_ref, o_ref, do_ref, lse_ref, cos_ref, sin_ref, dq_ref, dk_ref, dv_ref, *, block, group
):
    i = pl.program_id(0)
    keys = WINDOW + block
    base = pl.multiple_of(i * block, block)
    k = kv_ref[pl.ds(base, keys), :HD]
    v = kv_ref[pl.ds(base, keys), HD:]
    first_valid = WINDOW - at_ref[0] - i * block
    scale = HD**-0.5 * LOG2E

    @pl.when(i == 0)
    def _():
        dk_ref[...] = jnp.zeros_like(dk_ref)
        dv_ref[...] = jnp.zeros_like(dv_ref)

    def run(limited):
        for g in range(HEADS // 2 // group):
            heads = range(g * group, (g + 1) * group)
            q = stacked(q_ref, heads)
            do = stacked(do_ref, heads)
            o = stacked(o_ref, heads)
            lse = jnp.concatenate([lse_ref[:, a : a + 1] for a in heads], axis=0)
            inner = jnp.sum(do.astype(f32) * o.astype(f32), axis=1, keepdims=True)
            scores = window_scores(nt(q, k), block, first_valid, limited)
            prob = jnp.exp2(scores * scale - lse)
            prob_grad = nt(do, v)
            score_grad = (prob * (prob_grad - inner)).astype(bf16)
            dv_ref[pl.ds(base, keys), :] += tn(prob.astype(bf16), do)
            dk_ref[pl.ds(base, keys), :] += tn(score_grad, q)
            dq = nn(score_grad, k) * (HD**-0.5)
            for h, a in enumerate(heads):
                t = dq[h * block : (h + 1) * block]
                t = t * cos_ref[...] - pltpu.roll(t, HD // 2, 1) * sin_ref[...]
                dq_ref[:, a * HD : (a + 1) * HD] = t.astype(bf16)

    @pl.when(first_valid <= 0)
    def _():
        run(False)

    @pl.when(first_valid > 0)
    def _():
        run(True)

    @pl.when(i == pl.num_programs(0) - 1)
    def _():
        dk_ref[...] *= HD**-0.5


def attention_bwd(start, half, q, kv, o, do, lse, cos2, sin2, block=128, group=2):
    length, total = q.shape[0], kv.shape[0]
    rows = pl.BlockSpec((block, HD), lambda i, s: (i, 0))
    wide = HEADS * HD // 2
    heads = pl.BlockSpec((block, wide), lambda i, s: (i, s[1]))
    whole = lambda w: pl.BlockSpec((total, w), lambda i, s: (0, 0))
    return pl.pallas_call(
        functools.partial(attention_bwd_kernel, block=block, group=group),
        grid_spec=pltpu.PrefetchScalarGridSpec(
            num_scalar_prefetch=1,
            grid=(length // block,),
            in_specs=[
                heads,
                whole(2 * HD),
                heads,
                heads,
                pl.BlockSpec((block, HD), lambda i, s: (i, s[1])),
                rows,
                rows,
            ],
            out_specs=[pl.BlockSpec((block, wide), lambda i, s: (i, 0)), whole(HD), whole(HD)],
        ),
        out_shape=[
            jax.ShapeDtypeStruct((length, wide), bf16),
            jax.ShapeDtypeStruct((total, HD), f32),
            jax.ShapeDtypeStruct((total, HD), f32),
        ],
        compiler_params=params(56),
        cost_estimate=cost(22 * length * wide * WINDOW, 8 << 20, length * HEADS * WINDOW // 2),
        name="attention_bwd",
    )(jnp.concatenate([start, half]), q, kv, o, do, lse, cos2, sin2)


def qkv_kernel(x_ref, gain_ref, w_ref, cos_ref, sin_ref, h_ref, q_ref, kv_ref):
    x = x_ref[...].astype(f32)
    scale = lax.rsqrt(jnp.mean(x * x, axis=-1, keepdims=True) + norm_epsilon)
    h = (x * scale * gain_ref[...]).astype(bf16)
    h_ref[...] = h
    cos2, sin2 = cos_ref[...], sin_ref[...]
    for a in range(0, HEADS, 2):
        lin = nn(h, w_ref[:, a * HD : (a + 2) * HD])
        for b in range(2):
            t = lin[:, b * HD : (b + 1) * HD]
            q_ref[:, (a + b) * HD : (a + b + 1) * HD] = (
                t * cos2 + pltpu.roll(t, HD // 2, 1) * sin2
            ).astype(bf16)
    lin = nn(h, w_ref[:, HEADS * HD :])
    t = lin[:, :HD]
    kv_ref[:, :HD] = (t * cos2 + pltpu.roll(t, HD // 2, 1) * sin2).astype(bf16)
    kv_ref[:, HD:] = lin[:, HD:].astype(bf16)


def qkv_forward(x, gain, w, cos2, sin2, block=256):
    length, width = x.shape
    rows = lambda n: pl.BlockSpec((block, n), lambda i: (i, 0))
    whole = lambda a: pl.BlockSpec(a.shape, lambda i: (0, 0))
    return pl.pallas_call(
        qkv_kernel,
        grid=(length // block,),
        in_specs=[rows(width), whole(gain), whole(w), rows(HD), rows(HD)],
        out_specs=[rows(width), rows(HEADS * HD), rows(2 * HD)],
        out_shape=[
            jax.ShapeDtypeStruct((length, width), bf16),
            jax.ShapeDtypeStruct((length, HEADS * HD), bf16),
            jax.ShapeDtypeStruct((length, 2 * HD), bf16),
        ],
        compiler_params=params(32),
        cost_estimate=cost(4 * length * w.size, 12 << 20),
        name="norm_qkv",
    )(x, gain, w, cos2, sin2)


def middle_kernel(x_ref, a_ref, w_ref, gain_ref, mid_ref, h_ref):
    mid = x_ref[...].astype(f32) + nn(a_ref[...], w_ref[...])
    mid_ref[...] = mid
    scale = lax.rsqrt(jnp.mean(mid * mid, axis=-1, keepdims=True) + norm_epsilon)
    h_ref[...] = (mid * scale * gain_ref[...]).astype(bf16)


def middle_forward(x, attended, w, gain, block=256):
    length, width = x.shape
    rows = pl.BlockSpec((block, width), lambda i: (i, 0))
    whole = lambda a: pl.BlockSpec(a.shape, lambda i: (0, 0))
    return pl.pallas_call(
        middle_kernel,
        grid=(length // block,),
        in_specs=[rows, pl.BlockSpec((block, attended.shape[1]), lambda i: (i, 0)), whole(w), whole(gain)],
        out_specs=[rows, rows],
        out_shape=[
            jax.ShapeDtypeStruct((length, width), f32),
            jax.ShapeDtypeStruct((length, width), bf16),
        ],
        compiler_params=params(32),
        cost_estimate=cost(4 * length * w.size, 12 << 20),
        name="project_norm",
    )(x, attended, w, gain)


def norm_back(dn, normed, scale):
    return scale * (dn - normed * jnp.mean(dn * normed, axis=-1, keepdims=True))


def middle_back_kernel(hg_ref, mid_ref, do_ref, gain_ref, w_ref, mg_ref, low_ref, ag_ref, gain_grad_ref):
    i = pl.program_id(0)
    mid = mid_ref[...]
    hg = hg_ref[...]
    scale = lax.rsqrt(jnp.mean(mid * mid, axis=-1, keepdims=True) + norm_epsilon)
    normed = mid * scale
    mg = do_ref[...].astype(f32) + norm_back(hg * gain_ref[...], normed, scale)
    mg_ref[...] = mg
    low = mg.astype(bf16)
    low_ref[...] = low
    ag_ref[...] = nt(low, w_ref[...]).astype(bf16)

    @pl.when(i == 0)
    def _():
        gain_grad_ref[...] = jnp.zeros_like(gain_grad_ref)

    gain_grad_ref[...] += jnp.sum(hg * normed, axis=0, keepdims=True)


def middle_back(hg, mid, do, gain, w, block=256):
    length, width = mid.shape
    rows = lambda n: pl.BlockSpec((block, n), lambda i: (i, 0))
    whole = lambda s: pl.BlockSpec(s, lambda i: (0, 0))
    return pl.pallas_call(
        middle_back_kernel,
        grid=(length // block,),
        in_specs=[rows(width), rows(width), rows(width), whole(gain.shape), whole(w.shape)],
        out_specs=[rows(width), rows(width), rows(w.shape[0]), whole((1, width))],
        out_shape=[
            jax.ShapeDtypeStruct((length, width), f32),
            jax.ShapeDtypeStruct((length, width), bf16),
            jax.ShapeDtypeStruct((length, w.shape[0]), bf16),
            jax.ShapeDtypeStruct((1, width), f32),
        ],
        compiler_params=params(40),
        cost_estimate=cost(4 * length * w.size, 22 << 20),
        name="norm_two_back",
    )(hg, mid, do, gain, w)


def input_back_kernel(half_ref, keep_ref, away_ref, dkv_ref, w_ref, x_ref, gain_ref, mg_ref, out_ref, gain_grad_ref):
    i = pl.program_id(0)
    wide = keep_ref.shape[1]
    own = pl.multiple_of(half_ref[0] * wide, wide)
    hg = nt(keep_ref[...], w_ref[:, pl.ds(own, wide)]) + nt(away_ref[...], w_ref[:, pl.ds(wide - own, wide)])
    hg += nt(dkv_ref[...], w_ref[:, 2 * wide :])
    x = x_ref[...].astype(f32)
    scale = lax.rsqrt(jnp.mean(x * x, axis=-1, keepdims=True) + norm_epsilon)
    normed = x * scale
    out_ref[...] = (mg_ref[...] + norm_back(hg * gain_ref[...], normed, scale)).astype(bf16)

    @pl.when(i == 0)
    def _():
        gain_grad_ref[...] = jnp.zeros_like(gain_grad_ref)

    gain_grad_ref[...] += jnp.sum(hg * normed, axis=0, keepdims=True)


def input_back(half, keep, away, dkv, w, x, gain, mg, block=256):
    length, width = x.shape
    rows = lambda n: pl.BlockSpec((block, n), lambda i, s: (i, 0))
    whole = lambda shape: pl.BlockSpec(shape, lambda i, s: (0, 0))
    return pl.pallas_call(
        input_back_kernel,
        grid_spec=pltpu.PrefetchScalarGridSpec(
            num_scalar_prefetch=1,
            grid=(length // block,),
            in_specs=[
                rows(keep.shape[1]),
                rows(away.shape[1]),
                rows(dkv.shape[1]),
                whole(w.shape),
                rows(width),
                whole(gain.shape),
                rows(width),
            ],
            out_specs=[rows(width), whole((1, width))],
        ),
        out_shape=[
            jax.ShapeDtypeStruct((length, width), bf16),
            jax.ShapeDtypeStruct((1, width), f32),
        ],
        compiler_params=params(40),
        cost_estimate=cost(4 * length * w.size, 16 << 20),
        name="norm_one_back",
    )(half, keep, away, dkv, w, x, gain, mg)


def gelu_parts(x):
    t = 1.0 / (1.0 + (0.3275911 * 0.7071067811865476) * jnp.abs(x))
    e = jnp.exp2(x * x * (-0.5 * LOG2E))
    poly = 0.5 * 1.061405429 * t - 0.5 * 1.453152027
    poly = poly * t + 0.5 * 1.421413741
    poly = poly * t - 0.5 * 0.284496736
    poly = (poly * t + 0.5 * 0.254829592) * t
    tail = poly * e
    return jnp.where(x >= 0, 1.0 - tail, tail), x * e * 0.3989422804014327


def feed_forward_kernel(
    h_ref, do_ref, wg_ref, wu_ref, wd_ref, mid_ref, act_ref, gg_ref, ug_ref, out_ref, hg_ref, acc
):
    j = pl.program_id(0)

    @pl.when(j == 0)
    def _():
        acc[...] = mid_ref[...]
        hg_ref[...] = jnp.zeros_like(hg_ref)

    h = h_ref[...]
    gate = nn(h, wg_ref[...])
    up = nn(h, wu_ref[...])
    act_grad = nt(do_ref[...], wd_ref[...])
    cdf, x_pdf = gelu_parts(gate)
    gelu = gate * cdf
    act = (gelu * up).astype(bf16)
    gate_grad = (act_grad * up * (cdf + x_pdf)).astype(bf16)
    up_grad = (act_grad * gelu).astype(bf16)
    act_ref[...] = act
    gg_ref[...] = gate_grad
    ug_ref[...] = up_grad
    acc[...] += nn(act, wd_ref[...])
    hg_ref[...] += nt(gate_grad, wg_ref[...]) + nt(up_grad, wu_ref[...])

    @pl.when(j == pl.num_programs(0) - 1)
    def _():
        out_ref[...] = acc[...].astype(bf16)


def feed_forward(h, do, wg, wu, wd, mid, chunk=512):
    length, width = h.shape
    hidden = wg.shape[1]
    whole = pl.BlockSpec((length, width), lambda j: (0, 0))
    col = lambda n: pl.BlockSpec((n, chunk), lambda j: (0, j))
    return pl.pallas_call(
        feed_forward_kernel,
        grid=(hidden // chunk,),
        in_specs=[whole, whole, col(width), col(width), pl.BlockSpec((chunk, width), lambda j: (j, 0)), whole],
        out_specs=[col(length)] * 3 + [whole, whole],
        out_shape=[jax.ShapeDtypeStruct((length, hidden), bf16)] * 3
        + [jax.ShapeDtypeStruct((length, width), bf16), jax.ShapeDtypeStruct((length, width), f32)],
        scratch_shapes=[pltpu.VMEM((length, width), f32)],
        compiler_params=params(60),
        cost_estimate=cost(16 * length * width * hidden, 60 << 20, length * hidden),
        name="feed_forward",
    )(h, do, wg, wu, wd, mid)


def weight_grad_kernel(half_ref, a_ref, b_ref, o_ref):
    o_ref[...] = tn(a_ref[...], b_ref[...]).astype(o_ref.dtype)


def weight_grad_add_kernel(half_ref, a_ref, b_ref, r_ref, o_ref):
    o_ref[...] = (tn(a_ref[...], b_ref[...]) + r_ref[...].astype(f32)).astype(o_ref.dtype)


def weight_grad(a, b, half, received=None, tall=1024, wide=768, parts=2):
    length, rows = a.shape
    cols = b.shape[1] // parts
    wide = min(wide, cols)
    tall = min(tall, rows)
    per = cols // wide
    out = pl.BlockSpec((tall, wide), lambda i, j, s: (i, j))
    ins = [
        pl.BlockSpec((length, tall), lambda i, j, s: (0, i)),
        pl.BlockSpec((length, wide), lambda i, j, s: (0, s[0] * per + j)),
    ]
    args = [a, b]
    if received is not None:
        ins.append(out)
        args.append(received)
    return pl.pallas_call(
        weight_grad_kernel if received is None else weight_grad_add_kernel,
        grid_spec=pltpu.PrefetchScalarGridSpec(
            num_scalar_prefetch=1, grid=(rows // tall, per), in_specs=ins, out_specs=out
        ),
        out_shape=jax.ShapeDtypeStruct((rows, cols), bf16),
        compiler_params=params(48),
        cost_estimate=cost(4 * length * rows * cols, 2 * (length * rows + length * cols + 2 * rows * cols)),
        name="weight_grad",
    )(half, *args)


def shift(value, axis, k):
    n = lax.axis_size(axis)
    return lax.ppermute(value, axis, [(i, (i + k) % n) for i in range(n)])


def assemble_kernel(place, *refs, deep, part, halves):
    ins, out = refs[:-1], refs[-1]
    z, x, c, y = place[0], place[1], place[2], place[3]
    for i, ref in enumerate(ins):
        xx = x if i % 2 == 0 else 1 - x
        cc = c if (i // 2) % 2 == 0 else 1 - c
        yy = 0 if halves == 1 else (y if i < 4 else 1 - y)
        for k in range(deep):
            zz = lax.rem(z - k + deep, deep)
            row = pl.multiple_of((((zz * 2 + xx) * 2 + cc) * halves + yy) * part, part)
            out[pl.ds(row, part), :] = ref[k, :part, :]


def assemble(place, pieces, rows):
    n, deep, cols = len(pieces), pieces[0].shape[0], pieces[0].shape[2]
    return pl.pallas_call(
        functools.partial(assemble_kernel, deep=deep, part=rows // (deep * n), halves=n // 4),
        out_shape=jax.ShapeDtypeStruct((rows, cols), bf16),
        in_specs=[pl.BlockSpec(memory_space=pltpu.SMEM)] + [pl.BlockSpec(memory_space=pltpu.VMEM)] * n,
        out_specs=pl.BlockSpec(memory_space=pltpu.VMEM),
        compiler_params=params(32),
        cost_estimate=cost(0, rows * cols * 4),
        name="assemble",
    )(place, *pieces)


def fence(*values):
    return lax.optimization_barrier(values)


def along_z(piece):
    return [piece] + [shift(piece, "z", k) for k in range(1, lax.axis_size("z"))]


def plus_core(pieces):
    return pieces + [shift(p, "c", 1) for p in pieces]


def half_of(value, axis, index):
    n = value.shape[axis] // 2
    return lax.dynamic_slice_in_dim(value, index * n, n, axis)


def add_low(a, b):
    return (a.astype(f32) + b.astype(f32)).astype(bf16)


class Scatter:
    def __init__(self, value, x_first):
        self.deep = lax.axis_size("z")
        self.rows, self.cols = value.shape
        self.part = self.rows // (4 * self.deep)
        self.kept = value.reshape(self.deep, 2, 2, self.part, self.cols)
        self.moving = None
        order = [("x", 1), ("y", 2)]
        self.order = order if x_first else order[::-1]
        self.pair()

    def pair(self):
        axis, at = self.order.pop(0)
        index = lax.axis_index(axis)
        self.moving = [shift(half_of(self.kept, at, 1 - index), axis, 1)]
        self.kept = half_of(self.kept, at, index)

    def second(self):
        self.kept = add_low(self.kept, self.moving[0])
        self.pair()

    def third(self):
        s = add_low(self.kept, self.moving[0]).reshape(self.deep, self.part, self.cols)
        z = lax.axis_index("z")
        self.kept = lax.dynamic_index_in_dim(s, z, 0, False)
        self.moving = [
            shift(lax.dynamic_index_in_dim(s, lax.rem(z + k, self.deep), 0, False), "z", k)
            for k in range(1, self.deep)
        ]

    def fourth(self):
        total = self.kept.astype(f32)
        for away in self.moving:
            total = total + away.astype(f32)
        self.kept = total.astype(bf16)
        self.moving = [shift(self.kept, "y", 1)]

    def last(self):
        c, y = lax.axis_index("c"), lax.axis_index("y")
        mine = jnp.where(c == y, self.kept, self.moving[0])
        received = shift(jnp.where(c == y, self.moving[0], self.kept), "c", 1)
        left = jnp.where(c == 0, mine, received).astype(f32)
        right = jnp.where(c == 0, received, mine).astype(f32)
        return left, right, mine

    def whole(self):
        return jnp.concatenate(self.last()[:2], axis=1)


def settle(values, scatters):
    values, moving = fence(values, [s.moving for s in scatters])
    for s, m in zip(scatters, moving):
        s.moving = m
    return values


def per_device(
    tokens,
    prenorm_gain,
    query_weight,
    key_weight,
    value_weight,
    project_weight,
    midnorm_gain,
    gate_weight,
    up_weight,
    down_weight,
    out_grad,
    *,
    by_hand,
):
    z, x, c, y = (lax.axis_index(a) for a in ALL)
    deep = lax.axis_size("z")
    seqs = lax.axis_size("y")
    batch, length, width = tokens.shape
    shard = query_weight.shape[0]
    owners = width // shard
    hidden = gate_weight.shape[1]
    wide = HEADS * HD
    tokens = tokens[0]
    do = out_grad[0]

    qkv_shard = jnp.concatenate([query_weight, key_weight, value_weight], axis=1)
    gains_shard = jnp.stack([prenorm_gain, midnorm_gain])

    positions = y * length + jnp.arange(length, dtype=jnp.int32)
    frequency = 10000.0 ** (-jnp.arange(HD // 2, dtype=f32) / (HD // 2))
    angles = positions[:, None].astype(f32) * frequency
    cosine, sine = jnp.cos(angles), jnp.sin(angles)
    cos2 = jnp.concatenate([cosine, cosine], axis=1)
    sin2 = jnp.concatenate([-sine, sine], axis=1)
    start = (y * length).astype(jnp.int32)[None]

    reach = min(seqs - 1, -(-WINDOW // length))

    def earlier_kv(own_kv):
        return [lax.ppermute(own_kv, "y", [(i, i + k) for i in range(seqs - k)]) for k in range(reach, 0, -1)]

    def window_kv(earlier, own_kv):
        have = reach * length
        if have < WINDOW:
            earlier = [jnp.zeros((WINDOW - have, 2 * HD), bf16)] + earlier
        return jnp.concatenate(earlier + [own_kv], axis=0)[-(WINDOW + length) :]

    if by_hand:
        place = jnp.stack([z, x, c, y]).astype(jnp.int32)
        extra = jnp.pad(gains_shard, ((0, 14), (0, qkv_shard.shape[1] - shard)))
        own_half = lambda w: lax.dynamic_slice_in_dim(w, y * (w.shape[0] // 2), w.shape[0] // 2, 0)
        gate_z = along_z(own_half(gate_weight))
        qkv_z = along_z(jnp.concatenate([qkv_shard, extra], axis=0))
        up_z = along_z(own_half(up_weight))
        gate_z, project_own = fence(gate_z, project_weight)
        gate_o = jnp.stack(gate_z)
        gate_x, gate_y = shift(gate_o, "x", 1), shift(gate_o, "y", 1)
        project_z = along_z(project_own)
        qkv_z, gate_x, gate_y, down_own = fence(qkv_z, gate_x, gate_y, own_half(down_weight))
        qkv_o = jnp.stack(qkv_z)
        qkv_x = shift(qkv_o, "x", 1)
        gate_xy = shift(gate_x, "y", 1)
        gate_near = plus_core([gate_o, gate_x])
        up_z, down_own = fence(up_z, down_own)
        up_o = jnp.stack(up_z)
        up_x, up_y = shift(up_o, "x", 1), shift(up_o, "y", 1)
        down_z = along_z(down_own)
        qkv_o, qkv_x = fence(qkv_o, qkv_x)
        pieces = plus_core([qkv_o, qkv_x])
        qkv_full = assemble(place, pieces, width)
        gain_rows = jnp.concatenate([p[:, shard : shard + 2, :shard] for p in pieces]).reshape(owners, 2 * shard)
        owner = jnp.arange(owners, dtype=jnp.int32)
        slot = (((owner // 2) % 2) ^ x) * deep + ((owner % 2) ^ c) * (2 * deep) + (z - owner // 4 + deep) % deep
        pick = (slot[:, None] == owner[None, :]).astype(bf16)
        gains = jnp.dot(pick, gain_rows, preferred_element_type=f32).reshape(owners, 2, shard)
        gains = gains.transpose(1, 0, 2).reshape(2, width)
        gain_one, gain_two = gains[0:1], gains[1:2]
        hidden_one, queries, own_kv = qkv_forward(tokens, gain_one, qkv_full, cos2, sin2)
        project_z, own_kv, gate_xy = fence(project_z, own_kv, gate_xy)
        earlier = earlier_kv(own_kv)
        project_o = jnp.stack(project_z)
        project_x = shift(project_o, "x", 1)
        up_x, up_y, down_z = fence(up_x, up_y, down_z)
        up_xy = shift(up_x, "y", 1)
        down_o = jnp.stack(down_z)
        down_x, down_y = shift(down_o, "x", 1), shift(down_o, "y", 1)
        gate_full = assemble(place, gate_near + plus_core([gate_y, gate_xy]), width)
        up_near = plus_core([up_o, up_x])
        earlier, project_x = fence(earlier, project_x)
        all_kv = window_kv(earlier, own_kv)
        project_full = assemble(place, plus_core([project_o, project_x]), wide)
        attended, log_totals = attention_fwd(start, queries, all_kv)
        attended, down_x, down_y, up_xy = fence(attended, down_x, down_y, up_xy)
        down_xy = shift(down_y, "x", 1)
        up_full = assemble(place, up_near + plus_core([up_y, up_xy]), width)
        down_near = plus_core([down_o, down_x])
        middle, hidden_two = middle_forward(tokens, attended, project_full, gain_two)
        down_full = assemble(place, down_near + plus_core([down_y, down_xy]), hidden)
    else:
        gather = lambda w: lax.all_gather(w, OWN, axis=0, tiled=True)
        qkv_full, project_full, down_full, gate_full, up_full = (
            gather(w) for w in (qkv_shard, project_weight, down_weight, gate_weight, up_weight)
        )
        gains = lax.all_gather(gains_shard, OWN, axis=1, tiled=True).astype(f32)
        gain_one, gain_two = gains[0:1], gains[1:2]
        hidden_one, queries, own_kv = qkv_forward(tokens, gain_one, qkv_full, cos2, sin2)
        all_kv = window_kv(earlier_kv(own_kv), own_kv)
        attended, log_totals = attention_fwd(start, queries, all_kv)
        middle, hidden_two = middle_forward(tokens, attended, project_full, gain_two)

    act, gate_low, up_low, block_output, hidden_two_grad = feed_forward(
        hidden_two, do, gate_full, up_full, down_full, middle
    )

    def key_value_sum(key_all, value_all):
        kv_all = jnp.concatenate([key_all, value_all], axis=1)
        parts = []
        for k in range(1, reach + 1):
            low = WINDOW - k * length
            part = kv_all[max(low, 0) : low + length].astype(bf16)
            if low < 0:
                part = jnp.pad(part, ((-low, 0), (0, 0)))
            parts.append(lax.ppermute(part, "y", [(i + k, i) for i in range(seqs - k)]))
        return kv_all[WINDOW:], parts

    def key_value_grad(own, parts):
        total = own
        for part in parts:
            total = total + part.astype(f32)
        key_sum = total[:, :HD]
        key_grad = key_sum * cos2 - jnp.roll(key_sum, HD // 2, axis=1) * sin2
        return jnp.concatenate([key_grad, total[:, HD:]], axis=1).astype(bf16)

    attention_back = lambda half, grad: attention_bwd(
        start, half, queries, all_kv, attended, grad, log_totals, cos2, sin2
    )
    zero, one = jnp.zeros((1,), jnp.int32), jnp.ones((1,), jnp.int32)
    if by_hand:
        half = c.astype(jnp.int32)[None]

        def chip_grad(a, b):
            away = weight_grad(a, b, 1 - half)
            return weight_grad(a, b, half, shift(away, "c", 1))

        gate_sum, up_sum = chip_grad(hidden_two, gate_low), chip_grad(hidden_two, up_low)
        gate_sum, up_sum, hidden_two_grad, act = fence(gate_sum, up_sum, hidden_two_grad, act)
        gate_s, up_s = Scatter(gate_sum, True), Scatter(up_sum, False)
        middle_grad, branch_low, attended_grad, midnorm_part = middle_back(
            hidden_two_grad, middle, do, gain_two, project_full
        )
        down_sum = chip_grad(act, do)
        project_sum = chip_grad(attended, branch_low)
        down_sum, project_sum, attended_grad = fence(down_sum, project_sum, attended_grad)
        down_s, project_s = Scatter(down_sum, True), Scatter(project_sum, False)
        away_q, away_k, away_v = attention_back(1 - half, attended_grad)
        away_q, attended_grad = settle((away_q, attended_grad), [gate_s, up_s])
        gate_s.second()
        up_s.second()
        query_away = shift(weight_grad(hidden_one, away_q, zero, parts=1), "c", 1)
        keep_q, keep_k, keep_v = attention_back(half, attended_grad)
        keep_q, keep_k, keep_v = settle((keep_q, keep_k, keep_v), [down_s, project_s, gate_s])
        kv_own, kv_parts = key_value_sum(away_k + keep_k, away_v + keep_v)
        gate_s.third()
        down_s.second()
        project_s.second()
        query_sum = weight_grad(hidden_one, keep_q, zero, query_away, parts=1)
        query_sum, kv_parts = settle((query_sum, kv_parts), [up_s])
        up_s.third()
        kv_grad = key_value_grad(kv_own, kv_parts)
        kv_away = shift(weight_grad(hidden_one, kv_grad, 1 - half), "c", 1)
        input_grad, prenorm_part = input_back(
            half, keep_q, away_q, kv_grad, qkv_full, tokens, gain_one, middle_grad
        )
        gain_part = jnp.pad(jnp.concatenate([prenorm_part, midnorm_part]).T, ((0, 0), (0, HD - 2))).astype(bf16)
        gain_sum = add_low(gain_part, shift(gain_part, "c", 1))
        kv_sum = weight_grad(hidden_one, kv_grad, half, kv_away)
        qkv_s = Scatter(jnp.concatenate([query_sum, kv_sum, gain_sum], axis=1), True)
        settle((), [qkv_s, gate_s, down_s, project_s])
        qkv_s.second()
        gate_s.fourth()
        down_s.third()
        project_s.third()
        settle((), [qkv_s, up_s])
        qkv_s.third()
        up_s.fourth()
        settle((), [qkv_s, down_s, project_s, gate_s])
        qkv_s.fourth()
        down_s.fourth()
        project_s.fourth()
        gate_gradient, up_gradient = gate_s.whole(), up_s.whole()
        down_gradient, project_gradient = down_s.whole(), project_s.whole()
        left, right, mine = qkv_s.last()
        cut = wide // 2
        query_gradient = jnp.concatenate([left[:, :cut], right[:, :cut]], axis=1)
        key_gradient, value_gradient = left[:, cut : cut + HD], right[:, cut : cut + HD]
        gain_mine = mine[:, cut + HD : cut + HD + 2].astype(f32).T
    else:

        def summed(a, b):
            value = jnp.concatenate([weight_grad(a, b, zero), weight_grad(a, b, one)], axis=1)
            return lax.psum(lax.psum_scatter(value, OWN, scatter_dimension=0, tiled=True), "y").astype(f32)

        gate_gradient, up_gradient = summed(hidden_two, gate_low), summed(hidden_two, up_low)
        middle_grad, branch_low, attended_grad, midnorm_part = middle_back(
            hidden_two_grad, middle, do, gain_two, project_full
        )
        down_gradient, project_gradient = summed(act, do), summed(attended, branch_low)
        left_q, left_k, left_v = attention_back(zero, attended_grad)
        right_q, right_k, right_v = attention_back(one, attended_grad)
        kv_grad = key_value_grad(*key_value_sum(left_k + right_k, left_v + right_v))
        input_grad, prenorm_part = input_back(
            zero, left_q, right_q, kv_grad, qkv_full, tokens, gain_one, middle_grad
        )
        query_gradient = summed(hidden_one, jnp.concatenate([left_q, right_q], axis=1))
        kv_gradient = summed(hidden_one, kv_grad)
        key_gradient, value_gradient = kv_gradient[:, :HD], kv_gradient[:, HD:]
        gain_sums = lax.psum(jnp.concatenate([prenorm_part, midnorm_part]), ALL)
        index = (z * 2 + x) * 2 + c
        gain_mine = lax.dynamic_slice_in_dim(gain_sums, index * shard, shard, 1)
    return (
        block_output[None],
        input_grad[None],
        gain_mine[0],
        query_gradient,
        key_gradient,
        value_gradient,
        project_gradient,
        gain_mine[1],
        gate_gradient,
        up_gradient,
        down_gradient,
    )


def solution(mesh):
    owners, seqs = mesh.shape["fsdp"], mesh.shape["seq"]
    deep = owners // 4
    split = Mesh(mesh.devices.reshape(deep, 2, 2, seqs), ALL)
    rows = P(OWN, "y", None)
    weight = P(OWN, None)
    in_specs = (
        rows,
        P(OWN),
        weight,
        weight,
        weight,
        weight,
        P(OWN),
        weight,
        weight,
        weight,
        rows,
    )
    out_specs = (
        rows,
        rows,
        P(OWN),
        weight,
        weight,
        weight,
        weight,
        P(OWN),
        weight,
        weight,
        weight,
    )
    by_hand = seqs == 2 and deep == 4
    return jax.shard_map(
        functools.partial(per_device, by_hand=by_hand),
        mesh=split,
        in_specs=in_specs,
        out_specs=out_specs,
        check_vma=False,
    )
```

```python
import functools

import jax
import jax.numpy as jnp
from jax import lax
from jax.experimental import pallas as pl
from jax.experimental.pallas import tpu as pltpu
from jax.sharding import Mesh
from jax.sharding import PartitionSpec as P

HEADS = 8
HD = 128
WINDOW = 1024

norm_epsilon = 1e-06
masked_value = -1e30
LOG2E = 1.4426950408889634
bf16 = jnp.bfloat16
f32 = jnp.float32
OWN = ("z", "x", "c")
ALL = ("z", "x", "c", "y")


def nn(a, b):
    return lax.dot_general(a, b, (((1,), (0,)), ((), ())), preferred_element_type=f32)


def nt(a, b):
    return lax.dot_general(a, b, (((1,), (1,)), ((), ())), preferred_element_type=f32)


def tn(a, b):
    return lax.dot_general(a, b, (((0,), (0,)), ((), ())), preferred_element_type=f32)


def params(mib):
    return pltpu.CompilerParams(vmem_limit_bytes=mib << 20)


def cost(flops, moved, exps=0):
    return pl.CostEstimate(flops=int(flops), bytes_accessed=int(moved), transcendentals=int(exps))


def window_scores(scores, block, first_valid, limited):
    rows, keys = scores.shape
    r = lax.rem(lax.broadcasted_iota(jnp.int32, (rows, block), 0), block)
    j = lax.broadcasted_iota(jnp.int32, (rows, block), 1)
    front = jnp.where(j > r, scores[:, :block], masked_value)
    back = jnp.where(j <= r, scores[:, keys - block :], masked_value)
    scores = jnp.concatenate([front, scores[:, block : keys - block], back], axis=1)
    if limited:
        place = lax.broadcasted_iota(jnp.int32, scores.shape, 1)
        scores = jnp.where(place >= first_valid, scores, masked_value)
    return scores


def stacked(ref, heads):
    return jnp.concatenate([ref[:, a * HD : (a + 1) * HD] for a in heads], axis=0)


def attention_fwd_kernel(start_ref, q_ref, kv_ref, o_ref, lse_ref, *, block, group):
    i = pl.program_id(0)
    keys = WINDOW + block
    base = pl.multiple_of(i * block, block)
    k = kv_ref[pl.ds(base, keys), :HD]
    v = kv_ref[pl.ds(base, keys), HD:]
    ones = jnp.ones_like(v)
    value_one = jnp.concatenate([v, ones], axis=1)
    first_valid = WINDOW - start_ref[0] - i * block
    scale = HD**-0.5 * LOG2E
    lane = lax.broadcasted_iota(jnp.int32, (block, HD), 1)

    def run(limited):
        stats = [jnp.zeros((block, HD), f32)] * 2
        for g in range(HEADS // group):
            heads = range(g * group, (g + 1) * group)
            scores = window_scores(nt(stacked(q_ref, heads), k), block, first_valid, limited)
            top = jnp.max(scores, axis=1, keepdims=True) * scale
            weight = jnp.exp2(scores * scale - top).astype(bf16)
            both = nn(weight, value_one)
            total = both[:, HD:]
            out = both[:, :HD] / total
            lse = top + jnp.log2(total)
            for h, a in enumerate(heads):
                o_ref[:, a * HD : (a + 1) * HD] = out[h * block : (h + 1) * block].astype(bf16)
                at, spot = divmod(a, HEADS // 2)
                stats[at] = jnp.where(lane == spot, lse[h * block : (h + 1) * block], stats[at])
        lse_ref[...] = jnp.concatenate(stats, axis=1)

    @pl.when(first_valid <= 0)
    def _():
        run(False)

    @pl.when(first_valid > 0)
    def _():
        run(True)


def attention_fwd(start, q, kv, block=256, group=2):
    length, total = q.shape[0], kv.shape[0]
    block = min(block, length)
    rows = lambda w: pl.BlockSpec((block, w), lambda i: (i, 0))
    return pl.pallas_call(
        functools.partial(attention_fwd_kernel, block=block, group=group),
        grid=(length // block,),
        in_specs=[
            pl.BlockSpec(memory_space=pltpu.SMEM),
            rows(HEADS * HD),
            pl.BlockSpec((total, 2 * HD), lambda i: (0, 0)),
        ],
        out_specs=[rows(HEADS * HD), rows(2 * HD)],
        out_shape=[
            jax.ShapeDtypeStruct((length, HEADS * HD), bf16),
            jax.ShapeDtypeStruct((length, 2 * HD), f32),
        ],
        compiler_params=params(60),
        cost_estimate=cost(
            20 * length * HEADS * HD * WINDOW, 6 << 20, length * HEADS * WINDOW
        ),
        name="attention_fwd",
    )(start, q, kv)


def attention_bwd_kernel(
    at_ref, q_ref, kv_ref, o_ref, do_ref, lse_ref, cos_ref, sin_ref, dq_ref, dk_ref, dv_ref, *, block, group
):
    i = pl.program_id(0)
    keys = WINDOW + block
    base = pl.multiple_of(i * block, block)
    k = kv_ref[pl.ds(base, keys), :HD]
    v = kv_ref[pl.ds(base, keys), HD:]
    first_valid = WINDOW - at_ref[0] - i * block
    scale = HD**-0.5 * LOG2E

    @pl.when(i == 0)
    def _():
        dk_ref[...] = jnp.zeros_like(dk_ref)
        dv_ref[...] = jnp.zeros_like(dv_ref)

    def run(limited):
        for g in range(HEADS // 2 // group):
            heads = range(g * group, (g + 1) * group)
            q = stacked(q_ref, heads)
            do = stacked(do_ref, heads)
            o = stacked(o_ref, heads)
            lse = jnp.concatenate([lse_ref[:, a : a + 1] for a in heads], axis=0)
            inner = jnp.sum(do.astype(f32) * o.astype(f32), axis=1, keepdims=True)
            scores = window_scores(nt(q, k), block, first_valid, limited)
            prob = jnp.exp2(scores * scale - lse)
            prob_grad = nt(do, v)
            score_grad = (prob * (prob_grad - inner)).astype(bf16)
            dv_ref[pl.ds(base, keys), :] += tn(prob.astype(bf16), do)
            dk_ref[pl.ds(base, keys), :] += tn(score_grad, q)
            dq = nn(score_grad, k) * (HD**-0.5)
            for h, a in enumerate(heads):
                t = dq[h * block : (h + 1) * block]
                t = t * cos_ref[...] - pltpu.roll(t, HD // 2, 1) * sin_ref[...]
                dq_ref[:, a * HD : (a + 1) * HD] = t.astype(bf16)

    @pl.when(first_valid <= 0)
    def _():
        run(False)

    @pl.when(first_valid > 0)
    def _():
        run(True)

    @pl.when(i == pl.num_programs(0) - 1)
    def _():
        dk_ref[...] *= HD**-0.5


def attention_bwd(start, half, q, kv, o, do, lse, cos2, sin2, block=128, group=2):
    length, total = q.shape[0], kv.shape[0]
    rows = pl.BlockSpec((block, HD), lambda i, s: (i, 0))
    wide = HEADS * HD // 2
    heads = pl.BlockSpec((block, wide), lambda i, s: (i, s[1]))
    whole = lambda w: pl.BlockSpec((total, w), lambda i, s: (0, 0))
    return pl.pallas_call(
        functools.partial(attention_bwd_kernel, block=block, group=group),
        grid_spec=pltpu.PrefetchScalarGridSpec(
            num_scalar_prefetch=1,
            grid=(length // block,),
            in_specs=[
                heads,
                whole(2 * HD),
                heads,
                heads,
                pl.BlockSpec((block, HD), lambda i, s: (i, s[1])),
                rows,
                rows,
            ],
            out_specs=[pl.BlockSpec((block, wide), lambda i, s: (i, 0)), whole(HD), whole(HD)],
        ),
        out_shape=[
            jax.ShapeDtypeStruct((length, wide), bf16),
            jax.ShapeDtypeStruct((total, HD), f32),
            jax.ShapeDtypeStruct((total, HD), f32),
        ],
        compiler_params=params(60),
        cost_estimate=cost(22 * length * wide * WINDOW, 8 << 20, length * HEADS * WINDOW // 2),
        name="attention_bwd",
    )(jnp.concatenate([start, half]), q, kv, o, do, lse, cos2, sin2)


def qkv_kernel(x_ref, gain_ref, w_ref, cos_ref, sin_ref, h_ref, q_ref, kv_ref):
    x = x_ref[...].astype(f32)
    scale = lax.rsqrt(jnp.mean(x * x, axis=-1, keepdims=True) + norm_epsilon)
    h = (x * scale * gain_ref[...]).astype(bf16)
    h_ref[...] = h
    cos2, sin2 = cos_ref[...], sin_ref[...]
    for a in range(0, HEADS, 2):
        lin = nn(h, w_ref[:, a * HD : (a + 2) * HD])
        for b in range(2):
            t = lin[:, b * HD : (b + 1) * HD]
            q_ref[:, (a + b) * HD : (a + b + 1) * HD] = (
                t * cos2 + pltpu.roll(t, HD // 2, 1) * sin2
            ).astype(bf16)
    lin = nn(h, w_ref[:, HEADS * HD :])
    t = lin[:, :HD]
    kv_ref[:, :HD] = (t * cos2 + pltpu.roll(t, HD // 2, 1) * sin2).astype(bf16)
    kv_ref[:, HD:] = lin[:, HD:].astype(bf16)


def qkv_forward(x, gain, w, cos2, sin2, block=256):
    length, width = x.shape
    rows = lambda n: pl.BlockSpec((block, n), lambda i: (i, 0))
    whole = lambda a: pl.BlockSpec(a.shape, lambda i: (0, 0))
    return pl.pallas_call(
        qkv_kernel,
        grid=(length // block,),
        in_specs=[rows(width), whole(gain), whole(w), rows(HD), rows(HD)],
        out_specs=[rows(width), rows(HEADS * HD), rows(2 * HD)],
        out_shape=[
            jax.ShapeDtypeStruct((length, width), bf16),
            jax.ShapeDtypeStruct((length, HEADS * HD), bf16),
            jax.ShapeDtypeStruct((length, 2 * HD), bf16),
        ],
        compiler_params=params(60),
        cost_estimate=cost(4 * length * w.size, 12 << 20),
        name="norm_qkv",
    )(x, gain, w, cos2, sin2)


def middle_kernel(x_ref, a_ref, w_ref, gain_ref, mid_ref, h_ref):
    mid = x_ref[...].astype(f32) + nn(a_ref[...], w_ref[...])
    mid_ref[...] = mid
    scale = lax.rsqrt(jnp.mean(mid * mid, axis=-1, keepdims=True) + norm_epsilon)
    h_ref[...] = (mid * scale * gain_ref[...]).astype(bf16)


def middle_forward(x, attended, w, gain, block=256):
    length, width = x.shape
    rows = pl.BlockSpec((block, width), lambda i: (i, 0))
    whole = lambda a: pl.BlockSpec(a.shape, lambda i: (0, 0))
    return pl.pallas_call(
        middle_kernel,
        grid=(length // block,),
        in_specs=[rows, pl.BlockSpec((block, attended.shape[1]), lambda i: (i, 0)), whole(w), whole(gain)],
        out_specs=[rows, rows],
        out_shape=[
            jax.ShapeDtypeStruct((length, width), f32),
            jax.ShapeDtypeStruct((length, width), bf16),
        ],
        compiler_params=params(60),
        cost_estimate=cost(4 * length * w.size, 12 << 20),
        name="project_norm",
    )(x, attended, w, gain)


def norm_back(dn, normed, scale):
    return scale * (dn - normed * jnp.mean(dn * normed, axis=-1, keepdims=True))


def middle_back_kernel(hg_ref, mid_ref, do_ref, gain_ref, w_ref, mg_ref, low_ref, ag_ref, gain_grad_ref):
    i = pl.program_id(0)
    mid = mid_ref[...]
    hg = hg_ref[...]
    scale = lax.rsqrt(jnp.mean(mid * mid, axis=-1, keepdims=True) + norm_epsilon)
    normed = mid * scale
    mg = do_ref[...].astype(f32) + norm_back(hg * gain_ref[...], normed, scale)
    mg_ref[...] = mg
    low = mg.astype(bf16)
    low_ref[...] = low
    ag_ref[...] = nt(low, w_ref[...]).astype(bf16)

    @pl.when(i == 0)
    def _():
        gain_grad_ref[...] = jnp.zeros_like(gain_grad_ref)

    gain_grad_ref[...] += jnp.sum(hg * normed, axis=0, keepdims=True)


def middle_back(hg, mid, do, gain, w, block=256):
    length, width = mid.shape
    rows = lambda n: pl.BlockSpec((block, n), lambda i: (i, 0))
    whole = lambda s: pl.BlockSpec(s, lambda i: (0, 0))
    return pl.pallas_call(
        middle_back_kernel,
        grid=(length // block,),
        in_specs=[rows(width), rows(width), rows(width), whole(gain.shape), whole(w.shape)],
        out_specs=[rows(width), rows(width), rows(w.shape[0]), whole((1, width))],
        out_shape=[
            jax.ShapeDtypeStruct((length, width), f32),
            jax.ShapeDtypeStruct((length, width), bf16),
            jax.ShapeDtypeStruct((length, w.shape[0]), bf16),
            jax.ShapeDtypeStruct((1, width), f32),
        ],
        compiler_params=params(60),
        cost_estimate=cost(4 * length * w.size, 22 << 20),
        name="norm_two_back",
    )(hg, mid, do, gain, w)


def input_back_kernel(half_ref, keep_ref, away_ref, dkv_ref, w_ref, x_ref, gain_ref, mg_ref, out_ref, gain_grad_ref):
    i = pl.program_id(0)
    wide = keep_ref.shape[1]
    own = pl.multiple_of(half_ref[0] * wide, wide)
    hg = nt(keep_ref[...], w_ref[:, pl.ds(own, wide)]) + nt(away_ref[...], w_ref[:, pl.ds(wide - own, wide)])
    hg += nt(dkv_ref[...], w_ref[:, 2 * wide :])
    x = x_ref[...].astype(f32)
    scale = lax.rsqrt(jnp.mean(x * x, axis=-1, keepdims=True) + norm_epsilon)
    normed = x * scale
    out_ref[...] = (mg_ref[...] + norm_back(hg * gain_ref[...], normed, scale)).astype(bf16)

    @pl.when(i == 0)
    def _():
        gain_grad_ref[...] = jnp.zeros_like(gain_grad_ref)

    gain_grad_ref[...] += jnp.sum(hg * normed, axis=0, keepdims=True)


def input_back(half, keep, away, dkv, w, x, gain, mg, block=256):
    length, width = x.shape
    rows = lambda n: pl.BlockSpec((block, n), lambda i, s: (i, 0))
    whole = lambda shape: pl.BlockSpec(shape, lambda i, s: (0, 0))
    return pl.pallas_call(
        input_back_kernel,
        grid_spec=pltpu.PrefetchScalarGridSpec(
            num_scalar_prefetch=1,
            grid=(length // block,),
            in_specs=[
                rows(keep.shape[1]),
                rows(away.shape[1]),
                rows(dkv.shape[1]),
                whole(w.shape),
                rows(width),
                whole(gain.shape),
                rows(width),
            ],
            out_specs=[rows(width), whole((1, width))],
        ),
        out_shape=[
            jax.ShapeDtypeStruct((length, width), bf16),
            jax.ShapeDtypeStruct((1, width), f32),
        ],
        compiler_params=params(60),
        cost_estimate=cost(4 * length * w.size, 16 << 20),
        name="norm_one_back",
    )(half, keep, away, dkv, w, x, gain, mg)


def gelu_parts(x):
    t = 1.0 / (1.0 + (0.3275911 * 0.7071067811865476) * jnp.abs(x))
    e = jnp.exp2(x * x * (-0.5 * LOG2E))
    poly = 0.5 * 1.061405429 * t - 0.5 * 1.453152027
    poly = poly * t + 0.5 * 1.421413741
    poly = poly * t - 0.5 * 0.284496736
    poly = (poly * t + 0.5 * 0.254829592) * t
    tail = poly * e
    return jnp.where(x >= 0, 1.0 - tail, tail), x * e * 0.3989422804014327


def feed_forward_kernel(
    h_ref, do_ref, wg_ref, wu_ref, wd_ref, mid_ref, act_ref, both_ref, out_ref, hg_ref, acc
):
    j = pl.program_id(0)

    @pl.when(j == 0)
    def _():
        acc[...] = mid_ref[...]
        hg_ref[...] = jnp.zeros_like(hg_ref)

    h = h_ref[...]
    gate = nn(h, wg_ref[...])
    up = nn(h, wu_ref[...])
    act_grad = nt(do_ref[...], wd_ref[...])
    cdf, x_pdf = gelu_parts(gate)
    gelu = gate * cdf
    act = (gelu * up).astype(bf16)
    gate_grad = (act_grad * up * (cdf + x_pdf)).astype(bf16)
    up_grad = (act_grad * gelu).astype(bf16)
    act_ref[...] = act
    both_ref[0] = gate_grad
    both_ref[1] = up_grad
    acc[...] += nn(act, wd_ref[...])
    hg_ref[...] += nt(gate_grad, wg_ref[...]) + nt(up_grad, wu_ref[...])

    @pl.when(j == pl.num_programs(0) - 1)
    def _():
        out_ref[...] = acc[...].astype(bf16)


def feed_forward(h, do, wg, wu, wd, mid, chunk=512):
    length, width = h.shape
    hidden = wg.shape[1]
    whole = pl.BlockSpec((length, width), lambda j: (0, 0))
    col = lambda n: pl.BlockSpec((n, chunk), lambda j: (0, j))
    return pl.pallas_call(
        feed_forward_kernel,
        grid=(hidden // chunk,),
        in_specs=[whole, whole, col(width), col(width), pl.BlockSpec((chunk, width), lambda j: (j, 0)), whole],
        out_specs=[col(length), pl.BlockSpec((2, length, chunk), lambda j: (0, 0, j)), whole, whole],
        out_shape=[jax.ShapeDtypeStruct((length, hidden), bf16), jax.ShapeDtypeStruct((2, length, hidden), bf16)]
        + [jax.ShapeDtypeStruct((length, width), bf16), jax.ShapeDtypeStruct((length, width), f32)],
        scratch_shapes=[pltpu.VMEM((length, width), f32)],
        compiler_params=params(60),
        cost_estimate=cost(16 * length * width * hidden, 60 << 20, length * hidden),
        name="feed_forward",
    )(h, do, wg, wu, wd, mid)


def weight_grad_kernel(at_ref, a_ref, b_ref, *refs, received, split):
    value = tn(a_ref[...], b_ref[...])
    if received:
        value = value + refs[0][...].astype(f32)
    outs = refs[received:]
    value = value.astype(bf16)
    if not split:
        outs[0][...] = value
        return
    deep = len(outs) // 2
    kept, away = outs[:deep], outs[deep:]
    tiles = deep * kept[0].shape[0] * kept[0].shape[1] * 2 // value.shape[0]
    for n in range(deep):
        count, part = kept[n].shape[:2]
        first = 0 if tiles > 1 else 2 * n * count * part
        here = pl.program_id(0) == (n if tiles > 1 else 0)
        index = at_ref[1] if n < deep // 2 else at_ref[2]
        for mine in range(2):

            @pl.when(here & (index == mine))
            def _(n=n, mine=mine, first=first, count=count, part=part):
                for m in range(count):
                    for side, to in ((mine, kept[n]), (1 - mine, away[n])):
                        low = first + (2 * m + side) * part
                        to[m] = value[low : low + part]


def weight_grad(at, a, b, received=None, deep=0, parts=2):
    length, rows = a.shape
    many = b.shape[0] if b.ndim == 3 else 1
    cols = b.shape[-1] // parts
    wide = min(768, cols)
    tall = rows if rows <= 1024 else rows // 4
    per = cols // wide
    whole = pl.BlockSpec((tall, wide), lambda i, j, s: (i, j))
    if b.ndim == 3:
        of_b = pl.BlockSpec((None, length, wide), lambda i, j, s: (j // per, 0, s[0] * per + j % per))
    else:
        of_b = pl.BlockSpec((length, wide), lambda i, j, s: (0, s[0] * per + j))
    ins = [pl.BlockSpec((length, tall), lambda i, j, s: (0, i)), of_b]
    args = [a, b]
    if received is not None:
        ins.append(whole)
        args.append(received)
    if not deep:
        outs, shapes = whole, jax.ShapeDtypeStruct((rows, many * cols), bf16)
    else:
        part = rows // (4 * deep)
        sizes = [(1, 2 * part) if n < deep // 2 else (2, part) for n in range(deep)] * 2
        outs = [pl.BlockSpec((*size, wide), lambda i, j, s: (0, 0, j)) for size in sizes]
        shapes = [jax.ShapeDtypeStruct((*size, many * cols), bf16) for size in sizes]
    return pl.pallas_call(
        functools.partial(weight_grad_kernel, received=received is not None, split=deep > 0),
        grid_spec=pltpu.PrefetchScalarGridSpec(
            num_scalar_prefetch=1, grid=(rows // tall, many * per), in_specs=ins, out_specs=outs
        ),
        out_shape=shapes,
        compiler_params=params(40),
        cost_estimate=cost(4 * length * rows * cols * many, 2 * (length * rows + length * cols + 2 * rows * cols)),
        name="weight_grad",
    )(at, *args)


def shift(value, axis, k):
    n = lax.axis_size(axis)
    return lax.ppermute(value, axis, [(i, (i + k) % n) for i in range(n)])


def piece_rows(place, n, deep, total):
    z, x, c, y = place[0], place[1], place[2], place[3]
    part = total // (n * deep)
    spots = []
    for i in range(n):
        xx = x if i % 2 == 0 else 1 - x
        cc = c if (i // 2) % 2 == 0 else 1 - c
        yy = 0 if n == 4 else (y if i < 4 else 1 - y)
        for k in range(deep):
            zz = lax.rem(z - k + deep, deep)
            row = (((zz * 2 + xx) * 2 + cc) * (n // 4) + yy) * part
            spots.append(pl.ds(pl.multiple_of(row, part), part))
    return spots


def assemble_kernel(place, *refs, deep, rows):
    n = len(refs) - 4
    ins, out, held, in_sems, out_sems = refs[:n], refs[n], refs[n + 1], refs[n + 2], refs[n + 3]
    moves = []
    for at, spot in enumerate(piece_rows(place, n, deep, rows)):
        i, k = divmod(at, deep)
        part = pl.ds(0, rows // (n * deep))
        moves.append(
            (
                pltpu.make_async_copy(ins[i].at[k, part], held.at[spot], in_sems.at[i, k]),
                pltpu.make_async_copy(held.at[spot], out.at[spot], out_sems.at[i, k]),
            )
        )
    for into, _ in moves:
        into.start()
    for into, back in moves:
        into.wait()
        back.start()
    for _, back in moves:
        back.wait()


def assemble(place, pieces, rows):
    n, deep, cols = len(pieces), pieces[0].shape[0], pieces[0].shape[2]
    return pl.pallas_call(
        functools.partial(assemble_kernel, deep=deep, rows=rows),
        out_shape=jax.ShapeDtypeStruct((rows, cols), bf16),
        in_specs=[pl.BlockSpec(memory_space=pltpu.SMEM)] + [pl.BlockSpec(memory_space=pltpu.HBM)] * n,
        out_specs=pl.BlockSpec(memory_space=pltpu.HBM),
        scratch_shapes=[
            pltpu.VMEM((rows, cols), bf16),
            pltpu.SemaphoreType.DMA((n, deep)),
            pltpu.SemaphoreType.DMA((n, deep)),
        ],
        compiler_params=params(60),
        cost_estimate=cost(0, rows * cols * 4),
        name="assemble",
    )(place, *pieces)


def fence(*values):
    return lax.optimization_barrier(values)


def along_z(piece):
    return [piece] + [shift(piece, "z", k) for k in range(1, lax.axis_size("z"))]


def plus_core(pieces):
    return pieces + [shift(p, "c", 1) for p in pieces]


def pair_sum_kernel(at_ref, *refs, deep):
    kept, came, (keep_ref, x_ref, y_ref) = refs[:deep], refs[deep : 2 * deep], refs[2 * deep :]
    half = deep // 2
    for n in range(deep):
        index = at_ref[2] if n < half else at_ref[1]
        for mine in range(2):

            @pl.when(index == mine)
            def _(n=n, mine=mine):
                total = lambda side: (kept[n][side].astype(f32) + came[n][side].astype(f32)).astype(bf16)
                keep_ref[n] = total(mine)
                if n < half:
                    y_ref[n] = total(1 - mine)
                else:
                    x_ref[n - half] = total(1 - mine)


def pair_sum(at, kept, came):
    deep = len(kept)
    _, part, cols = kept[0].shape
    whole = lambda shape: pl.BlockSpec(shape, lambda i, s: (0,) * len(shape))
    shapes = [(deep, part, cols), (deep // 2, part, cols), (deep // 2, part, cols)]
    return pl.pallas_call(
        functools.partial(pair_sum_kernel, deep=deep),
        grid_spec=pltpu.PrefetchScalarGridSpec(
            num_scalar_prefetch=1,
            grid=(1,),
            in_specs=[whole((2, part, cols))] * (2 * deep),
            out_specs=[whole(shape) for shape in shapes],
        ),
        out_shape=[jax.ShapeDtypeStruct(shape, bf16) for shape in shapes],
        compiler_params=params(24),
        cost_estimate=cost(4 * deep * part * cols, 24 * deep * part * cols),
        name="pair_sum",
    )(at, *kept, *came)


def ring_sum_kernel(at_ref, a_ref, x_ref, y_ref, *outs):
    deep = len(outs)
    half = deep // 2
    for here in range(deep):

        @pl.when(at_ref[3] == here)
        def _(here=here):
            for k in range(deep):
                n = (here + k) % deep
                came = y_ref[n] if n < half else x_ref[n - half]
                outs[k][...] = (a_ref[n].astype(f32) + came.astype(f32)).astype(bf16)


def ring_sum(at, kept, over_x, over_y):
    deep, part, cols = kept.shape
    whole = lambda shape: pl.BlockSpec(shape, lambda i, s: (0,) * len(shape))
    return pl.pallas_call(
        ring_sum_kernel,
        grid_spec=pltpu.PrefetchScalarGridSpec(
            num_scalar_prefetch=1,
            grid=(1,),
            in_specs=[whole(kept.shape), whole(over_x.shape), whole(over_y.shape)],
            out_specs=[whole((part, cols))] * deep,
        ),
        out_shape=[jax.ShapeDtypeStruct((part, cols), bf16)] * deep,
        compiler_params=params(16),
        cost_estimate=cost(2 * kept.size, 12 * kept.size),
        name="ring_sum",
    )(at, kept, over_x, over_y)


def add_low(a, b):
    return (a.astype(f32) + b.astype(f32)).astype(bf16)


class Scatter:
    def __init__(self, at, arrays):
        self.at = at
        self.deep = len(arrays) // 2
        self.kept, self.away = arrays[: self.deep], arrays[self.deep :]
        self.moving = []

    def send(self, n):
        self.moving += [shift(self.away[n], "x", 1), shift(self.away[self.deep // 2 + n], "y", 1)]

    def second(self):
        shaped = lambda v: v.reshape(2, -1, v.shape[-1])
        came = self.moving[::2] + self.moving[1::2]
        self.kept, x, y = pair_sum(self.at, [shaped(k) for k in self.kept], [shaped(m) for m in came])
        self.moving = [shift(x, "x", 1), shift(y, "y", 1)]

    def total(self):
        self.kept, *self.away = ring_sum(self.at, self.kept, *self.moving)
        self.moving = []

    def along(self, k):
        self.moving.append(shift(self.away[k - 1], "z", k))

    def third(self):
        self.total()
        for k in range(1, self.deep):
            self.along(k)

    def fourth(self):
        total = self.kept.astype(f32)
        for away in self.moving:
            total = total + away.astype(f32)
        self.kept = total.astype(bf16)
        self.moving = [shift(self.kept, "y", 1)]

    def last(self):
        c, y = lax.axis_index("c"), lax.axis_index("y")
        mine = jnp.where(c == y, self.kept, self.moving[0])
        received = shift(jnp.where(c == y, self.moving[0], self.kept), "c", 1)
        left = jnp.where(c == 0, mine, received).astype(f32)
        right = jnp.where(c == 0, received, mine).astype(f32)
        return left, right, mine

    def whole(self):
        return jnp.concatenate(self.last()[:2], axis=1)


def settle(values, scatters):
    values, moving = fence(values, [s.moving for s in scatters])
    for s, m in zip(scatters, moving):
        s.moving = m
    return values


def per_device(
    tokens,
    prenorm_gain,
    query_weight,
    key_weight,
    value_weight,
    project_weight,
    midnorm_gain,
    gate_weight,
    up_weight,
    down_weight,
    out_grad,
    *,
    by_hand,
):
    z, x, c, y = (lax.axis_index(a) for a in ALL)
    deep = lax.axis_size("z")
    seqs = lax.axis_size("y")
    batch, length, width = tokens.shape
    shard = query_weight.shape[0]
    owners = width // shard
    hidden = gate_weight.shape[1]
    wide = HEADS * HD
    tokens = tokens[0]
    do = out_grad[0]

    qkv_shard = jnp.concatenate([query_weight, key_weight, value_weight], axis=1)
    gains_shard = jnp.stack([prenorm_gain, midnorm_gain])

    positions = y * length + jnp.arange(length, dtype=jnp.int32)
    frequency = 10000.0 ** (-jnp.arange(HD // 2, dtype=f32) / (HD // 2))
    angles = positions[:, None].astype(f32) * frequency
    cosine, sine = jnp.cos(angles), jnp.sin(angles)
    cos2 = jnp.concatenate([cosine, cosine], axis=1)
    sin2 = jnp.concatenate([-sine, sine], axis=1)
    start = (y * length).astype(jnp.int32)[None]

    reach = min(seqs - 1, -(-WINDOW // length))

    def earlier_kv(own_kv):
        return [lax.ppermute(own_kv, "y", [(i, i + k) for i in range(seqs - k)]) for k in range(reach, 0, -1)]

    def window_kv(earlier, own_kv):
        have = reach * length
        if have < WINDOW:
            earlier = [jnp.zeros((WINDOW - have, 2 * HD), bf16)] + earlier
        return jnp.concatenate(earlier + [own_kv], axis=0)[-(WINDOW + length) :]

    if by_hand:
        place = jnp.stack([z, x, c, y]).astype(jnp.int32)
        extra = jnp.pad(gains_shard, ((0, 14), (0, qkv_shard.shape[1] - shard)))
        own_half = lambda w: lax.dynamic_slice_in_dim(w, y * (w.shape[0] // 2), w.shape[0] // 2, 0)
        gate_z = along_z(own_half(gate_weight))
        gate_z, qkv_own = fence(gate_z, jnp.concatenate([qkv_shard, extra], axis=0))

        gate_o = jnp.stack(gate_z)
        gate_x, gate_y = shift(gate_o, "x", 1), shift(gate_o, "y", 1)
        qkv_z = along_z(qkv_own)
        qkv_z, gate_x, gate_y, up_own = fence(qkv_z, gate_x, gate_y, own_half(up_weight))

        gate_xy = shift(gate_x, "y", 1)
        gate_near = plus_core([gate_o, gate_x])
        qkv_o = jnp.stack(qkv_z)
        qkv_x = shift(qkv_o, "x", 1)
        up_z = along_z(up_own)
        up_z, qkv_x, gate_xy, gate_near, project_own = fence(up_z, qkv_x, gate_xy, gate_near, project_weight)

        up_o = jnp.stack(up_z)
        up_x, up_y = shift(up_o, "x", 1), shift(up_o, "y", 1)
        project_z = along_z(project_own)
        pieces = plus_core([qkv_o, qkv_x])
        qkv_full = assemble(place, pieces, width)
        gain_rows = jnp.concatenate([p[:, shard : shard + 2, :shard] for p in pieces]).reshape(owners, 2 * shard)
        owner = jnp.arange(owners, dtype=jnp.int32)
        slot = (((owner // 2) % 2) ^ x) * deep + ((owner % 2) ^ c) * (2 * deep) + (z - owner // 4 + deep) % deep
        pick = (slot[:, None] == owner[None, :]).astype(bf16)
        gains = jnp.dot(pick, gain_rows, preferred_element_type=f32).reshape(owners, 2, shard)
        gains = gains.transpose(1, 0, 2).reshape(2, width)
        gain_one, gain_two = gains[0:1], gains[1:2]
        hidden_one, queries, own_kv = qkv_forward(tokens, gain_one, qkv_full, cos2, sin2)
        gate_far = plus_core([gate_y, gate_xy])
        own_kv, up_x, up_y, project_z, down_own, gate_far = fence(
            own_kv, up_x, up_y, project_z, own_half(down_weight), gate_far
        )

        earlier = earlier_kv(own_kv)
        down_z = along_z(down_own)
        project_o = jnp.stack(project_z)
        project_x = shift(project_o, "x", 1)
        gate_full = assemble(place, gate_near + gate_far, width)
        up_near = plus_core([up_o, up_x])
        earlier, down_z, project_x, gate_full, up_near = fence(earlier, down_z, project_x, gate_full, up_near)

        down_o = jnp.stack(down_z)
        down_x, down_y = shift(down_o, "x", 1), shift(down_o, "y", 1)
        up_xy = shift(up_x, "y", 1)
        project_pieces = plus_core([project_o, project_x])
        all_kv = window_kv(earlier, own_kv)
        project_full = assemble(place, project_pieces, wide)
        attended, log_totals = attention_fwd(start, queries, all_kv)
        attended, down_x, down_y, up_xy, project_full = fence(attended, down_x, down_y, up_xy, project_full)

        cut = down_y.shape[1] // 2
        down_xy = jnp.concatenate([shift(down_y[:, :cut], "x", 1), shift(down_x[:, cut:], "y", 1)], axis=1)
        down_near = plus_core([down_o, down_x])
        up_full = assemble(place, up_near + plus_core([up_y, up_xy]), width)
        middle, hidden_two = middle_forward(tokens, attended, project_full, gain_two)
        down_full = assemble(place, down_near + plus_core([down_y, down_xy]), hidden)
    else:
        gather = lambda w: lax.all_gather(w, OWN, axis=0, tiled=True)
        qkv_full, project_full, down_full, gate_full, up_full = (
            gather(w) for w in (qkv_shard, project_weight, down_weight, gate_weight, up_weight)
        )
        gains = lax.all_gather(gains_shard, OWN, axis=1, tiled=True).astype(f32)
        gain_one, gain_two = gains[0:1], gains[1:2]
        hidden_one, queries, own_kv = qkv_forward(tokens, gain_one, qkv_full, cos2, sin2)
        all_kv = window_kv(earlier_kv(own_kv), own_kv)
        attended, log_totals = attention_fwd(start, queries, all_kv)
        middle, hidden_two = middle_forward(tokens, attended, project_full, gain_two)

    act, gate_up_low, block_output, hidden_two_grad = feed_forward(
        hidden_two, do, gate_full, up_full, down_full, middle
    )

    def key_value_sum(key_all, value_all):
        kv_all = jnp.concatenate([key_all, value_all], axis=1)
        parts = []
        for k in range(1, reach + 1):
            low = WINDOW - k * length
            part = kv_all[max(low, 0) : low + length].astype(bf16)
            if low < 0:
                part = jnp.pad(part, ((-low, 0), (0, 0)))
            parts.append(lax.ppermute(part, "y", [(i + k, i) for i in range(seqs - k)]))
        return kv_all[WINDOW:], parts

    def key_value_grad(own, parts):
        total = own
        for part in parts:
            total = total + part.astype(f32)
        key_sum = total[:, :HD]
        key_grad = key_sum * cos2 - jnp.roll(key_sum, HD // 2, axis=1) * sin2
        return jnp.concatenate([key_grad, total[:, HD:]], axis=1).astype(bf16)

    attention_back = lambda half, grad: attention_bwd(
        start, half, queries, all_kv, attended, grad, log_totals, cos2, sin2
    )
    zero, one = jnp.zeros((1,), jnp.int32), jnp.ones((1,), jnp.int32)
    if by_hand:
        half = c.astype(jnp.int32)[None]

        half32, x32, y32, z32 = (v.astype(jnp.int32) for v in (c, x, y, z))
        own, other = jnp.stack([half32, x32, y32, z32]), jnp.stack([1 - half32, x32, y32, z32])
        every = jnp.stack([half32 * 0, x32, y32, z32])
        gate_up_away = shift(weight_grad(other, hidden_two, gate_up_low), "c", 1)
        middle_grad, branch_low, attended_grad, midnorm_part = middle_back(
            hidden_two_grad, middle, do, gain_two, project_full
        )
        gate_up_away, branch_low, act = fence(gate_up_away, branch_low, act)

        gate_up_arrays = weight_grad(own, hidden_two, gate_up_low, gate_up_away, deep)
        down_away = shift(weight_grad(other, act, do), "c", 1)
        gate_up_arrays, down_away, branch_low, act = fence(gate_up_arrays, down_away, branch_low, act)

        gate_up_s = Scatter(own, gate_up_arrays)
        gate_up_s.send(0)
        down_arrays = weight_grad(own, act, do, down_away, deep)
        project_away = shift(weight_grad(other, attended, branch_low), "c", 1)
        down_arrays, project_away, attended_grad = settle((down_arrays, project_away, attended_grad), [gate_up_s])

        gate_up_s.send(1)
        down_s = Scatter(own, down_arrays)
        down_s.send(0)
        away_q, away_k, away_v = attention_back(1 - half, attended_grad)
        away_q, attended_grad, project_away = settle((away_q, attended_grad, project_away), [gate_up_s, down_s])

        gate_up_s.second()
        down_s.send(1)
        query_away = shift(weight_grad(every, hidden_one, away_q, parts=1), "c", 1)
        keep_q, keep_k, keep_v = attention_back(half, attended_grad)
        keep_q, keep_k, keep_v, query_away = settle((keep_q, keep_k, keep_v, query_away), [gate_up_s, down_s])

        gate_up_s.total()
        gate_up_s.kept, gate_up_s.away, keep_k, keep_v, keep_q = fence(
            gate_up_s.kept, gate_up_s.away, keep_k, keep_v, keep_q
        )
        kv_own, kv_parts = key_value_sum(away_k + keep_k, away_v + keep_v)
        gate_up_s.along(1), gate_up_s.along(2)
        query_sum = weight_grad(every, hidden_one, keep_q, query_away, parts=1)
        project_sum = weight_grad(own, attended, branch_low, project_away)
        query_sum, project_sum, kv_parts = settle((query_sum, project_sum, kv_parts), [gate_up_s])

        down_s.second()
        gate_up_s.along(3)
        kv_grad = key_value_grad(kv_own, kv_parts)
        kv_away = shift(weight_grad(other, hidden_one, kv_grad), "c", 1)
        input_grad, prenorm_part = input_back(
            half, keep_q, away_q, kv_grad, qkv_full, tokens, gain_one, middle_grad
        )
        gain_part = jnp.pad(jnp.concatenate([prenorm_part, midnorm_part]).T, ((0, 0), (0, HD - 2))).astype(bf16)
        gain_sum = add_low(gain_part, shift(gain_part, "c", 1))
        kv_sum = weight_grad(own, hidden_one, kv_grad, kv_away)
        rest = jnp.concatenate([query_sum, project_sum, kv_sum, gain_sum], axis=1)
        cols = rest.shape[1]
        rest = rest.reshape(deep, 2, 2, -1, cols)
        of_x = lambda n, index: lax.dynamic_index_in_dim(rest[n], index, 0, False).reshape(1, -1, cols)
        of_y = lambda n, index: lax.dynamic_index_in_dim(rest[n], index, 1, False)
        low, high = range(deep // 2), range(deep // 2, deep)
        stays = [of_x(n, x) for n in low] + [of_y(n, y) for n in high]
        goes = jnp.concatenate([of_x(n, 1 - x) for n in low]), jnp.concatenate([of_y(n, 1 - y) for n in high])
        stays, goes = settle((stays, goes), [down_s])

        came_x, came_y = shift(goes[0], "x", 1), shift(goes[1], "y", 1)
        down_s.third()
        came_x, came_y = settle((came_x, came_y), [gate_up_s])
        rest_s = Scatter(own, stays + stays)
        came_y = came_y.reshape(deep // 2, 2, -1, cols)
        for n in low:
            rest_s.moving += [came_x[n], came_y[n]]

        rest_s.second()
        gate_up_s.fourth()
        settle((), [rest_s, down_s, gate_up_s])

        rest_s.third()
        down_s.fourth()
        settle((), [rest_s, down_s])

        rest_s.fourth()
        left, right, _ = gate_up_s.last()
        wide_half = hidden // 2
        gate_gradient = jnp.concatenate([left[:, :wide_half], right[:, :wide_half]], axis=1)
        up_gradient = jnp.concatenate([left[:, wide_half:], right[:, wide_half:]], axis=1)
        down_gradient = down_s.whole()
        left, right, mine = rest_s.last()
        cut = wide // 2
        query_gradient = jnp.concatenate([left[:, :cut], right[:, :cut]], axis=1)
        project_gradient = jnp.concatenate([left[:, cut : 2 * cut], right[:, cut : 2 * cut]], axis=1)
        key_gradient, value_gradient = left[:, 2 * cut : 2 * cut + HD], right[:, 2 * cut : 2 * cut + HD]
        gain_mine = mine[:, 2 * cut + HD : 2 * cut + HD + 2].astype(f32).T
    else:

        def summed(a, b):
            value = jnp.concatenate([weight_grad(zero, a, b), weight_grad(one, a, b)], axis=1)
            return lax.psum(lax.psum_scatter(value, OWN, scatter_dimension=0, tiled=True), "y").astype(f32)

        gate_gradient, up_gradient = summed(hidden_two, gate_up_low[0]), summed(hidden_two, gate_up_low[1])
        middle_grad, branch_low, attended_grad, midnorm_part = middle_back(
            hidden_two_grad, middle, do, gain_two, project_full
        )
        down_gradient, project_gradient = summed(act, do), summed(attended, branch_low)
        left_q, left_k, left_v = attention_back(zero, attended_grad)
        right_q, right_k, right_v = attention_back(one, attended_grad)
        kv_grad = key_value_grad(*key_value_sum(left_k + right_k, left_v + right_v))
        input_grad, prenorm_part = input_back(
            zero, left_q, right_q, kv_grad, qkv_full, tokens, gain_one, middle_grad
        )
        query_gradient = summed(hidden_one, jnp.concatenate([left_q, right_q], axis=1))
        kv_gradient = summed(hidden_one, kv_grad)
        key_gradient, value_gradient = kv_gradient[:, :HD], kv_gradient[:, HD:]
        gain_sums = lax.psum(jnp.concatenate([prenorm_part, midnorm_part]), ALL)
        index = (z * 2 + x) * 2 + c
        gain_mine = lax.dynamic_slice_in_dim(gain_sums, index * shard, shard, 1)
    return (
        block_output[None],
        input_grad[None],
        gain_mine[0],
        query_gradient,
        key_gradient,
        value_gradient,
        project_gradient,
        gain_mine[1],
        gate_gradient,
        up_gradient,
        down_gradient,
    )


def solution(mesh):
    owners, seqs = mesh.shape["fsdp"], mesh.shape["seq"]
    deep = owners // 4
    split = Mesh(mesh.devices.reshape(deep, 2, 2, seqs), ALL)
    rows = P(OWN, "y", None)
    weight = P(OWN, None)
    in_specs = (
        rows,
        P(OWN),
        weight,
        weight,
        weight,
        weight,
        P(OWN),
        weight,
        weight,
        weight,
        rows,
    )
    out_specs = (
        rows,
        rows,
        P(OWN),
        weight,
        weight,
        weight,
        weight,
        P(OWN),
        weight,
        weight,
        weight,
    )
    by_hand = seqs == 2 and deep == 4
    return jax.shard_map(
        functools.partial(per_device, by_hand=by_hand),
        mesh=split,
        in_specs=in_specs,
        out_specs=out_specs,
        check_vma=False,
    )
```

```python
import functools

import jax
import jax.numpy as jnp
from jax import lax
from jax.experimental import pallas as pl
from jax.experimental.pallas import tpu as pltpu
from jax.sharding import Mesh
from jax.sharding import PartitionSpec as P

HEADS = 8
HD = 128
WINDOW = 1024

norm_epsilon = 1e-06
masked_value = -1e30
LOG2E = 1.4426950408889634
bf16 = jnp.bfloat16
f32 = jnp.float32
OWN = ("z", "x", "c")
ALL = ("z", "x", "c", "y")


def nn(a, b):
    return lax.dot_general(a, b, (((1,), (0,)), ((), ())), preferred_element_type=f32)


def nt(a, b):
    return lax.dot_general(a, b, (((1,), (1,)), ((), ())), preferred_element_type=f32)


def tn(a, b):
    return lax.dot_general(a, b, (((0,), (0,)), ((), ())), preferred_element_type=f32)


def params(mib):
    return pltpu.CompilerParams(vmem_limit_bytes=mib << 20)


def cost(flops, moved, exps=0):
    return pl.CostEstimate(flops=int(flops), bytes_accessed=int(moved), transcendentals=int(exps))


def window_scores(scores, block, first_valid, limited):
    rows, keys = scores.shape
    r = lax.rem(lax.broadcasted_iota(jnp.int32, (rows, block), 0), block)
    j = lax.broadcasted_iota(jnp.int32, (rows, block), 1)
    front = jnp.where(j > r, scores[:, :block], masked_value)
    back = jnp.where(j <= r, scores[:, keys - block :], masked_value)
    scores = jnp.concatenate([front, scores[:, block : keys - block], back], axis=1)
    if limited:
        place = lax.broadcasted_iota(jnp.int32, scores.shape, 1)
        scores = jnp.where(place >= first_valid, scores, masked_value)
    return scores


def stacked(ref, heads):
    return jnp.concatenate([ref[:, a * HD : (a + 1) * HD] for a in heads], axis=0)


def attention_fwd_kernel(start_ref, q_ref, kv_ref, o_ref, lse_ref, *, block, group):
    i = pl.program_id(0)
    keys = WINDOW + block
    base = pl.multiple_of(i * block, block)
    k = kv_ref[pl.ds(base, keys), :HD]
    v = kv_ref[pl.ds(base, keys), HD:]
    ones = jnp.ones_like(v)
    value_one = jnp.concatenate([v, ones], axis=1)
    first_valid = WINDOW - start_ref[0] - i * block
    scale = HD**-0.5 * LOG2E
    lane = lax.broadcasted_iota(jnp.int32, (block, HD), 1)

    def run(limited):
        stats = [jnp.zeros((block, HD), f32)] * 2
        for g in range(HEADS // group):
            heads = range(g * group, (g + 1) * group)
            scores = window_scores(nt(stacked(q_ref, heads), k), block, first_valid, limited)
            top = jnp.max(scores, axis=1, keepdims=True) * scale
            weight = jnp.exp2(scores * scale - top).astype(bf16)
            both = nn(weight, value_one)
            total = both[:, HD:]
            out = both[:, :HD] / total
            lse = top + jnp.log2(total)
            for h, a in enumerate(heads):
                o_ref[:, a * HD : (a + 1) * HD] = out[h * block : (h + 1) * block].astype(bf16)
                at, spot = divmod(a, HEADS // 2)
                stats[at] = jnp.where(lane == spot, lse[h * block : (h + 1) * block], stats[at])
        lse_ref[...] = jnp.concatenate(stats, axis=1)

    @pl.when(first_valid <= 0)
    def _():
        run(False)

    @pl.when(first_valid > 0)
    def _():
        run(True)


def attention_fwd(start, q, kv, block=256, group=2):
    length, total = q.shape[0], kv.shape[0]
    block = min(block, length)
    rows = lambda w: pl.BlockSpec((block, w), lambda i: (i, 0))
    return pl.pallas_call(
        functools.partial(attention_fwd_kernel, block=block, group=group),
        grid=(length // block,),
        in_specs=[
            pl.BlockSpec(memory_space=pltpu.SMEM),
            rows(HEADS * HD),
            pl.BlockSpec((total, 2 * HD), lambda i: (0, 0)),
        ],
        out_specs=[rows(HEADS * HD), rows(2 * HD)],
        out_shape=[
            jax.ShapeDtypeStruct((length, HEADS * HD), bf16),
            jax.ShapeDtypeStruct((length, 2 * HD), f32),
        ],
        compiler_params=params(60),
        cost_estimate=cost(
            20 * length * HEADS * HD * WINDOW, 6 << 20, length * HEADS * WINDOW
        ),
        name="attention_fwd",
    )(start, q, kv)


def attention_bwd_kernel(
    at_ref, q_ref, kv_ref, o_ref, do_ref, lse_ref, cos_ref, sin_ref, dq_ref, dk_ref, dv_ref, *, block, group
):
    i = pl.program_id(0)
    keys = WINDOW + block
    base = pl.multiple_of(i * block, block)
    k = kv_ref[pl.ds(base, keys), :HD]
    v = kv_ref[pl.ds(base, keys), HD:]
    first_valid = WINDOW - at_ref[0] - i * block
    scale = HD**-0.5 * LOG2E

    @pl.when(i == 0)
    def _():
        dk_ref[...] = jnp.zeros_like(dk_ref)
        dv_ref[...] = jnp.zeros_like(dv_ref)

    def run(limited):
        for g in range(HEADS // 2 // group):
            heads = range(g * group, (g + 1) * group)
            q = stacked(q_ref, heads)
            do = stacked(do_ref, heads)
            o = stacked(o_ref, heads)
            lse = jnp.concatenate([lse_ref[:, a : a + 1] for a in heads], axis=0)
            inner = jnp.sum(do.astype(f32) * o.astype(f32), axis=1, keepdims=True)
            scores = window_scores(nt(q, k), block, first_valid, limited)
            prob = jnp.exp2(scores * scale - lse)
            prob_grad = nt(do, v)
            score_grad = (prob * (prob_grad - inner)).astype(bf16)
            dv_ref[pl.ds(base, keys), :] += tn(prob.astype(bf16), do)
            dk_ref[pl.ds(base, keys), :] += tn(score_grad, q)
            dq = nn(score_grad, k) * (HD**-0.5)
            for h, a in enumerate(heads):
                t = dq[h * block : (h + 1) * block]
                t = t * cos_ref[...] - pltpu.roll(t, HD // 2, 1) * sin_ref[...]
                dq_ref[:, a * HD : (a + 1) * HD] = t.astype(bf16)

    @pl.when(first_valid <= 0)
    def _():
        run(False)

    @pl.when(first_valid > 0)
    def _():
        run(True)

    @pl.when(i == pl.num_programs(0) - 1)
    def _():
        dk_ref[...] *= HD**-0.5


def attention_bwd(start, half, q, kv, o, do, lse, cos2, sin2, block=128, group=2):
    length, total = q.shape[0], kv.shape[0]
    rows = pl.BlockSpec((block, HD), lambda i, s: (i, 0))
    wide = HEADS * HD // 2
    heads = pl.BlockSpec((block, wide), lambda i, s: (i, s[1]))
    whole = lambda w: pl.BlockSpec((total, w), lambda i, s: (0, 0))
    return pl.pallas_call(
        functools.partial(attention_bwd_kernel, block=block, group=group),
        grid_spec=pltpu.PrefetchScalarGridSpec(
            num_scalar_prefetch=1,
            grid=(length // block,),
            in_specs=[
                heads,
                whole(2 * HD),
                heads,
                heads,
                pl.BlockSpec((block, HD), lambda i, s: (i, s[1])),
                rows,
                rows,
            ],
            out_specs=[pl.BlockSpec((block, wide), lambda i, s: (i, 0)), whole(HD), whole(HD)],
        ),
        out_shape=[
            jax.ShapeDtypeStruct((length, wide), bf16),
            jax.ShapeDtypeStruct((total, HD), f32),
            jax.ShapeDtypeStruct((total, HD), f32),
        ],
        compiler_params=params(60),
        cost_estimate=cost(22 * length * wide * WINDOW, 8 << 20, length * HEADS * WINDOW // 2),
        name="attention_bwd",
    )(jnp.concatenate([start, half]), q, kv, o, do, lse, cos2, sin2)


def qkv_kernel(x_ref, gain_ref, w_ref, cos_ref, sin_ref, h_ref, q_ref, kv_ref):
    x = x_ref[...].astype(f32)
    scale = lax.rsqrt(jnp.mean(x * x, axis=-1, keepdims=True) + norm_epsilon)
    h = (x * scale * gain_ref[...]).astype(bf16)
    h_ref[...] = h
    cos2, sin2 = cos_ref[...], sin_ref[...]
    for a in range(0, HEADS, 2):
        lin = nn(h, w_ref[:, a * HD : (a + 2) * HD])
        for b in range(2):
            t = lin[:, b * HD : (b + 1) * HD]
            q_ref[:, (a + b) * HD : (a + b + 1) * HD] = (
                t * cos2 + pltpu.roll(t, HD // 2, 1) * sin2
            ).astype(bf16)
    lin = nn(h, w_ref[:, HEADS * HD :])
    t = lin[:, :HD]
    kv_ref[:, :HD] = (t * cos2 + pltpu.roll(t, HD // 2, 1) * sin2).astype(bf16)
    kv_ref[:, HD:] = lin[:, HD:].astype(bf16)


def qkv_forward(x, gain, w, cos2, sin2, block=256):
    length, width = x.shape
    rows = lambda n: pl.BlockSpec((block, n), lambda i: (i, 0))
    whole = lambda a: pl.BlockSpec(a.shape, lambda i: (0, 0))
    return pl.pallas_call(
        qkv_kernel,
        grid=(length // block,),
        in_specs=[rows(width), whole(gain), whole(w), rows(HD), rows(HD)],
        out_specs=[rows(width), rows(HEADS * HD), rows(2 * HD)],
        out_shape=[
            jax.ShapeDtypeStruct((length, width), bf16),
            jax.ShapeDtypeStruct((length, HEADS * HD), bf16),
            jax.ShapeDtypeStruct((length, 2 * HD), bf16),
        ],
        compiler_params=params(60),
        cost_estimate=cost(4 * length * w.size, 12 << 20),
        name="norm_qkv",
    )(x, gain, w, cos2, sin2)


def middle_kernel(x_ref, a_ref, w_ref, gain_ref, mid_ref, h_ref):
    mid = x_ref[...].astype(f32) + nn(a_ref[...], w_ref[...])
    mid_ref[...] = mid
    scale = lax.rsqrt(jnp.mean(mid * mid, axis=-1, keepdims=True) + norm_epsilon)
    h_ref[...] = (mid * scale * gain_ref[...]).astype(bf16)


def middle_forward(x, attended, w, gain, block=256):
    length, width = x.shape
    rows = pl.BlockSpec((block, width), lambda i: (i, 0))
    whole = lambda a: pl.BlockSpec(a.shape, lambda i: (0, 0))
    return pl.pallas_call(
        middle_kernel,
        grid=(length // block,),
        in_specs=[rows, pl.BlockSpec((block, attended.shape[1]), lambda i: (i, 0)), whole(w), whole(gain)],
        out_specs=[rows, rows],
        out_shape=[
            jax.ShapeDtypeStruct((length, width), f32),
            jax.ShapeDtypeStruct((length, width), bf16),
        ],
        compiler_params=params(60),
        cost_estimate=cost(4 * length * w.size, 12 << 20),
        name="project_norm",
    )(x, attended, w, gain)


def norm_back(dn, normed, scale):
    return scale * (dn - normed * jnp.mean(dn * normed, axis=-1, keepdims=True))


def middle_back_kernel(hg_ref, mid_ref, do_ref, gain_ref, w_ref, mg_ref, low_ref, ag_ref, gain_grad_ref):
    i = pl.program_id(0)
    mid = mid_ref[...]
    hg = hg_ref[...]
    scale = lax.rsqrt(jnp.mean(mid * mid, axis=-1, keepdims=True) + norm_epsilon)
    normed = mid * scale
    mg = do_ref[...].astype(f32) + norm_back(hg * gain_ref[...], normed, scale)
    mg_ref[...] = mg
    low = mg.astype(bf16)
    low_ref[...] = low
    ag_ref[...] = nt(low, w_ref[...]).astype(bf16)

    @pl.when(i == 0)
    def _():
        gain_grad_ref[...] = jnp.zeros_like(gain_grad_ref)

    gain_grad_ref[...] += jnp.sum(hg * normed, axis=0, keepdims=True)


def middle_back(hg, mid, do, gain, w, block=256):
    length, width = mid.shape
    rows = lambda n: pl.BlockSpec((block, n), lambda i: (i, 0))
    whole = lambda s: pl.BlockSpec(s, lambda i: (0, 0))
    return pl.pallas_call(
        middle_back_kernel,
        grid=(length // block,),
        in_specs=[rows(width), rows(width), rows(width), whole(gain.shape), whole(w.shape)],
        out_specs=[rows(width), rows(width), rows(w.shape[0]), whole((1, width))],
        out_shape=[
            jax.ShapeDtypeStruct((length, width), f32),
            jax.ShapeDtypeStruct((length, width), bf16),
            jax.ShapeDtypeStruct((length, w.shape[0]), bf16),
            jax.ShapeDtypeStruct((1, width), f32),
        ],
        compiler_params=params(60),
        cost_estimate=cost(4 * length * w.size, 22 << 20),
        name="norm_two_back",
    )(hg, mid, do, gain, w)


def input_back_kernel(half_ref, keep_ref, away_ref, dkv_ref, w_ref, x_ref, gain_ref, mg_ref, out_ref, gain_grad_ref):
    i = pl.program_id(0)
    wide = keep_ref.shape[1]
    own = pl.multiple_of(half_ref[0] * wide, wide)
    hg = nt(keep_ref[...], w_ref[:, pl.ds(own, wide)]) + nt(away_ref[...], w_ref[:, pl.ds(wide - own, wide)])
    hg += nt(dkv_ref[...], w_ref[:, 2 * wide :])
    x = x_ref[...].astype(f32)
    scale = lax.rsqrt(jnp.mean(x * x, axis=-1, keepdims=True) + norm_epsilon)
    normed = x * scale
    out_ref[...] = (mg_ref[...] + norm_back(hg * gain_ref[...], normed, scale)).astype(bf16)

    @pl.when(i == 0)
    def _():
        gain_grad_ref[...] = jnp.zeros_like(gain_grad_ref)

    gain_grad_ref[...] += jnp.sum(hg * normed, axis=0, keepdims=True)


def input_back(half, keep, away, dkv, w, x, gain, mg, block=256):
    length, width = x.shape
    rows = lambda n: pl.BlockSpec((block, n), lambda i, s: (i, 0))
    whole = lambda shape: pl.BlockSpec(shape, lambda i, s: (0, 0))
    return pl.pallas_call(
        input_back_kernel,
        grid_spec=pltpu.PrefetchScalarGridSpec(
            num_scalar_prefetch=1,
            grid=(length // block,),
            in_specs=[
                rows(keep.shape[1]),
                rows(away.shape[1]),
                rows(dkv.shape[1]),
                whole(w.shape),
                rows(width),
                whole(gain.shape),
                rows(width),
            ],
            out_specs=[rows(width), whole((1, width))],
        ),
        out_shape=[
            jax.ShapeDtypeStruct((length, width), bf16),
            jax.ShapeDtypeStruct((1, width), f32),
        ],
        compiler_params=params(60),
        cost_estimate=cost(4 * length * w.size, 16 << 20),
        name="norm_one_back",
    )(half, keep, away, dkv, w, x, gain, mg)


def gelu_parts(x):
    t = 1.0 / (1.0 + (0.3275911 * 0.7071067811865476) * jnp.abs(x))
    e = jnp.exp2(x * x * (-0.5 * LOG2E))
    poly = 0.5 * 1.061405429 * t - 0.5 * 1.453152027
    poly = poly * t + 0.5 * 1.421413741
    poly = poly * t - 0.5 * 0.284496736
    poly = (poly * t + 0.5 * 0.254829592) * t
    tail = poly * e
    return jnp.where(x >= 0, 1.0 - tail, tail), x * e * 0.3989422804014327


def feed_forward_kernel(
    h_ref, do_ref, wg_ref, wu_ref, wd_ref, mid_ref, act_ref, both_ref, out_ref, hg_ref, acc
):
    j = pl.program_id(0)

    @pl.when(j == 0)
    def _():
        acc[...] = mid_ref[...]
        hg_ref[...] = jnp.zeros_like(hg_ref)

    h = h_ref[...]
    gate = nn(h, wg_ref[...])
    up = nn(h, wu_ref[...])
    act_grad = nt(do_ref[...], wd_ref[...])
    cdf, x_pdf = gelu_parts(gate)
    gelu = gate * cdf
    act = (gelu * up).astype(bf16)
    gate_grad = (act_grad * up * (cdf + x_pdf)).astype(bf16)
    up_grad = (act_grad * gelu).astype(bf16)
    act_ref[...] = act
    both_ref[0] = gate_grad
    both_ref[1] = up_grad
    acc[...] += nn(act, wd_ref[...])
    hg_ref[...] += nt(gate_grad, wg_ref[...]) + nt(up_grad, wu_ref[...])

    @pl.when(j == pl.num_programs(0) - 1)
    def _():
        out_ref[...] = acc[...].astype(bf16)


def feed_forward(h, do, wg, wu, wd, mid, chunk=512):
    length, width = h.shape
    hidden = wg.shape[1]
    whole = pl.BlockSpec((length, width), lambda j: (0, 0))
    col = lambda n: pl.BlockSpec((n, chunk), lambda j: (0, j))
    return pl.pallas_call(
        feed_forward_kernel,
        grid=(hidden // chunk,),
        in_specs=[whole, whole, col(width), col(width), pl.BlockSpec((chunk, width), lambda j: (j, 0)), whole],
        out_specs=[col(length), pl.BlockSpec((2, length, chunk), lambda j: (0, 0, j)), whole, whole],
        out_shape=[jax.ShapeDtypeStruct((length, hidden), bf16), jax.ShapeDtypeStruct((2, length, hidden), bf16)]
        + [jax.ShapeDtypeStruct((length, width), bf16), jax.ShapeDtypeStruct((length, width), f32)],
        scratch_shapes=[pltpu.VMEM((length, width), f32)],
        compiler_params=params(60),
        cost_estimate=cost(16 * length * width * hidden, 60 << 20, length * hidden),
        name="feed_forward",
    )(h, do, wg, wu, wd, mid)


def weight_grad_kernel(at_ref, a_ref, b_ref, *refs, received, split):
    value = tn(a_ref[...], b_ref[...])
    if received:
        value = value + refs[0][...].astype(f32)
    outs = refs[received:]
    value = value.astype(bf16)
    if not split:
        outs[0][...] = value
        return
    deep = len(outs) // 2
    kept, away = outs[:deep], outs[deep:]
    tiles = deep * kept[0].shape[0] * kept[0].shape[1] * 2 // value.shape[0]
    for n in range(deep):
        count, part = kept[n].shape[:2]
        first = 0 if tiles > 1 else 2 * n * count * part
        here = pl.program_id(0) == (n if tiles > 1 else 0)
        index = at_ref[1] if n < deep // 2 else at_ref[2]
        for mine in range(2):

            @pl.when(here & (index == mine))
            def _(n=n, mine=mine, first=first, count=count, part=part):
                for m in range(count):
                    for side, to in ((mine, kept[n]), (1 - mine, away[n])):
                        low = first + (2 * m + side) * part
                        to[m] = value[low : low + part]


def weight_grad(at, a, b, received=None, deep=0, parts=2):
    length, rows = a.shape
    many = b.shape[0] if b.ndim == 3 else 1
    cols = b.shape[-1] // parts
    wide = 768 if cols % 768 == 0 else min(512, cols)
    tall = rows if rows <= 1024 else rows // 4
    per = cols // wide
    whole = pl.BlockSpec((tall, wide), lambda i, j, s: (i, j))
    if b.ndim == 3:
        of_b = pl.BlockSpec((None, length, wide), lambda i, j, s: (j // per, 0, s[0] * per + j % per))
    else:
        of_b = pl.BlockSpec((length, wide), lambda i, j, s: (0, s[0] * per + j))
    ins = [pl.BlockSpec((length, tall), lambda i, j, s: (0, i)), of_b]
    args = [a, b]
    if received is not None:
        ins.append(whole)
        args.append(received)
    if not deep:
        outs, shapes = whole, jax.ShapeDtypeStruct((rows, many * cols), bf16)
    else:
        part = rows // (4 * deep)
        sizes = [(1, 2 * part) if n < deep // 2 else (2, part) for n in range(deep)] * 2
        outs = [pl.BlockSpec((*size, wide), lambda i, j, s: (0, 0, j)) for size in sizes]
        shapes = [jax.ShapeDtypeStruct((*size, many * cols), bf16) for size in sizes]
    return pl.pallas_call(
        functools.partial(weight_grad_kernel, received=received is not None, split=deep > 0),
        grid_spec=pltpu.PrefetchScalarGridSpec(
            num_scalar_prefetch=1, grid=(rows // tall, many * per), in_specs=ins, out_specs=outs
        ),
        out_shape=shapes,
        compiler_params=params(40),
        cost_estimate=cost(4 * length * rows * cols * many, 2 * (length * rows + length * cols + 2 * rows * cols)),
        name="weight_grad",
    )(at, *args)


def shift(value, axis, k):
    n = lax.axis_size(axis)
    return lax.ppermute(value, axis, [(i, (i + k) % n) for i in range(n)])


def piece_rows(place, n, deep, total):
    z, x, c, y = place[0], place[1], place[2], place[3]
    part = total // (n * deep)
    spots = []
    for i in range(n):
        xx = x if i % 2 == 0 else 1 - x
        cc = c if (i // 2) % 2 == 0 else 1 - c
        yy = 0 if n == 4 else (y if i < 4 else 1 - y)
        for k in range(deep):
            zz = lax.rem(z - k + deep, deep)
            row = (((zz * 2 + xx) * 2 + cc) * (n // 4) + yy) * part
            spots.append(pl.ds(pl.multiple_of(row, part), part))
    return spots


def assemble_kernel(place, *refs, deep, rows):
    n = len(refs) - 4
    ins, out, held, in_sems, out_sems = refs[:n], refs[n], refs[n + 1], refs[n + 2], refs[n + 3]
    moves = []
    for at, spot in enumerate(piece_rows(place, n, deep, rows)):
        i, k = divmod(at, deep)
        part = pl.ds(0, rows // (n * deep))
        moves.append(
            (
                pltpu.make_async_copy(ins[i].at[k, part], held.at[spot], in_sems.at[i, k]),
                pltpu.make_async_copy(held.at[spot], out.at[spot], out_sems.at[i, k]),
            )
        )
    for into, _ in moves:
        into.start()
    for into, back in moves:
        into.wait()
        back.start()
    for _, back in moves:
        back.wait()


def assemble(place, pieces, rows):
    n, deep, cols = len(pieces), pieces[0].shape[0], pieces[0].shape[2]
    return pl.pallas_call(
        functools.partial(assemble_kernel, deep=deep, rows=rows),
        out_shape=jax.ShapeDtypeStruct((rows, cols), bf16),
        in_specs=[pl.BlockSpec(memory_space=pltpu.SMEM)] + [pl.BlockSpec(memory_space=pltpu.HBM)] * n,
        out_specs=pl.BlockSpec(memory_space=pltpu.HBM),
        scratch_shapes=[
            pltpu.VMEM((rows, cols), bf16),
            pltpu.SemaphoreType.DMA((n, deep)),
            pltpu.SemaphoreType.DMA((n, deep)),
        ],
        compiler_params=params(60),
        cost_estimate=cost(0, rows * cols * 4),
        name="assemble",
    )(place, *pieces)


def fence(*values):
    return lax.optimization_barrier(values)


def along_z(piece):
    return [piece] + [shift(piece, "z", k) for k in range(1, lax.axis_size("z"))]


def plus_core(pieces):
    return pieces + [shift(p, "c", 1) for p in pieces]


def pair_sum_kernel(at_ref, *refs, deep):
    kept, came, (keep_ref, x_ref, y_ref) = refs[:deep], refs[deep : 2 * deep], refs[2 * deep :]
    half = deep // 2
    for n in range(deep):
        index = at_ref[2] if n < half else at_ref[1]
        for mine in range(2):

            @pl.when(index == mine)
            def _(n=n, mine=mine):
                total = lambda side: (kept[n][side].astype(f32) + came[n][side].astype(f32)).astype(bf16)
                keep_ref[n] = total(mine)
                if n < half:
                    y_ref[n] = total(1 - mine)
                else:
                    x_ref[n - half] = total(1 - mine)


def pair_sum(at, kept, came):
    deep = len(kept)
    _, part, cols = kept[0].shape
    whole = lambda shape: pl.BlockSpec(shape, lambda i, s: (0,) * len(shape))
    shapes = [(deep, part, cols), (deep // 2, part, cols), (deep // 2, part, cols)]
    return pl.pallas_call(
        functools.partial(pair_sum_kernel, deep=deep),
        grid_spec=pltpu.PrefetchScalarGridSpec(
            num_scalar_prefetch=1,
            grid=(1,),
            in_specs=[whole((2, part, cols))] * (2 * deep),
            out_specs=[whole(shape) for shape in shapes],
        ),
        out_shape=[jax.ShapeDtypeStruct(shape, bf16) for shape in shapes],
        compiler_params=params(24),
        cost_estimate=cost(4 * deep * part * cols, 24 * deep * part * cols),
        name="pair_sum",
    )(at, *kept, *came)


def ring_sum_kernel(at_ref, a_ref, x_ref, y_ref, *outs):
    deep = len(outs)
    half = deep // 2
    for here in range(deep):

        @pl.when(at_ref[3] == here)
        def _(here=here):
            for k in range(deep):
                n = (here + k) % deep
                came = y_ref[n] if n < half else x_ref[n - half]
                outs[k][...] = (a_ref[n].astype(f32) + came.astype(f32)).astype(bf16)


def ring_sum(at, kept, over_x, over_y):
    deep, part, cols = kept.shape
    whole = lambda shape: pl.BlockSpec(shape, lambda i, s: (0,) * len(shape))
    return pl.pallas_call(
        ring_sum_kernel,
        grid_spec=pltpu.PrefetchScalarGridSpec(
            num_scalar_prefetch=1,
            grid=(1,),
            in_specs=[whole(kept.shape), whole(over_x.shape), whole(over_y.shape)],
            out_specs=[whole((part, cols))] * deep,
        ),
        out_shape=[jax.ShapeDtypeStruct((part, cols), bf16)] * deep,
        compiler_params=params(16),
        cost_estimate=cost(2 * kept.size, 12 * kept.size),
        name="ring_sum",
    )(at, kept, over_x, over_y)


def add_low(a, b):
    return (a.astype(f32) + b.astype(f32)).astype(bf16)


class Scatter:
    def __init__(self, at, arrays):
        self.at = at
        self.deep = len(arrays) // 2
        self.kept, self.away = arrays[: self.deep], arrays[self.deep :]
        self.moving = []

    def send(self, n):
        self.moving += [shift(self.away[n], "x", 1), shift(self.away[self.deep // 2 + n], "y", 1)]

    def second(self):
        shaped = lambda v: v.reshape(2, -1, v.shape[-1])
        came = self.moving[::2] + self.moving[1::2]
        self.kept, x, y = pair_sum(self.at, [shaped(k) for k in self.kept], [shaped(m) for m in came])
        self.moving = [shift(x, "x", 1), shift(y, "y", 1)]

    def total(self):
        self.kept, *self.away = ring_sum(self.at, self.kept, *self.moving)
        self.moving = []

    def along(self, k):
        self.moving.append(shift(self.away[k - 1], "z", k))

    def third(self):
        self.total()
        for k in range(1, self.deep):
            self.along(k)

    def fourth(self):
        total = self.kept.astype(f32)
        for away in self.moving:
            total = total + away.astype(f32)
        self.kept = total.astype(bf16)
        self.moving = [shift(self.kept, "y", 1)]

    def last(self):
        c, y = lax.axis_index("c"), lax.axis_index("y")
        mine = jnp.where(c == y, self.kept, self.moving[0])
        received = shift(jnp.where(c == y, self.moving[0], self.kept), "c", 1)
        left = jnp.where(c == 0, mine, received).astype(f32)
        right = jnp.where(c == 0, received, mine).astype(f32)
        return left, right, mine

    def whole(self):
        return jnp.concatenate(self.last()[:2], axis=1)


def settle(values, scatters):
    values, moving = fence(values, [s.moving for s in scatters])
    for s, m in zip(scatters, moving):
        s.moving = m
    return values


def per_device(
    tokens,
    prenorm_gain,
    query_weight,
    key_weight,
    value_weight,
    project_weight,
    midnorm_gain,
    gate_weight,
    up_weight,
    down_weight,
    out_grad,
    *,
    by_hand,
):
    z, x, c, y = (lax.axis_index(a) for a in ALL)
    deep = lax.axis_size("z")
    seqs = lax.axis_size("y")
    batch, length, width = tokens.shape
    shard = query_weight.shape[0]
    owners = width // shard
    hidden = gate_weight.shape[1]
    wide = HEADS * HD
    tokens = tokens[0]
    do = out_grad[0]

    qkv_shard = jnp.concatenate([query_weight, key_weight, value_weight], axis=1)
    gains_shard = jnp.stack([prenorm_gain, midnorm_gain])

    positions = y * length + jnp.arange(length, dtype=jnp.int32)
    frequency = 10000.0 ** (-jnp.arange(HD // 2, dtype=f32) / (HD // 2))
    angles = positions[:, None].astype(f32) * frequency
    cosine, sine = jnp.cos(angles), jnp.sin(angles)
    cos2 = jnp.concatenate([cosine, cosine], axis=1)
    sin2 = jnp.concatenate([-sine, sine], axis=1)
    start = (y * length).astype(jnp.int32)[None]

    reach = min(seqs - 1, -(-WINDOW // length))

    def earlier_kv(own_kv):
        return [lax.ppermute(own_kv, "y", [(i, i + k) for i in range(seqs - k)]) for k in range(reach, 0, -1)]

    def window_kv(earlier, own_kv):
        have = reach * length
        if have < WINDOW:
            earlier = [jnp.zeros((WINDOW - have, 2 * HD), bf16)] + earlier
        return jnp.concatenate(earlier + [own_kv], axis=0)[-(WINDOW + length) :]

    if by_hand:
        place = jnp.stack([z, x, c, y]).astype(jnp.int32)
        extra = jnp.pad(gains_shard, ((0, 14), (0, qkv_shard.shape[1] - shard)))
        own_half = lambda w: lax.dynamic_slice_in_dim(w, y * (w.shape[0] // 2), w.shape[0] // 2, 0)
        down_full = lax.all_gather(down_weight, OWN, axis=0, tiled=True)
        gate_z = along_z(own_half(gate_weight))
        gate_z, qkv_own = fence(gate_z, jnp.concatenate([qkv_shard, extra], axis=0))

        gate_o = jnp.stack(gate_z)
        gate_x, gate_y = shift(gate_o, "x", 1), shift(gate_o, "y", 1)
        qkv_z = along_z(qkv_own)
        qkv_z, gate_x, gate_y, up_own = fence(qkv_z, gate_x, gate_y, own_half(up_weight))

        gate_xy = shift(gate_x, "y", 1)
        gate_near = plus_core([gate_o, gate_x])
        qkv_o = jnp.stack(qkv_z)
        qkv_x = shift(qkv_o, "x", 1)
        up_z = along_z(up_own)
        up_z, qkv_x, gate_xy, gate_near, project_own = fence(up_z, qkv_x, gate_xy, gate_near, project_weight)

        up_o = jnp.stack(up_z)
        up_x, up_y = shift(up_o, "x", 1), shift(up_o, "y", 1)
        project_z = along_z(project_own)
        pieces = plus_core([qkv_o, qkv_x])
        qkv_full = assemble(place, pieces, width)
        gain_rows = jnp.concatenate([p[:, shard : shard + 2, :shard] for p in pieces]).reshape(owners, 2 * shard)
        owner = jnp.arange(owners, dtype=jnp.int32)
        slot = (((owner // 2) % 2) ^ x) * deep + ((owner % 2) ^ c) * (2 * deep) + (z - owner // 4 + deep) % deep
        pick = (slot[:, None] == owner[None, :]).astype(bf16)
        gains = jnp.dot(pick, gain_rows, preferred_element_type=f32).reshape(owners, 2, shard)
        gains = gains.transpose(1, 0, 2).reshape(2, width)
        gain_one, gain_two = gains[0:1], gains[1:2]
        hidden_one, queries, own_kv = qkv_forward(tokens, gain_one, qkv_full, cos2, sin2)
        own_kv, up_x, up_y, project_z, gate_y, gate_xy = fence(own_kv, up_x, up_y, project_z, gate_y, gate_xy)

        earlier = earlier_kv(own_kv)
        project_o = jnp.stack(project_z)
        project_x = shift(project_o, "x", 1)
        up_xy = shift(up_y, "x", 1)
        gate_near, gate_far = plus_core([gate_o, gate_x]), plus_core([gate_y, gate_xy])
        gate_full = assemble(place, gate_near + gate_far, width)
        earlier, gate_full, up_o, up_x, up_y = fence(earlier, gate_full, up_o, up_x, up_y)

        all_kv = window_kv(earlier, own_kv)
        attended, log_totals = attention_fwd(start, queries, all_kv)
        up_near = plus_core([up_o, up_x])
        attended, project_x, up_xy, up_near = fence(attended, project_x, up_xy, up_near)

        project_full = assemble(place, plus_core([project_o, project_x]), wide)
        up_far = plus_core([up_y, up_xy])
        middle, hidden_two = middle_forward(tokens, attended, project_full, gain_two)
        up_full = assemble(place, up_near + up_far, width)
    else:
        gather = lambda w: lax.all_gather(w, OWN, axis=0, tiled=True)
        qkv_full, project_full, down_full, gate_full, up_full = (
            gather(w) for w in (qkv_shard, project_weight, down_weight, gate_weight, up_weight)
        )
        gains = lax.all_gather(gains_shard, OWN, axis=1, tiled=True).astype(f32)
        gain_one, gain_two = gains[0:1], gains[1:2]
        hidden_one, queries, own_kv = qkv_forward(tokens, gain_one, qkv_full, cos2, sin2)
        all_kv = window_kv(earlier_kv(own_kv), own_kv)
        attended, log_totals = attention_fwd(start, queries, all_kv)
        middle, hidden_two = middle_forward(tokens, attended, project_full, gain_two)

    act, gate_up_low, block_output, hidden_two_grad = feed_forward(
        hidden_two, do, gate_full, up_full, down_full, middle
    )

    def key_value_sum(key_all, value_all):
        kv_all = jnp.concatenate([key_all, value_all], axis=1)
        parts = []
        for k in range(1, reach + 1):
            low = WINDOW - k * length
            part = kv_all[max(low, 0) : low + length].astype(bf16)
            if low < 0:
                part = jnp.pad(part, ((-low, 0), (0, 0)))
            parts.append(lax.ppermute(part, "y", [(i + k, i) for i in range(seqs - k)]))
        return kv_all[WINDOW:], parts

    def key_value_grad(own, parts):
        total = own
        for part in parts:
            total = total + part.astype(f32)
        key_sum = total[:, :HD]
        key_grad = key_sum * cos2 - jnp.roll(key_sum, HD // 2, axis=1) * sin2
        return jnp.concatenate([key_grad, total[:, HD:]], axis=1).astype(bf16)

    attention_back = lambda half, grad: attention_bwd(
        start, half, queries, all_kv, attended, grad, log_totals, cos2, sin2
    )
    zero, one = jnp.zeros((1,), jnp.int32), jnp.ones((1,), jnp.int32)
    if by_hand:
        half = c.astype(jnp.int32)[None]

        half32, x32, y32, z32 = (v.astype(jnp.int32) for v in (c, x, y, z))
        own, other = jnp.stack([half32, x32, y32, z32]), jnp.stack([1 - half32, x32, y32, z32])
        every = jnp.stack([half32 * 0, x32, y32, z32])
        gate_up_away = shift(weight_grad(other, hidden_two, gate_up_low), "c", 1)
        middle_grad, branch_low, attended_grad, midnorm_part = middle_back(
            hidden_two_grad, middle, do, gain_two, project_full
        )
        gate_up_away, branch_low, act = fence(gate_up_away, branch_low, act)

        gate_up_arrays = weight_grad(own, hidden_two, gate_up_low, gate_up_away, deep)
        gate_up_arrays, branch_low, act = fence(gate_up_arrays, branch_low, act)

        gate_up_s = Scatter(own, gate_up_arrays)
        gate_up_s.send(0)
        project_away = weight_grad(other, attended, branch_low)
        away_q, away_k, away_v = attention_back(1 - half, attended_grad)
        away_q, project_away, attended_grad, act = settle((away_q, project_away, attended_grad, act), [gate_up_s])

        gate_up_s.send(1)
        down_part = weight_grad(every, act, do, parts=1)
        query_away = weight_grad(every, hidden_one, away_q, parts=1)
        down_part, query_away, attended_grad = settle((down_part, query_away, attended_grad), [gate_up_s])

        down_share = lax.psum_scatter(down_part, OWN, scatter_dimension=0, tiled=True)
        gate_up_s.second()
        project_away, query_away = shift(project_away, "c", 1), shift(query_away, "c", 1)
        keep_q, keep_k, keep_v = attention_back(half, attended_grad)
        keep_q, keep_k, keep_v, project_away, query_away = settle(
            (keep_q, keep_k, keep_v, project_away, query_away), [gate_up_s]
        )

        kv_own, kv_parts = key_value_sum(away_k + keep_k, away_v + keep_v)
        gate_up_s.total()
        gate_up_s.along(1), gate_up_s.along(2)
        project_sum = weight_grad(own, attended, branch_low, project_away)
        query_sum = weight_grad(every, hidden_one, keep_q, query_away, parts=1)
        query_sum, project_sum, kv_parts, gate_up_s.kept, gate_up_s.away = fence(
            query_sum, project_sum, kv_parts, gate_up_s.kept, gate_up_s.away
        )

        gate_up_s.along(3)

        kv_grad = key_value_grad(kv_own, kv_parts)
        kv_away = shift(weight_grad(other, hidden_one, kv_grad), "c", 1)
        input_grad, prenorm_part = input_back(
            half, keep_q, away_q, kv_grad, qkv_full, tokens, gain_one, middle_grad
        )
        gain_part = jnp.pad(jnp.concatenate([prenorm_part, midnorm_part]).T, ((0, 0), (0, HD - 2))).astype(bf16)
        gain_sum = add_low(gain_part, shift(gain_part, "c", 1))
        kv_sum = weight_grad(own, hidden_one, kv_grad, kv_away)
        rest = jnp.concatenate([query_sum, project_sum, kv_sum, gain_sum], axis=1)
        cols = rest.shape[1]
        rest = rest.reshape(deep, 2, 2, -1, cols)
        of_x = lambda n, index: lax.dynamic_index_in_dim(rest[n], index, 0, False).reshape(1, -1, cols)
        of_y = lambda n, index: lax.dynamic_index_in_dim(rest[n], index, 1, False)
        low, high = range(deep // 2), range(deep // 2, deep)
        stays = [of_x(n, x) for n in low] + [of_y(n, y) for n in high]
        goes = jnp.concatenate([of_x(n, 1 - x) for n in low]), jnp.concatenate([of_y(n, 1 - y) for n in high])
        stays, goes = fence(stays, goes)

        came_x, came_y = fence(shift(goes[0], "x", 1), shift(goes[1], "y", 1))
        rest_s = Scatter(own, stays + stays)
        came_y = came_y.reshape(deep // 2, 2, -1, cols)
        for n in low:
            rest_s.moving += [came_x[n], came_y[n]]

        rest_s.second()
        (down_share,) = settle((down_share,), [rest_s, gate_up_s])

        rest_s.third()
        gate_up_s.fourth()
        down_other = shift(down_share, "y", 1)
        (down_other,) = settle((down_other,), [rest_s, gate_up_s])

        rest_s.fourth()
        left, right, _ = gate_up_s.last()
        wide_half = hidden // 2
        gate_gradient = jnp.concatenate([left[:, :wide_half], right[:, :wide_half]], axis=1)
        up_gradient = jnp.concatenate([left[:, wide_half:], right[:, wide_half:]], axis=1)
        down_gradient = down_share.astype(f32) + down_other.astype(f32)
        left, right, mine = rest_s.last()
        cut = wide // 2
        query_gradient = jnp.concatenate([left[:, :cut], right[:, :cut]], axis=1)
        project_gradient = jnp.concatenate([left[:, cut : 2 * cut], right[:, cut : 2 * cut]], axis=1)
        key_gradient, value_gradient = left[:, 2 * cut : 2 * cut + HD], right[:, 2 * cut : 2 * cut + HD]
        gain_mine = mine[:, 2 * cut + HD : 2 * cut + HD + 2].astype(f32).T
    else:

        def summed(a, b):
            value = jnp.concatenate([weight_grad(zero, a, b), weight_grad(one, a, b)], axis=1)
            return lax.psum(lax.psum_scatter(value, OWN, scatter_dimension=0, tiled=True), "y").astype(f32)

        gate_gradient, up_gradient = summed(hidden_two, gate_up_low[0]), summed(hidden_two, gate_up_low[1])
        middle_grad, branch_low, attended_grad, midnorm_part = middle_back(
            hidden_two_grad, middle, do, gain_two, project_full
        )
        down_gradient, project_gradient = summed(act, do), summed(attended, branch_low)
        left_q, left_k, left_v = attention_back(zero, attended_grad)
        right_q, right_k, right_v = attention_back(one, attended_grad)
        kv_grad = key_value_grad(*key_value_sum(left_k + right_k, left_v + right_v))
        input_grad, prenorm_part = input_back(
            zero, left_q, right_q, kv_grad, qkv_full, tokens, gain_one, middle_grad
        )
        query_gradient = summed(hidden_one, jnp.concatenate([left_q, right_q], axis=1))
        kv_gradient = summed(hidden_one, kv_grad)
        key_gradient, value_gradient = kv_gradient[:, :HD], kv_gradient[:, HD:]
        gain_sums = lax.psum(jnp.concatenate([prenorm_part, midnorm_part]), ALL)
        index = (z * 2 + x) * 2 + c
        gain_mine = lax.dynamic_slice_in_dim(gain_sums, index * shard, shard, 1)
    return (
        block_output[None],
        input_grad[None],
        gain_mine[0],
        query_gradient,
        key_gradient,
        value_gradient,
        project_gradient,
        gain_mine[1],
        gate_gradient,
        up_gradient,
        down_gradient,
    )


def solution(mesh):
    owners, seqs = mesh.shape["fsdp"], mesh.shape["seq"]
    deep = owners // 4
    split = Mesh(mesh.devices.reshape(deep, 2, 2, seqs), ALL)
    rows = P(OWN, "y", None)
    weight = P(OWN, None)
    in_specs = (
        rows,
        P(OWN),
        weight,
        weight,
        weight,
        weight,
        P(OWN),
        weight,
        weight,
        weight,
        rows,
    )
    out_specs = (
        rows,
        rows,
        P(OWN),
        weight,
        weight,
        weight,
        weight,
        P(OWN),
        weight,
        weight,
        weight,
    )
    by_hand = seqs == 2 and deep == 4
    return jax.shard_map(
        functools.partial(per_device, by_hand=by_hand),
        mesh=split,
        in_specs=in_specs,
        out_specs=out_specs,
        check_vma=False,
    )
```

```python
import functools

import jax
import jax.numpy as jnp
from jax import lax
from jax.experimental import pallas as pl
from jax.experimental.pallas import tpu as pltpu
from jax.sharding import Mesh
from jax.sharding import PartitionSpec as P

HEADS = 8
HD = 128
WINDOW = 1024

norm_epsilon = 1e-06
masked_value = -1e30
LOG2E = 1.4426950408889634
bf16 = jnp.bfloat16
f32 = jnp.float32
OWN = ("z", "x", "c")
ALL = ("z", "x", "c", "y")


def nn(a, b):
    return lax.dot_general(a, b, (((1,), (0,)), ((), ())), preferred_element_type=f32)


def nt(a, b):
    return lax.dot_general(a, b, (((1,), (1,)), ((), ())), preferred_element_type=f32)


def tn(a, b):
    return lax.dot_general(a, b, (((0,), (0,)), ((), ())), preferred_element_type=f32)


def params(mib):
    return pltpu.CompilerParams(vmem_limit_bytes=mib << 20)


def cost(flops, moved, exps=0):
    return pl.CostEstimate(flops=int(flops), bytes_accessed=int(moved), transcendentals=int(exps))


def window_scores(scores, block, first_valid, limited):
    rows, keys = scores.shape
    r = lax.rem(lax.broadcasted_iota(jnp.int32, (rows, block), 0), block)
    j = lax.broadcasted_iota(jnp.int32, (rows, block), 1)
    front = jnp.where(j > r, scores[:, :block], masked_value)
    back = jnp.where(j <= r, scores[:, keys - block :], masked_value)
    scores = jnp.concatenate([front, scores[:, block : keys - block], back], axis=1)
    if limited:
        place = lax.broadcasted_iota(jnp.int32, scores.shape, 1)
        scores = jnp.where(place >= first_valid, scores, masked_value)
    return scores


def stacked(ref, heads):
    return jnp.concatenate([ref[:, a * HD : (a + 1) * HD] for a in heads], axis=0)


def attention_fwd_kernel(start_ref, q_ref, kv_ref, o_ref, lse_ref, *, block, group):
    i = pl.program_id(0)
    keys = WINDOW + block
    base = pl.multiple_of(i * block, block)
    k = kv_ref[pl.ds(base, keys), :HD]
    v = kv_ref[pl.ds(base, keys), HD:]
    ones = jnp.ones_like(v)
    value_one = jnp.concatenate([v, ones], axis=1)
    first_valid = WINDOW - start_ref[0] - i * block
    scale = HD**-0.5 * LOG2E
    lane = lax.broadcasted_iota(jnp.int32, (block, HD), 1)

    def run(limited):
        stats = [jnp.zeros((block, HD), f32)] * 2
        for g in range(HEADS // group):
            heads = range(g * group, (g + 1) * group)
            scores = window_scores(nt(stacked(q_ref, heads), k), block, first_valid, limited)
            top = jnp.max(scores, axis=1, keepdims=True) * scale
            weight = jnp.exp2(scores * scale - top).astype(bf16)
            both = nn(weight, value_one)
            total = both[:, HD:]
            out = both[:, :HD] / total
            lse = top + jnp.log2(total)
            for h, a in enumerate(heads):
                o_ref[:, a * HD : (a + 1) * HD] = out[h * block : (h + 1) * block].astype(bf16)
                at, spot = divmod(a, HEADS // 2)
                stats[at] = jnp.where(lane == spot, lse[h * block : (h + 1) * block], stats[at])
        lse_ref[...] = jnp.concatenate(stats, axis=1)

    @pl.when(first_valid <= 0)
    def _():
        run(False)

    @pl.when(first_valid > 0)
    def _():
        run(True)


def attention_fwd(start, q, kv, block=256, group=2):
    length, total = q.shape[0], kv.shape[0]
    block = min(block, length)
    rows = lambda w: pl.BlockSpec((block, w), lambda i: (i, 0))
    return pl.pallas_call(
        functools.partial(attention_fwd_kernel, block=block, group=group),
        grid=(length // block,),
        in_specs=[
            pl.BlockSpec(memory_space=pltpu.SMEM),
            rows(HEADS * HD),
            pl.BlockSpec((total, 2 * HD), lambda i: (0, 0)),
        ],
        out_specs=[rows(HEADS * HD), rows(2 * HD)],
        out_shape=[
            jax.ShapeDtypeStruct((length, HEADS * HD), bf16),
            jax.ShapeDtypeStruct((length, 2 * HD), f32),
        ],
        compiler_params=params(60),
        cost_estimate=cost(
            20 * length * HEADS * HD * WINDOW, 6 << 20, length * HEADS * WINDOW
        ),
        name="attention_fwd",
    )(start, q, kv)


def attention_bwd_kernel(
    at_ref, q_ref, kv_ref, o_ref, do_ref, lse_ref, cos_ref, sin_ref, dq_ref, dk_ref, dv_ref, *, block, group
):
    i = pl.program_id(0)
    keys = WINDOW + block
    base = pl.multiple_of(i * block, block)
    k = kv_ref[pl.ds(base, keys), :HD]
    v = kv_ref[pl.ds(base, keys), HD:]
    first_valid = WINDOW - at_ref[0] - i * block
    scale = HD**-0.5 * LOG2E

    @pl.when(i == 0)
    def _():
        dk_ref[...] = jnp.zeros_like(dk_ref)
        dv_ref[...] = jnp.zeros_like(dv_ref)

    def run(limited):
        for g in range(HEADS // 2 // group):
            heads = range(g * group, (g + 1) * group)
            q = stacked(q_ref, heads)
            do = stacked(do_ref, heads)
            o = stacked(o_ref, heads)
            lse = jnp.concatenate([lse_ref[:, a : a + 1] for a in heads], axis=0)
            inner = jnp.sum(do.astype(f32) * o.astype(f32), axis=1, keepdims=True)
            scores = window_scores(nt(q, k), block, first_valid, limited)
            prob = jnp.exp2(scores * scale - lse)
            prob_grad = nt(do, v)
            score_grad = (prob * (prob_grad - inner)).astype(bf16)
            dv_ref[pl.ds(base, keys), :] += tn(prob.astype(bf16), do)
            dk_ref[pl.ds(base, keys), :] += tn(score_grad, q)
            dq = nn(score_grad, k) * (HD**-0.5)
            for h, a in enumerate(heads):
                t = dq[h * block : (h + 1) * block]
                t = t * cos_ref[...] - pltpu.roll(t, HD // 2, 1) * sin_ref[...]
                dq_ref[:, a * HD : (a + 1) * HD] = t.astype(bf16)

    @pl.when(first_valid <= 0)
    def _():
        run(False)

    @pl.when(first_valid > 0)
    def _():
        run(True)

    @pl.when(i == pl.num_programs(0) - 1)
    def _():
        dk_ref[...] *= HD**-0.5


def attention_bwd(start, half, q, kv, o, do, lse, cos2, sin2, block=128, group=2):
    length, total = q.shape[0], kv.shape[0]
    rows = pl.BlockSpec((block, HD), lambda i, s: (i, 0))
    wide = HEADS * HD // 2
    heads = pl.BlockSpec((block, wide), lambda i, s: (i, s[1]))
    whole = lambda w: pl.BlockSpec((total, w), lambda i, s: (0, 0))
    return pl.pallas_call(
        functools.partial(attention_bwd_kernel, block=block, group=group),
        grid_spec=pltpu.PrefetchScalarGridSpec(
            num_scalar_prefetch=1,
            grid=(length // block,),
            in_specs=[
                heads,
                whole(2 * HD),
                heads,
                heads,
                pl.BlockSpec((block, HD), lambda i, s: (i, s[1])),
                rows,
                rows,
            ],
            out_specs=[pl.BlockSpec((block, wide), lambda i, s: (i, 0)), whole(HD), whole(HD)],
        ),
        out_shape=[
            jax.ShapeDtypeStruct((length, wide), bf16),
            jax.ShapeDtypeStruct((total, HD), f32),
            jax.ShapeDtypeStruct((total, HD), f32),
        ],
        compiler_params=params(60),
        cost_estimate=cost(22 * length * wide * WINDOW, 8 << 20, length * HEADS * WINDOW // 2),
        name="attention_bwd",
    )(jnp.concatenate([start, half]), q, kv, o, do, lse, cos2, sin2)


def qkv_kernel(x_ref, gain_ref, w_ref, cos_ref, sin_ref, h_ref, q_ref, kv_ref):
    x = x_ref[...].astype(f32)
    scale = lax.rsqrt(jnp.mean(x * x, axis=-1, keepdims=True) + norm_epsilon)
    h = (x * scale * gain_ref[...]).astype(bf16)
    h_ref[...] = h
    cos2, sin2 = cos_ref[...], sin_ref[...]
    for a in range(0, HEADS, 2):
        lin = nn(h, w_ref[:, a * HD : (a + 2) * HD])
        for b in range(2):
            t = lin[:, b * HD : (b + 1) * HD]
            q_ref[:, (a + b) * HD : (a + b + 1) * HD] = (
                t * cos2 + pltpu.roll(t, HD // 2, 1) * sin2
            ).astype(bf16)
    lin = nn(h, w_ref[:, HEADS * HD :])
    t = lin[:, :HD]
    kv_ref[:, :HD] = (t * cos2 + pltpu.roll(t, HD // 2, 1) * sin2).astype(bf16)
    kv_ref[:, HD:] = lin[:, HD:].astype(bf16)


def qkv_forward(x, gain, w, cos2, sin2, block=256):
    length, width = x.shape
    rows = lambda n: pl.BlockSpec((block, n), lambda i: (i, 0))
    whole = lambda a: pl.BlockSpec(a.shape, lambda i: (0, 0))
    return pl.pallas_call(
        qkv_kernel,
        grid=(length // block,),
        in_specs=[rows(width), whole(gain), whole(w), rows(HD), rows(HD)],
        out_specs=[rows(width), rows(HEADS * HD), rows(2 * HD)],
        out_shape=[
            jax.ShapeDtypeStruct((length, width), bf16),
            jax.ShapeDtypeStruct((length, HEADS * HD), bf16),
            jax.ShapeDtypeStruct((length, 2 * HD), bf16),
        ],
        compiler_params=params(60),
        cost_estimate=cost(4 * length * w.size, 12 << 20),
        name="norm_qkv",
    )(x, gain, w, cos2, sin2)


def middle_kernel(x_ref, a_ref, w_ref, gain_ref, mid_ref, h_ref):
    mid = x_ref[...].astype(f32) + nn(a_ref[...], w_ref[...])
    mid_ref[...] = mid
    scale = lax.rsqrt(jnp.mean(mid * mid, axis=-1, keepdims=True) + norm_epsilon)
    h_ref[...] = (mid * scale * gain_ref[...]).astype(bf16)


def middle_forward(x, attended, w, gain, block=256):
    length, width = x.shape
    rows = pl.BlockSpec((block, width), lambda i: (i, 0))
    whole = lambda a: pl.BlockSpec(a.shape, lambda i: (0, 0))
    return pl.pallas_call(
        middle_kernel,
        grid=(length // block,),
        in_specs=[rows, pl.BlockSpec((block, attended.shape[1]), lambda i: (i, 0)), whole(w), whole(gain)],
        out_specs=[rows, rows],
        out_shape=[
            jax.ShapeDtypeStruct((length, width), f32),
            jax.ShapeDtypeStruct((length, width), bf16),
        ],
        compiler_params=params(60),
        cost_estimate=cost(4 * length * w.size, 12 << 20),
        name="project_norm",
    )(x, attended, w, gain)


def norm_back(dn, normed, scale):
    return scale * (dn - normed * jnp.mean(dn * normed, axis=-1, keepdims=True))


def middle_back_kernel(hg_ref, mid_ref, do_ref, gain_ref, w_ref, mg_ref, low_ref, ag_ref, gain_grad_ref):
    i = pl.program_id(0)
    mid = mid_ref[...]
    hg = hg_ref[...]
    scale = lax.rsqrt(jnp.mean(mid * mid, axis=-1, keepdims=True) + norm_epsilon)
    normed = mid * scale
    mg = do_ref[...].astype(f32) + norm_back(hg * gain_ref[...], normed, scale)
    mg_ref[...] = mg
    low = mg.astype(bf16)
    low_ref[...] = low
    ag_ref[...] = nt(low, w_ref[...]).astype(bf16)

    @pl.when(i == 0)
    def _():
        gain_grad_ref[...] = jnp.zeros_like(gain_grad_ref)

    gain_grad_ref[...] += jnp.sum(hg * normed, axis=0, keepdims=True)


def middle_back(hg, mid, do, gain, w, block=256):
    length, width = mid.shape
    rows = lambda n: pl.BlockSpec((block, n), lambda i: (i, 0))
    whole = lambda s: pl.BlockSpec(s, lambda i: (0, 0))
    return pl.pallas_call(
        middle_back_kernel,
        grid=(length // block,),
        in_specs=[rows(width), rows(width), rows(width), whole(gain.shape), whole(w.shape)],
        out_specs=[rows(width), rows(width), rows(w.shape[0]), whole((1, width))],
        out_shape=[
            jax.ShapeDtypeStruct((length, width), f32),
            jax.ShapeDtypeStruct((length, width), bf16),
            jax.ShapeDtypeStruct((length, w.shape[0]), bf16),
            jax.ShapeDtypeStruct((1, width), f32),
        ],
        compiler_params=params(60),
        cost_estimate=cost(4 * length * w.size, 22 << 20),
        name="norm_two_back",
    )(hg, mid, do, gain, w)


def input_back_kernel(half_ref, keep_ref, away_ref, dkv_ref, w_ref, x_ref, gain_ref, mg_ref, out_ref, gain_grad_ref):
    i = pl.program_id(0)
    wide = keep_ref.shape[1]
    own = pl.multiple_of(half_ref[0] * wide, wide)
    hg = nt(keep_ref[...], w_ref[:, pl.ds(own, wide)]) + nt(away_ref[...], w_ref[:, pl.ds(wide - own, wide)])
    hg += nt(dkv_ref[...], w_ref[:, 2 * wide :])
    x = x_ref[...].astype(f32)
    scale = lax.rsqrt(jnp.mean(x * x, axis=-1, keepdims=True) + norm_epsilon)
    normed = x * scale
    out_ref[...] = (mg_ref[...] + norm_back(hg * gain_ref[...], normed, scale)).astype(bf16)

    @pl.when(i == 0)
    def _():
        gain_grad_ref[...] = jnp.zeros_like(gain_grad_ref)

    gain_grad_ref[...] += jnp.sum(hg * normed, axis=0, keepdims=True)


def input_back(half, keep, away, dkv, w, x, gain, mg, block=256):
    length, width = x.shape
    rows = lambda n: pl.BlockSpec((block, n), lambda i, s: (i, 0))
    whole = lambda shape: pl.BlockSpec(shape, lambda i, s: (0, 0))
    return pl.pallas_call(
        input_back_kernel,
        grid_spec=pltpu.PrefetchScalarGridSpec(
            num_scalar_prefetch=1,
            grid=(length // block,),
            in_specs=[
                rows(keep.shape[1]),
                rows(away.shape[1]),
                rows(dkv.shape[1]),
                whole(w.shape),
                rows(width),
                whole(gain.shape),
                rows(width),
            ],
            out_specs=[rows(width), whole((1, width))],
        ),
        out_shape=[
            jax.ShapeDtypeStruct((length, width), bf16),
            jax.ShapeDtypeStruct((1, width), f32),
        ],
        compiler_params=params(60),
        cost_estimate=cost(4 * length * w.size, 16 << 20),
        name="norm_one_back",
    )(half, keep, away, dkv, w, x, gain, mg)


def gelu_parts(x):
    t = 1.0 / (1.0 + (0.3275911 * 0.7071067811865476) * jnp.abs(x))
    e = jnp.exp2(x * x * (-0.5 * LOG2E))
    poly = 0.5 * 1.061405429 * t - 0.5 * 1.453152027
    poly = poly * t + 0.5 * 1.421413741
    poly = poly * t - 0.5 * 0.284496736
    poly = (poly * t + 0.5 * 0.254829592) * t
    tail = poly * e
    return jnp.where(x >= 0, 1.0 - tail, tail), x * e * 0.3989422804014327


def feed_forward_kernel(
    h_ref, do_ref, wg_ref, wu_ref, wd_ref, mid_ref, act_ref, both_ref, out_ref, hg_ref, acc
):
    j = pl.program_id(0)

    @pl.when(j == 0)
    def _():
        acc[...] = mid_ref[...]
        hg_ref[...] = jnp.zeros_like(hg_ref)

    h = h_ref[...]
    gate = nn(h, wg_ref[...])
    up = nn(h, wu_ref[...])
    act_grad = nt(do_ref[...], wd_ref[...])
    cdf, x_pdf = gelu_parts(gate)
    gelu = gate * cdf
    act = (gelu * up).astype(bf16)
    gate_grad = (act_grad * up * (cdf + x_pdf)).astype(bf16)
    up_grad = (act_grad * gelu).astype(bf16)
    act_ref[...] = act
    both_ref[0] = gate_grad
    both_ref[1] = up_grad
    acc[...] += nn(act, wd_ref[...])
    hg_ref[...] += nt(gate_grad, wg_ref[...]) + nt(up_grad, wu_ref[...])

    @pl.when(j == pl.num_programs(0) - 1)
    def _():
        out_ref[...] = acc[...].astype(bf16)


def feed_forward(h, do, wg, wu, wd, mid, chunk=512):
    length, width = h.shape
    hidden = wg.shape[1]
    whole = pl.BlockSpec((length, width), lambda j: (0, 0))
    col = lambda n: pl.BlockSpec((n, chunk), lambda j: (0, j))
    return pl.pallas_call(
        feed_forward_kernel,
        grid=(hidden // chunk,),
        in_specs=[whole, whole, col(width), col(width), pl.BlockSpec((chunk, width), lambda j: (j, 0)), whole],
        out_specs=[col(length), pl.BlockSpec((2, length, chunk), lambda j: (0, 0, j)), whole, whole],
        out_shape=[jax.ShapeDtypeStruct((length, hidden), bf16), jax.ShapeDtypeStruct((2, length, hidden), bf16)]
        + [jax.ShapeDtypeStruct((length, width), bf16), jax.ShapeDtypeStruct((length, width), f32)],
        scratch_shapes=[pltpu.VMEM((length, width), f32)],
        compiler_params=params(60),
        cost_estimate=cost(16 * length * width * hidden, 60 << 20, length * hidden),
        name="feed_forward",
    )(h, do, wg, wu, wd, mid)


def weight_grad_kernel(at_ref, a_ref, b_ref, *refs, received, split):
    value = tn(a_ref[...], b_ref[...])
    if received:
        value = value + refs[0][...].astype(f32)
    outs = refs[received:]
    value = value.astype(bf16)
    if not split:
        outs[0][...] = value
        return
    deep = len(outs) // 2
    kept, away = outs[:deep], outs[deep:]
    tiles = deep * kept[0].shape[0] * kept[0].shape[1] * 2 // value.shape[0]
    for n in range(deep):
        count, part = kept[n].shape[:2]
        first = 0 if tiles > 1 else 2 * n * count * part
        here = pl.program_id(0) == (n if tiles > 1 else 0)
        index = at_ref[1] if n < deep // 2 else at_ref[2]
        for mine in range(2):

            @pl.when(here & (index == mine))
            def _(n=n, mine=mine, first=first, count=count, part=part):
                for m in range(count):
                    for side, to in ((mine, kept[n]), (1 - mine, away[n])):
                        low = first + (2 * m + side) * part
                        to[m] = value[low : low + part]


def weight_grad(at, a, b, received=None, deep=0, parts=2):
    length, rows = a.shape
    many = b.shape[0] if b.ndim == 3 else 1
    cols = b.shape[-1] // parts
    wide = 768 if cols % 768 == 0 else min(512, cols)
    tall = rows if rows <= 1024 else rows // 4
    per = cols // wide
    whole = pl.BlockSpec((tall, wide), lambda i, j, s: (i, j))
    if b.ndim == 3:
        of_b = pl.BlockSpec((None, length, wide), lambda i, j, s: (j // per, 0, s[0] * per + j % per))
    else:
        of_b = pl.BlockSpec((length, wide), lambda i, j, s: (0, s[0] * per + j))
    ins = [pl.BlockSpec((length, tall), lambda i, j, s: (0, i)), of_b]
    args = [a, b]
    if received is not None:
        ins.append(whole)
        args.append(received)
    if not deep:
        outs, shapes = whole, jax.ShapeDtypeStruct((rows, many * cols), bf16)
    else:
        part = rows // (4 * deep)
        sizes = [(1, 2 * part) if n < deep // 2 else (2, part) for n in range(deep)] * 2
        outs = [pl.BlockSpec((*size, wide), lambda i, j, s: (0, 0, j)) for size in sizes]
        shapes = [jax.ShapeDtypeStruct((*size, many * cols), bf16) for size in sizes]
    return pl.pallas_call(
        functools.partial(weight_grad_kernel, received=received is not None, split=deep > 0),
        grid_spec=pltpu.PrefetchScalarGridSpec(
            num_scalar_prefetch=1, grid=(rows // tall, many * per), in_specs=ins, out_specs=outs
        ),
        out_shape=shapes,
        compiler_params=params(40),
        cost_estimate=cost(4 * length * rows * cols * many, 2 * (length * rows + length * cols + 2 * rows * cols)),
        name="weight_grad",
    )(at, *args)


def shift(value, axis, k):
    n = lax.axis_size(axis)
    return lax.ppermute(value, axis, [(i, (i + k) % n) for i in range(n)])


def piece_rows(place, n, deep, total):
    z, x, c, y = place[0], place[1], place[2], place[3]
    part = total // (n * deep)
    spots = []
    for i in range(n):
        xx = x if i % 2 == 0 else 1 - x
        cc = c if (i // 2) % 2 == 0 else 1 - c
        yy = 0 if n == 4 else (y if i < 4 else 1 - y)
        for k in range(deep):
            zz = lax.rem(z - k + deep, deep)
            row = (((zz * 2 + xx) * 2 + cc) * (n // 4) + yy) * part
            spots.append(pl.ds(pl.multiple_of(row, part), part))
    return spots


def assemble_kernel(place, *refs, deep, rows):
    n = len(refs) - 4
    ins, out, held, in_sems, out_sems = refs[:n], refs[n], refs[n + 1], refs[n + 2], refs[n + 3]
    moves = []
    for at, spot in enumerate(piece_rows(place, n, deep, rows)):
        i, k = divmod(at, deep)
        part = pl.ds(0, rows // (n * deep))
        moves.append(
            (
                pltpu.make_async_copy(ins[i].at[k, part], held.at[spot], in_sems.at[i, k]),
                pltpu.make_async_copy(held.at[spot], out.at[spot], out_sems.at[i, k]),
            )
        )
    for into, _ in moves:
        into.start()
    for into, back in moves:
        into.wait()
        back.start()
    for _, back in moves:
        back.wait()


def assemble(place, pieces, rows):
    n, deep, cols = len(pieces), pieces[0].shape[0], pieces[0].shape[2]
    return pl.pallas_call(
        functools.partial(assemble_kernel, deep=deep, rows=rows),
        out_shape=jax.ShapeDtypeStruct((rows, cols), bf16),
        in_specs=[pl.BlockSpec(memory_space=pltpu.SMEM)] + [pl.BlockSpec(memory_space=pltpu.HBM)] * n,
        out_specs=pl.BlockSpec(memory_space=pltpu.HBM),
        scratch_shapes=[
            pltpu.VMEM((rows, cols), bf16),
            pltpu.SemaphoreType.DMA((n, deep)),
            pltpu.SemaphoreType.DMA((n, deep)),
        ],
        compiler_params=params(60),
        cost_estimate=cost(0, rows * cols * 4),
        name="assemble",
    )(place, *pieces)


def fence(*values):
    return lax.optimization_barrier(values)


def along_z(piece):
    return [piece] + [shift(piece, "z", k) for k in range(1, lax.axis_size("z"))]


def plus_core(pieces):
    return pieces + [shift(p, "c", 1) for p in pieces]


def pair_sum_kernel(at_ref, *refs, deep):
    kept, came, (keep_ref, x_ref, y_ref) = refs[:deep], refs[deep : 2 * deep], refs[2 * deep :]
    half = deep // 2
    for n in range(deep):
        index = at_ref[2] if n < half else at_ref[1]
        for mine in range(2):

            @pl.when(index == mine)
            def _(n=n, mine=mine):
                total = lambda side: (kept[n][side].astype(f32) + came[n][side].astype(f32)).astype(bf16)
                keep_ref[n] = total(mine)
                if n < half:
                    y_ref[n] = total(1 - mine)
                else:
                    x_ref[n - half] = total(1 - mine)


def pair_sum(at, kept, came):
    deep = len(kept)
    _, part, cols = kept[0].shape
    whole = lambda shape: pl.BlockSpec(shape, lambda i, s: (0,) * len(shape))
    shapes = [(deep, part, cols), (deep // 2, part, cols), (deep // 2, part, cols)]
    return pl.pallas_call(
        functools.partial(pair_sum_kernel, deep=deep),
        grid_spec=pltpu.PrefetchScalarGridSpec(
            num_scalar_prefetch=1,
            grid=(1,),
            in_specs=[whole((2, part, cols))] * (2 * deep),
            out_specs=[whole(shape) for shape in shapes],
        ),
        out_shape=[jax.ShapeDtypeStruct(shape, bf16) for shape in shapes],
        compiler_params=params(24),
        cost_estimate=cost(4 * deep * part * cols, 24 * deep * part * cols),
        name="pair_sum",
    )(at, *kept, *came)


def ring_sum_kernel(at_ref, a_ref, x_ref, y_ref, *outs):
    deep = len(outs)
    half = deep // 2
    for here in range(deep):

        @pl.when(at_ref[3] == here)
        def _(here=here):
            for k in range(deep):
                n = (here + k) % deep
                came = y_ref[n] if n < half else x_ref[n - half]
                outs[k][...] = (a_ref[n].astype(f32) + came.astype(f32)).astype(bf16)


def ring_sum(at, kept, over_x, over_y):
    deep, part, cols = kept.shape
    whole = lambda shape: pl.BlockSpec(shape, lambda i, s: (0,) * len(shape))
    return pl.pallas_call(
        ring_sum_kernel,
        grid_spec=pltpu.PrefetchScalarGridSpec(
            num_scalar_prefetch=1,
            grid=(1,),
            in_specs=[whole(kept.shape), whole(over_x.shape), whole(over_y.shape)],
            out_specs=[whole((part, cols))] * deep,
        ),
        out_shape=[jax.ShapeDtypeStruct((part, cols), bf16)] * deep,
        compiler_params=params(16),
        cost_estimate=cost(2 * kept.size, 12 * kept.size),
        name="ring_sum",
    )(at, kept, over_x, over_y)


def add_low(a, b):
    return (a.astype(f32) + b.astype(f32)).astype(bf16)


class Scatter:
    def __init__(self, at, arrays):
        self.at = at
        self.deep = len(arrays) // 2
        self.kept, self.away = arrays[: self.deep], arrays[self.deep :]
        self.moving = []

    def send(self, n):
        self.moving += [shift(self.away[n], "x", 1), shift(self.away[self.deep // 2 + n], "y", 1)]

    def second(self):
        shaped = lambda v: v.reshape(2, -1, v.shape[-1])
        came = self.moving[::2] + self.moving[1::2]
        self.kept, x, y = pair_sum(self.at, [shaped(k) for k in self.kept], [shaped(m) for m in came])
        self.moving = [shift(x, "x", 1), shift(y, "y", 1)]

    def total(self):
        self.kept, *self.away = ring_sum(self.at, self.kept, *self.moving)
        self.moving = []

    def along(self, k):
        self.moving.append(shift(self.away[k - 1], "z", k))

    def third(self):
        self.total()
        for k in range(1, self.deep):
            self.along(k)

    def fourth(self):
        total = self.kept.astype(f32)
        for away in self.moving:
            total = total + away.astype(f32)
        self.kept = total.astype(bf16)
        self.moving = [shift(self.kept, "y", 1)]

    def last(self):
        c, y = lax.axis_index("c"), lax.axis_index("y")
        mine = jnp.where(c == y, self.kept, self.moving[0])
        received = shift(jnp.where(c == y, self.moving[0], self.kept), "c", 1)
        left = jnp.where(c == 0, mine, received).astype(f32)
        right = jnp.where(c == 0, received, mine).astype(f32)
        return left, right, mine

    def whole(self):
        return jnp.concatenate(self.last()[:2], axis=1)


def settle(values, scatters):
    values, moving = fence(values, [s.moving for s in scatters])
    for s, m in zip(scatters, moving):
        s.moving = m
    return values


def per_device(
    tokens,
    prenorm_gain,
    query_weight,
    key_weight,
    value_weight,
    project_weight,
    midnorm_gain,
    gate_weight,
    up_weight,
    down_weight,
    out_grad,
    *,
    by_hand,
):
    z, x, c, y = (lax.axis_index(a) for a in ALL)
    deep = lax.axis_size("z")
    seqs = lax.axis_size("y")
    batch, length, width = tokens.shape
    shard = query_weight.shape[0]
    owners = width // shard
    hidden = gate_weight.shape[1]
    wide = HEADS * HD
    tokens = tokens[0]
    do = out_grad[0]

    qkv_shard = jnp.concatenate([query_weight, key_weight, value_weight], axis=1)
    gains_shard = jnp.stack([prenorm_gain, midnorm_gain])

    positions = y * length + jnp.arange(length, dtype=jnp.int32)
    frequency = 10000.0 ** (-jnp.arange(HD // 2, dtype=f32) / (HD // 2))
    angles = positions[:, None].astype(f32) * frequency
    cosine, sine = jnp.cos(angles), jnp.sin(angles)
    cos2 = jnp.concatenate([cosine, cosine], axis=1)
    sin2 = jnp.concatenate([-sine, sine], axis=1)
    start = (y * length).astype(jnp.int32)[None]

    reach = min(seqs - 1, -(-WINDOW // length))

    def earlier_kv(own_kv):
        return [lax.ppermute(own_kv, "y", [(i, i + k) for i in range(seqs - k)]) for k in range(reach, 0, -1)]

    def window_kv(earlier, own_kv):
        have = reach * length
        if have < WINDOW:
            earlier = [jnp.zeros((WINDOW - have, 2 * HD), bf16)] + earlier
        return jnp.concatenate(earlier + [own_kv], axis=0)[-(WINDOW + length) :]

    if by_hand:
        place = jnp.stack([z, x, c, y]).astype(jnp.int32)
        extra = jnp.pad(gains_shard, ((0, 14), (0, qkv_shard.shape[1] - shard)))
        own_half = lambda w: lax.dynamic_slice_in_dim(w, y * (w.shape[0] // 2), w.shape[0] // 2, 0)
        gate_z = along_z(own_half(gate_weight))
        gate_z, qkv_own = fence(gate_z, jnp.concatenate([qkv_shard, extra], axis=0))

        gate_o = jnp.stack(gate_z)
        gate_x, gate_y = shift(gate_o, "x", 1), shift(gate_o, "y", 1)
        qkv_z = along_z(qkv_own)
        qkv_z, gate_x, gate_y, up_own = fence(qkv_z, gate_x, gate_y, own_half(up_weight))

        gate_xy = shift(gate_x, "y", 1)
        gate_near = plus_core([gate_o, gate_x])
        qkv_o = jnp.stack(qkv_z)
        qkv_x = shift(qkv_o, "x", 1)
        up_z = along_z(up_own)
        up_z, qkv_x, gate_xy, gate_near, project_own, down_own = fence(
            up_z, qkv_x, gate_xy, gate_near, project_weight, down_weight
        )
        down_full = lax.all_gather(down_own, OWN, axis=0, tiled=True)

        up_o = jnp.stack(up_z)
        up_x, up_y = shift(up_o, "x", 1), shift(up_o, "y", 1)
        project_z = along_z(project_own)
        pieces = plus_core([qkv_o, qkv_x])
        qkv_full = assemble(place, pieces, width)
        gain_rows = jnp.concatenate([p[:, shard : shard + 2, :shard] for p in pieces]).reshape(owners, 2 * shard)
        owner = jnp.arange(owners, dtype=jnp.int32)
        slot = (((owner // 2) % 2) ^ x) * deep + ((owner % 2) ^ c) * (2 * deep) + (z - owner // 4 + deep) % deep
        pick = (slot[:, None] == owner[None, :]).astype(bf16)
        gains = jnp.dot(pick, gain_rows, preferred_element_type=f32).reshape(owners, 2, shard)
        gains = gains.transpose(1, 0, 2).reshape(2, width)
        gain_one, gain_two = gains[0:1], gains[1:2]
        hidden_one, queries, own_kv = qkv_forward(tokens, gain_one, qkv_full, cos2, sin2)
        own_kv, up_x, up_y, project_z, gate_y, gate_xy = fence(own_kv, up_x, up_y, project_z, gate_y, gate_xy)

        earlier = earlier_kv(own_kv)
        project_o = jnp.stack(project_z)
        project_x = shift(project_o, "x", 1)
        up_xy = shift(up_x, "y", 1)
        gate_near, gate_far = plus_core([gate_o, gate_x]), plus_core([gate_y, gate_xy])
        gate_full = assemble(place, gate_near + gate_far, width)
        earlier, gate_full, up_o, up_x, up_y = fence(earlier, gate_full, up_o, up_x, up_y)

        all_kv = window_kv(earlier, own_kv)
        attended, log_totals = attention_fwd(start, queries, all_kv)
        up_near = plus_core([up_o, up_x])
        attended, project_x, up_xy, up_near = fence(attended, project_x, up_xy, up_near)

        project_full = assemble(place, plus_core([project_o, project_x]), wide)
        up_far = plus_core([up_y, up_xy])
        middle, hidden_two = middle_forward(tokens, attended, project_full, gain_two)
        up_full = assemble(place, up_near + up_far, width)
    else:
        gather = lambda w: lax.all_gather(w, OWN, axis=0, tiled=True)
        qkv_full, project_full, down_full, gate_full, up_full = (
            gather(w) for w in (qkv_shard, project_weight, down_weight, gate_weight, up_weight)
        )
        gains = lax.all_gather(gains_shard, OWN, axis=1, tiled=True).astype(f32)
        gain_one, gain_two = gains[0:1], gains[1:2]
        hidden_one, queries, own_kv = qkv_forward(tokens, gain_one, qkv_full, cos2, sin2)
        all_kv = window_kv(earlier_kv(own_kv), own_kv)
        attended, log_totals = attention_fwd(start, queries, all_kv)
        middle, hidden_two = middle_forward(tokens, attended, project_full, gain_two)

    act, gate_up_low, block_output, hidden_two_grad = feed_forward(
        hidden_two, do, gate_full, up_full, down_full, middle
    )

    def key_value_sum(key_all, value_all):
        kv_all = jnp.concatenate([key_all, value_all], axis=1)
        parts = []
        for k in range(1, reach + 1):
            low = WINDOW - k * length
            part = kv_all[max(low, 0) : low + length].astype(bf16)
            if low < 0:
                part = jnp.pad(part, ((-low, 0), (0, 0)))
            parts.append(lax.ppermute(part, "y", [(i + k, i) for i in range(seqs - k)]))
        return kv_all[WINDOW:], parts

    def key_value_grad(own, parts):
        total = own
        for part in parts:
            total = total + part.astype(f32)
        key_sum = total[:, :HD]
        key_grad = key_sum * cos2 - jnp.roll(key_sum, HD // 2, axis=1) * sin2
        return jnp.concatenate([key_grad, total[:, HD:]], axis=1).astype(bf16)

    attention_back = lambda half, grad: attention_bwd(
        start, half, queries, all_kv, attended, grad, log_totals, cos2, sin2
    )
    zero, one = jnp.zeros((1,), jnp.int32), jnp.ones((1,), jnp.int32)
    if by_hand:
        half = c.astype(jnp.int32)[None]

        half32, x32, y32, z32 = (v.astype(jnp.int32) for v in (c, x, y, z))
        own, other = jnp.stack([half32, x32, y32, z32]), jnp.stack([1 - half32, x32, y32, z32])
        every = jnp.stack([half32 * 0, x32, y32, z32])
        gate_up_away = shift(weight_grad(other, hidden_two, gate_up_low), "c", 1)
        middle_grad, branch_low, attended_grad, midnorm_part = middle_back(
            hidden_two_grad, middle, do, gain_two, project_full
        )
        gate_up_away, branch_low, act = fence(gate_up_away, branch_low, act)

        gate_up_arrays = weight_grad(own, hidden_two, gate_up_low, gate_up_away, deep)
        gate_up_arrays, branch_low, act = fence(gate_up_arrays, branch_low, act)

        gate_up_s = Scatter(own, gate_up_arrays)
        gate_up_s.send(0)
        project_away = weight_grad(other, attended, branch_low)
        away_q, away_k, away_v = attention_back(1 - half, attended_grad)
        away_q, project_away, attended_grad, act = settle((away_q, project_away, attended_grad, act), [gate_up_s])

        gate_up_s.send(1)
        down_part = weight_grad(every, act, do, parts=1)
        query_away = weight_grad(every, hidden_one, away_q, parts=1)
        down_part, query_away, attended_grad = settle((down_part, query_away, attended_grad), [gate_up_s])

        down_share = lax.psum_scatter(down_part, OWN, scatter_dimension=0, tiled=True)
        gate_up_s.second()
        project_away, query_away = shift(project_away, "c", 1), shift(query_away, "c", 1)
        keep_q, keep_k, keep_v = attention_back(half, attended_grad)
        keep_q, keep_k, keep_v, project_away, query_away = settle(
            (keep_q, keep_k, keep_v, project_away, query_away), [gate_up_s]
        )

        kv_own, kv_parts = key_value_sum(away_k + keep_k, away_v + keep_v)
        gate_up_s.total()
        gate_up_s.along(1), gate_up_s.along(2)
        project_sum = weight_grad(own, attended, branch_low, project_away)
        query_sum = weight_grad(every, hidden_one, keep_q, query_away, parts=1)
        query_sum, project_sum, kv_parts, gate_up_s.kept, gate_up_s.away = fence(
            query_sum, project_sum, kv_parts, gate_up_s.kept, gate_up_s.away
        )

        gate_up_s.along(3)

        kv_grad = key_value_grad(kv_own, kv_parts)
        kv_away = shift(weight_grad(other, hidden_one, kv_grad), "c", 1)
        input_grad, prenorm_part = input_back(
            half, keep_q, away_q, kv_grad, qkv_full, tokens, gain_one, middle_grad
        )
        gain_part = jnp.pad(jnp.concatenate([prenorm_part, midnorm_part]).T, ((0, 0), (0, HD - 2))).astype(bf16)
        gain_sum = add_low(gain_part, shift(gain_part, "c", 1))
        kv_sum = weight_grad(own, hidden_one, kv_grad, kv_away)
        rest = jnp.concatenate([query_sum, project_sum, kv_sum, gain_sum], axis=1)
        cols = rest.shape[1]
        rest = rest.reshape(deep, 2, 2, -1, cols)
        of_x = lambda n, index: lax.dynamic_index_in_dim(rest[n], index, 0, False).reshape(1, -1, cols)
        of_y = lambda n, index: lax.dynamic_index_in_dim(rest[n], index, 1, False)
        low, high = range(deep // 2), range(deep // 2, deep)
        stays = [of_x(n, x) for n in low] + [of_y(n, y) for n in high]
        goes = jnp.concatenate([of_x(n, 1 - x) for n in low]), jnp.concatenate([of_y(n, 1 - y) for n in high])
        stays, goes = fence(stays, goes)

        came_x, came_y = fence(shift(goes[0], "x", 1), shift(goes[1], "y", 1))
        rest_s = Scatter(own, stays + stays)
        came_y = came_y.reshape(deep // 2, 2, -1, cols)
        for n in low:
            rest_s.moving += [came_x[n], came_y[n]]

        rest_s.second()
        (down_share,) = settle((down_share,), [rest_s, gate_up_s])

        rest_s.third()
        gate_up_s.fourth()
        down_other = shift(down_share, "y", 1)
        (down_other,) = settle((down_other,), [rest_s, gate_up_s])

        rest_s.fourth()
        left, right, _ = gate_up_s.last()
        wide_half = hidden // 2
        gate_gradient = jnp.concatenate([left[:, :wide_half], right[:, :wide_half]], axis=1)
        up_gradient = jnp.concatenate([left[:, wide_half:], right[:, wide_half:]], axis=1)
        down_gradient = down_share.astype(f32) + down_other.astype(f32)
        left, right, mine = rest_s.last()
        cut = wide // 2
        query_gradient = jnp.concatenate([left[:, :cut], right[:, :cut]], axis=1)
        project_gradient = jnp.concatenate([left[:, cut : 2 * cut], right[:, cut : 2 * cut]], axis=1)
        key_gradient, value_gradient = left[:, 2 * cut : 2 * cut + HD], right[:, 2 * cut : 2 * cut + HD]
        gain_mine = mine[:, 2 * cut + HD : 2 * cut + HD + 2].astype(f32).T
    else:

        def summed(a, b):
            value = jnp.concatenate([weight_grad(zero, a, b), weight_grad(one, a, b)], axis=1)
            return lax.psum(lax.psum_scatter(value, OWN, scatter_dimension=0, tiled=True), "y").astype(f32)

        gate_gradient, up_gradient = summed(hidden_two, gate_up_low[0]), summed(hidden_two, gate_up_low[1])
        middle_grad, branch_low, attended_grad, midnorm_part = middle_back(
            hidden_two_grad, middle, do, gain_two, project_full
        )
        down_gradient, project_gradient = summed(act, do), summed(attended, branch_low)
        left_q, left_k, left_v = attention_back(zero, attended_grad)
        right_q, right_k, right_v = attention_back(one, attended_grad)
        kv_grad = key_value_grad(*key_value_sum(left_k + right_k, left_v + right_v))
        input_grad, prenorm_part = input_back(
            zero, left_q, right_q, kv_grad, qkv_full, tokens, gain_one, middle_grad
        )
        query_gradient = summed(hidden_one, jnp.concatenate([left_q, right_q], axis=1))
        kv_gradient = summed(hidden_one, kv_grad)
        key_gradient, value_gradient = kv_gradient[:, :HD], kv_gradient[:, HD:]
        gain_sums = lax.psum(jnp.concatenate([prenorm_part, midnorm_part]), ALL)
        index = (z * 2 + x) * 2 + c
        gain_mine = lax.dynamic_slice_in_dim(gain_sums, index * shard, shard, 1)
    return (
        block_output[None],
        input_grad[None],
        gain_mine[0],
        query_gradient,
        key_gradient,
        value_gradient,
        project_gradient,
        gain_mine[1],
        gate_gradient,
        up_gradient,
        down_gradient,
    )


def solution(mesh):
    owners, seqs = mesh.shape["fsdp"], mesh.shape["seq"]
    deep = owners // 4
    split = Mesh(mesh.devices.reshape(deep, 2, 2, seqs), ALL)
    rows = P(OWN, "y", None)
    weight = P(OWN, None)
    in_specs = (
        rows,
        P(OWN),
        weight,
        weight,
        weight,
        weight,
        P(OWN),
        weight,
        weight,
        weight,
        rows,
    )
    out_specs = (
        rows,
        rows,
        P(OWN),
        weight,
        weight,
        weight,
        weight,
        P(OWN),
        weight,
        weight,
        weight,
    )
    by_hand = seqs == 2 and deep == 4
    return jax.shard_map(
        functools.partial(per_device, by_hand=by_hand),
        mesh=split,
        in_specs=in_specs,
        out_specs=out_specs,
        check_vma=False,
    )
```
